32 devices in a mesh: wide: 8 (over z, core), narrow: 4 (over y, x).
Axes of the slice: x: 2, y: 2, z: 4, core: 2. Of those that a mesh axis runs over, the one named last changes fastest.
Arguments:
- video: bfloat16 [32, 11, 64, 512], P(('wide', 'narrow')), may hold values from -6 to 6
- frames: int32 [32], P(('wide', 'narrow')), may hold values from 1 to 21, as said below
- cotangent: bfloat16 [32, 11, 64, 512], P(('wide', 'narrow')), may hold values from -6 to 6
- qkv_weight: float32 [2, 512, 1536], P(None, ('wide', 'narrow')), may hold values from -0.25 to 0.25
- out_weight: float32 [2, 512, 512], P(None, ('wide', 'narrow')), may hold values from -0.75 to 0.75
- in_weight: float32 [2, 512, 2048], P(None, ('wide', 'narrow')), may hold values from -0.25 to 0.25
- down_weight: float32 [2, 2048, 512], P(None, ('wide', 'narrow')), may hold values from -0.125 to 0.125
- attn_gain: float32 [2, 512], P(None, ('wide', 'narrow')), may hold values from 0.25 to 1.75
- mlp_gain: float32 [2, 512], P(None, ('wide', 'narrow')), may hold values from 0.25 to 1.75
Outputs:
- output: bfloat16 [32, 11, 64, 512], P(('wide', 'narrow'))
- grad_video: bfloat16 [32, 11, 64, 512], P(('wide', 'narrow'))
- grad_qkv: float32 [2, 512, 1536], P(None, ('wide', 'narrow'))
- grad_out: float32 [2, 512, 512], P(None, ('wide', 'narrow'))
- grad_in: float32 [2, 512, 2048], P(None, ('wide', 'narrow'))
- grad_down: float32 [2, 2048, 512], P(None, ('wide', 'narrow'))
- grad_attn_gain: float32 [2, 512], P(None, ('wide', 'narrow'))
- grad_mlp_gain: float32 [2, 512], P(None, ('wide', 'narrow'))
The draws below stay inside these ranges and needn't reach their ends.
Inputs may be any that keep to these rules, and one draw needn't show every extreme that they name: Every draw has a clip of 21 frames and a clip of 1 frame.
All inputs are finite; a program needn't handle non-finite values.
Results may differ from the reference program's by a relative error of at most 0.02.
Values may be sent and summed in bfloat16 or wider, within the bound.
A program may use at most 192 MiB of HBM per device.

```python
import jax
import jax.numpy as jnp
from jax import lax

D = 512
HEADS = 8
FF = 2048
PATCHES = 64
MAX_FRAMES = 21
SLOTS = 11
CLIPS = 32


def draw_frames(key, part):
    key = jax.random.fold_in(key, 7)
    first, second, third = jax.random.split(key, 3)
    counts = jax.random.randint(first, (CLIPS,), 1, MAX_FRAMES + 1)
    longest = jax.random.randint(second, (), 0, CLIPS)
    shortest = (longest + 1 + jax.random.randint(third, (), 0, CLIPS - 1)) % CLIPS
    counts = counts.at[longest].set(MAX_FRAMES)
    counts = counts.at[shortest].set(1)
    return counts.astype(jnp.int32)


def level_of(stream_key, extent, pieces, smallest, high):
    factor_of, own = 1.0, jax.random.fold_in(stream_key, 6)
    for dim, parts in pieces:
        heights = jnp.exp(jax.random.uniform(jax.random.fold_in(own, dim), (parts,), jnp.float32, smallest / len(pieces), high / len(pieces)))
        factor_of = factor_of * jnp.repeat(heights, extent[dim] // parts).reshape([-1 if axis == dim else 1 for axis in range(len(extent))])
    return factor_of


def normal_values(key, extent, scale, limit, shards=(), kind=jnp.bfloat16):
    level = level_of(key, extent, shards, -0.22, 0.18) if shards else 1.0
    values = jax.random.normal(key, extent, jnp.float32) * scale * level
    return jnp.minimum(jnp.maximum(values, -limit), limit).astype(kind)


def setup_inputs(seed: int = 0) -> dict:
    splits = jax.random.split(jax.random.key(seed), 10)
    video = normal_values(splits[0], (CLIPS, SLOTS, PATCHES, D), 1.0, 6.0, ((0, 32),))
    frames = draw_frames(jax.random.fold_in(splits[9], 71), 0)
    cotangent = normal_values(splits[2], (CLIPS, SLOTS, PATCHES, D), 1.0, 6.0, ((0, 32),))
    qkv_weight = normal_values(splits[3], (2, D, 3 * D), D ** -0.5, 0.25, ((1, 32),), jnp.float32)
    out_weight = normal_values(splits[4], (2, D, D), (D // 8) ** -0.5, 0.75, ((1, 32),), jnp.float32)
    in_weight = normal_values(splits[5], (2, D, FF), D ** -0.5, 0.25, ((1, 32),), jnp.float32)
    down_weight = normal_values(splits[6], (2, FF, D), FF ** -0.5, 0.125, ((1, 32),), jnp.float32)
    attn_gain = jnp.clip(1.0 + 0.15 * jax.random.normal(splits[7], (2, D), jnp.float32), 0.25, 1.75)
    mlp_gain = jnp.clip(1.0 + 0.15 * jax.random.normal(splits[8], (2, D), jnp.float32), 0.25, 1.75)
    return dict(video=video, frames=frames, cotangent=cotangent, qkv_weight=qkv_weight, out_weight=out_weight, in_weight=in_weight, down_weight=down_weight, attn_gain=attn_gain, mlp_gain=mlp_gain)


highest = lax.Precision.HIGHEST
epsilon = 1e-05

@jax.custom_vjp
def low(v):
    return lax.optimization_barrier(v.astype(jnp.bfloat16)).astype(jnp.float32)

@jax.custom_vjp
def low_back(v):
    return v

def low_keep(v):
    return (low(v), None)

def low_pass(kept, grad):
    return (grad,)

def back_keep(v):
    return (v, None)

def back_low(kept, grad):
    return (low(grad),)
low.defvjp(low_keep, low_pass)
low_back.defvjp(back_keep, back_low)

def round_both(values):
    return low(low_back(values))

def norm_rows(inputs, scaling):
    centre = lax.optimization_barrier(jnp.mean(inputs, axis=-1, keepdims=True))
    centred = inputs - centre
    spread = lax.optimization_barrier(jnp.mean(centred * centred, axis=-1, keepdims=True))
    return centred * lax.rsqrt(spread + epsilon) * scaling

def project(rows_in, matrix):
    return jnp.einsum('spd,de->spe', rows_in, matrix, precision=highest)

def block_forward(inputs, weights, which_block, allowed):
    qkv_matrix, out_matrix, in_matrix, down_matrix, attn_scaling, mlp_scaling = weights
    full_shape = inputs.shape
    head_size = full_shape[-1] // HEADS
    normed = low(norm_rows(inputs, low(attn_scaling)))
    qkv_rows = round_both(project(normed, low(qkv_matrix)))
    split = qkv_rows.reshape(full_shape[:2] + (3, HEADS, head_size))
    queries = split[:, :, 0]
    key_rows = split[:, :, 1]
    value_rows = split[:, :, 2]
    if which_block == 0:
        scores = jnp.einsum('sphe,sqhe->shpq', queries, key_rows, precision=highest)
    else:
        scores = jnp.einsum('sphe,tphe->phst', queries, key_rows, precision=highest)
    scores = low_back(scores * head_size ** (-0.5))
    if which_block == 1:
        scores = jnp.where(allowed[None, None], scores, -1000000000.0)
    row_max = lax.optimization_barrier(jnp.max(scores, axis=-1, keepdims=True))
    shifted = jnp.exp(scores - row_max)
    attn_probs = low(shifted / lax.optimization_barrier(jnp.sum(shifted, axis=-1, keepdims=True)))
    if which_block == 0:
        attended = jnp.einsum('shpq,sqhe->sphe', attn_probs, value_rows, precision=highest)
    else:
        attended = jnp.einsum('phst,tphe->sphe', attn_probs, value_rows, precision=highest)
    attended = round_both(attended.reshape(full_shape))
    middle = inputs + low_back(project(attended, low(out_matrix)))
    normed_mlp = low(norm_rows(middle, low(mlp_scaling)))
    hidden = low_back(project(normed_mlp, low(in_matrix)))
    active = low(jax.nn.gelu(hidden))
    return middle + low_back(project(active, low(down_matrix)))

def layer_forward(clip_rows, slot_count, weights):
    positions = jnp.arange(clip_rows.shape[0], dtype=jnp.int32)
    allowed = (positions[None, :] <= positions[:, None]) & (positions[None, :] < slot_count)
    spatial = tuple((stacked[0] for stacked in weights))
    temporal = tuple((stacked[1] for stacked in weights))
    after = block_forward(clip_rows, spatial, 0, allowed)
    after = block_forward(after, temporal, 1, allowed)
    valid_slot = (positions < slot_count).astype(jnp.float32)
    return after * valid_slot[:, None, None]

def reference(video, frames, cotangent, qkv_weight, out_weight, in_weight, down_weight, attn_gain, mlp_gain):
    weights = (qkv_weight, out_weight, in_weight, down_weight, attn_gain, mlp_gain)
    slot_counts = ((frames + 1) // 2).astype(jnp.int32)

    def per_clip(running, clip_item):
        clip_rows, slot_count, clip_grad = clip_item

        def forward(rows_in, params):
            return layer_forward(rows_in, slot_count, params)
        result, pullback = jax.vjp(forward, clip_rows.astype(jnp.float32), weights)
        grad_rows, grad_params = pullback(clip_grad.astype(jnp.float32))
        running = jax.tree.map(jnp.add, running, grad_params)
        return (running, (result.astype(jnp.bfloat16), grad_rows.astype(jnp.bfloat16)))
    zero_grads = jax.tree.map(jnp.zeros_like, weights)
    totals, outputs = lax.scan(per_clip, zero_grads, (video, slot_counts, cotangent))
    return (outputs[0], outputs[1], totals[0], totals[1], totals[2], totals[3], totals[4], totals[5])
```

```python
import functools

import jax
import jax.numpy as jnp
from jax import lax
from jax.experimental import pallas as pl
from jax.experimental.pallas import tpu as pltpu
from jax.sharding import PartitionSpec as P

HEADS = 8
EPS = 1e-05
BF = jnp.bfloat16
F32 = jnp.float32
MESH = pl.DeviceIdType.MESH
VMEM_LIMIT = 62 * 2**20
TILE = 256


def dot(a, b, ca, cb):
    return lax.dot_general(a, b, (((ca,), (cb,)), ((), ())), preferred_element_type=F32)


def ds(start, size):
    if isinstance(start, int):
        return pl.ds(start, size)
    return pl.ds(pl.multiple_of(start, size), size)


def loop(count, body, first=0):
    def step(i, carry):
        body(i)
        return carry

    lax.fori_loop(first, count, step, 0)


class Place:
    def __init__(self, depth):
        self.depth = depth
        self.w = lax.axis_index("wide")
        self.n = lax.axis_index("narrow")
        self.z = self.w // 2
        self.c = self.w % 2
        first = 1 + self.c
        self.na = self.flip(self.n, first)
        self.nb = self.flip(self.n, 3 - first)
        self.nab = 3 - self.n

    @staticmethod
    def flip(n, step):
        bit = (n // step) % 2
        return n + step - 2 * step * bit

    def sib(self):
        return (self.z * 2 + 1 - self.c, self.n)

    def a(self):
        return (self.w, self.na)

    def b(self):
        return (self.w, self.nb)

    def along(self, d):
        return (lax.rem(self.z + d, self.depth) * 2 + self.c, self.n)

    def zat(self, d):
        return lax.rem(self.z + d, self.depth)

    def greet(self):
        bar = pltpu.get_barrier_semaphore()
        targets = [self.sib(), self.a(), self.b()] + [self.along(d) for d in range(1, self.depth)]
        for t in targets:
            pl.semaphore_signal(bar, inc=1, device_id=t, device_id_type=MESH)
        pl.semaphore_wait(bar, len(targets))


def remote(src, dst, send, recv, target):
    return pltpu.make_async_remote_copy(src, dst, send, recv, device_id=target, device_id_type=MESH)


class Gather:
    def __init__(self, place, full, send, recv):
        self.p, self.full, self.send, self.recv = place, full, send, recv
        self.started = []

    def go(self, slot, src_index, dst_index, target):
        copy = remote(
            self.full.at[src_index], self.full.at[dst_index], self.send.at[slot], self.recv.at[slot], target
        )
        copy.start()
        self.started.append(copy)

    def take(self, slot, index):
        view = self.full.at[index]
        remote(view, view, self.send.at[slot], self.recv.at[slot], self.p.sib()).wait_recv()

    def step0(self):
        p = self.p
        own = (p.z, p.c, p.n)
        for d in range(1, p.depth):
            self.go(d - 1, own, own, p.along(d))

    def column(self, n, core=None):
        core = self.p.c if core is None else core
        return (slice(None), core, n)

    def sibling(self, slot, n):
        col = self.column(n)
        self.go(self.p.depth + 2 + slot, col, col, self.p.sib())

    def step1(self):
        p, base = self.p, self.p.depth - 1
        for d in range(1, p.depth):
            self.take(d - 1, (p.zat(p.depth - d), p.c, p.n))
        col = self.column(p.n)
        self.go(base, col, col, p.a())
        self.go(base + 1, col, col, p.b())
        self.sibling(0, p.n)

    def step2(self):
        p, base = self.p, self.p.depth - 1
        self.take(base, self.column(p.na))
        col = self.column(p.na)
        self.go(base + 2, col, col, p.b())
        self.sibling(1, p.na)

    def step3(self):
        p, base = self.p, self.p.depth - 1
        self.take(base + 1, self.column(p.nb))
        self.sibling(2, p.nb)
        self.take(base + 2, self.column(p.nab))
        self.sibling(3, p.nab)

    def step4(self):
        p = self.p
        for slot, n in enumerate((p.n, p.nb, p.na, p.nab)):
            self.take(p.depth + 2 + slot, self.column(n, 1 - p.c))

    def finish(self):
        for copy in self.started:
            copy.wait_send()

    steps = 5

    def step(self, i):
        (self.step0, self.step1, self.step2, self.step3, self.step4)[i]()


class Scatter:
    def __init__(self, place, full, from_sib, from_b, from_a, from_z, out, send, recv):
        self.p, self.full, self.out, self.send, self.recv = place, full, out, send, recv
        self.from_sib, self.from_b, self.from_a, self.from_z = from_sib, from_b, from_a, from_z
        self.started = []

    def go(self, slot, src, dst, target):
        copy = remote(src, dst, self.send.at[slot], self.recv.at[slot], target)
        copy.start()
        self.started.append(copy)

    def take(self, slot, view):
        remote(view, view, self.send.at[slot], self.recv.at[slot], self.p.sib()).wait_recv()

    def add(self, n, part):
        c = self.p.c

        def body(z):
            self.full[z, c, n] = self.full[z, c, n] + part(z)

        loop(self.p.depth, body)

    def step0(self):
        self.go(0, self.full.at[:, 1 - self.p.c], self.from_sib, self.p.sib())

    def step1(self):
        p = self.p
        self.take(0, self.from_sib)
        for slot, n in ((1, p.nab), (2, p.nb)):
            self.add(n, lambda z, n=n: self.from_sib[z, n])
            self.go(slot, self.full.at[:, p.c, n], self.from_b.at[slot - 1], p.b())
        for n in (p.na, p.n):
            self.add(n, lambda z, n=n: self.from_sib[z, n])

    def step2(self):
        p = self.p
        self.take(1, self.from_b.at[0])
        self.add(p.na, lambda z: self.from_b[0, z])
        self.go(3, self.full.at[:, p.c, p.na], self.from_a, p.a())
        self.take(2, self.from_b.at[1])
        self.add(p.n, lambda z: self.from_b[1, z])

    def step3(self):
        p = self.p
        self.take(3, self.from_a)
        self.add(p.n, lambda z: self.from_a[z])
        for d in range(1, p.depth):
            self.go(3 + d, self.full.at[p.zat(d), p.c, p.n], self.from_z.at[d - 1], p.along(d))

    def step4(self):
        p = self.p
        total = self.full[p.z, p.c, p.n].astype(F32)
        for d in range(1, p.depth):
            self.take(3 + d, self.from_z.at[d - 1])
            total = total + self.from_z[d - 1].astype(F32)
        self.out[...] = total

    def finish(self):
        for copy in self.started:
            copy.wait_send()

    def step(self, i):
        (self.step0, self.step1, self.step2, self.step3, self.step4)[i]()


def stats(x):
    centre = jnp.mean(x, axis=-1, keepdims=True)
    centred = x - centre
    spread = jnp.mean(centred * centred, axis=-1, keepdims=True)
    r = lax.rsqrt(spread + EPS)
    return centred * r, r


def norm_into(src, gain, dst, rows):
    total = src.shape[0]

    def body(i):
        at = ds(i * rows, rows)
        xn, _ = stats(src[at, :].astype(F32))
        dst[at, :] = (xn * gain).astype(BF)

    loop(total // rows, body)


def halves(shape):
    return lax.broadcasted_iota(jnp.int32, shape, 1) < shape[1] // 2


def split_heads(x):
    low = halves(x.shape)
    zero = jnp.zeros_like(x)
    return jnp.concatenate([jnp.where(low, x, zero), jnp.where(low, zero, x)], 0)


def spatial_forward(qkv, probs, att, patches, width, first, last):
    head = width // HEADS
    scale = head ** -0.5

    def body(s):
        at = ds(s * patches, patches)
        for pair in range(HEADS // 2):
            lane = pair * 2 * head
            q = qkv[at, lane : lane + 2 * head]
            k2 = split_heads(qkv[at, width + lane : width + lane + 2 * head])
            v2 = split_heads(qkv[at, 2 * width + lane : 2 * width + lane + 2 * head])
            scores = dot(q, k2, 1, 1) * scale
            low = halves(scores.shape)
            top0 = jnp.max(jnp.where(low, scores, -jnp.inf), axis=-1, keepdims=True)
            top1 = jnp.max(jnp.where(low, -jnp.inf, scores), axis=-1, keepdims=True)
            e = jnp.exp(scores - jnp.where(low, top0, top1))
            sum0 = jnp.sum(jnp.where(low, e, 0.0), axis=-1, keepdims=True)
            sum1 = jnp.sum(jnp.where(low, 0.0, e), axis=-1, keepdims=True)
            p = (e / jnp.where(low, sum0, sum1)).astype(BF)
            probs[s, pair] = p
            att[at, lane : lane + 2 * head] = dot(p, v2, 1, 0).astype(BF)

    loop(last, body, first)


def pad_heads(x, lanes):
    low = halves(x.shape)
    zero = jnp.zeros_like(x)
    fill = jnp.zeros((lanes - x.shape[0], x.shape[1]), x.dtype)
    return jnp.concatenate([jnp.where(low, x, zero), fill, jnp.where(low, zero, x), fill], 0).astype(BF)


LANES = 128
SUB = 8


def temporal_forward(qkv, probs, att, bias, slots, width, first, last):
    head = width // HEADS
    scale = head ** -0.5
    group = slots * SUB

    def body(i):
        at = ds(i * 2 * group, 2 * group)
        for pair in range(HEADS // 2):
            lane = pair * 2 * head
            q = qkv[at, lane : lane + 2 * head].astype(F32)
            k = qkv[at, width + lane : width + lane + 2 * head].astype(F32)
            v = qkv[at, 2 * width + lane : 2 * width + lane + 2 * head].astype(F32)
            out = []
            for half in range(2):
                rows = slice(half * group, (half + 1) * group)
                scores = dot(q[rows].astype(BF), pad_heads(k[rows], LANES), 1, 1) * scale
                ps = []
                for h in range(2):
                    one = scores[:, h * LANES : (h + 1) * LANES] + bias[...]
                    e = jnp.exp(one - jnp.max(one, axis=-1, keepdims=True))
                    ps.append(e / jnp.sum(e, axis=-1, keepdims=True))
                p = jnp.concatenate(ps, 1).astype(BF)
                probs[i * 2 + half, pair] = p
                out.append(dot(p, pad_heads(v[rows], LANES), 1, 0))
            att[at, lane : lane + 2 * head] = jnp.concatenate(out, 0).astype(BF)

    loop(last, body, first)


def make_bias(bias, count, slots):
    group = slots * SUB
    q = lax.broadcasted_iota(jnp.int32, (group, LANES), 0)
    k = lax.broadcasted_iota(jnp.int32, (group, LANES), 1)
    sq, sk = q // SUB, k // SUB
    ok = (q - sq * SUB == k - sk * SUB) & (sk <= sq) & (sk < count)
    bias[...] = jnp.where(ok, 0.0, -1e9)


def gelu_pair(z):
    k0 = 0.7978845608028654
    z2 = z * z
    t = jnp.tanh(z * (k0 + (k0 * 0.044715) * z2))
    half = 0.5 + 0.5 * t
    slope = half + (0.5 * z) * (1.0 - t * t) * (k0 + (3.0 * k0 * 0.044715) * z2)
    return z * half, slope


def wide_rows(ref, width, columns=None):
    x = ref[...] if columns is None else ref[:, :, :, :, columns]
    return x.reshape(width, x.shape[-1])


def unsplit_heads(x, second, rows):
    low = halves((rows, x.shape[1]))
    return jnp.where(low, x[:rows], x[second : second + rows])


def spatial_backward(qkv, probs, grad, patches, width, first, last):
    head = width // HEADS
    scale = head ** -0.5

    def body(s):
        at = ds(s * patches, patches)
        for pair in range(HEADS // 2):
            lane = pair * 2 * head
            cq, ck, cv = (slice(t * width + lane, t * width + lane + 2 * head) for t in range(3))
            q = qkv[at, cq]
            k2 = split_heads(qkv[at, ck])
            v2 = split_heads(qkv[at, cv])
            g = grad[at, lane : lane + 2 * head]
            p = probs[s, pair]
            soft = p.astype(F32)
            gp = dot(g, v2, 1, 1)
            low = halves(gp.shape)
            both = gp * soft
            sum0 = jnp.sum(jnp.where(low, both, 0.0), axis=-1, keepdims=True)
            sum1 = jnp.sum(jnp.where(low, 0.0, both), axis=-1, keepdims=True)
            gs = (soft * (gp - jnp.where(low, sum0, sum1))).astype(BF)
            qkv[at, cq] = (dot(gs, k2, 1, 0) * scale).astype(BF)
            qkv[at, ck] = (unsplit_heads(dot(gs, q, 0, 0), patches, patches) * scale).astype(BF)
            qkv[at, cv] = unsplit_heads(dot(p, g, 0, 0), patches, patches).astype(BF)

    loop(last, body, first)


def temporal_backward(qkv, probs, grad, slots, width, first, last):
    head = width // HEADS
    scale = head ** -0.5
    group = slots * SUB

    def body(i):
        at = ds(i * 2 * group, 2 * group)
        for pair in range(HEADS // 2):
            lane = pair * 2 * head
            cols = [slice(t * width + lane, t * width + lane + 2 * head) for t in range(3)]
            q, k, v = (qkv[at, c].astype(F32) for c in cols)
            g = grad[at, lane : lane + 2 * head].astype(F32)
            outs = ([], [], [])
            for half in range(2):
                rows = slice(half * group, (half + 1) * group)
                gl = g[rows].astype(BF)
                p = probs[i * 2 + half, pair]
                gp = dot(gl, pad_heads(v[rows], LANES), 1, 1)
                parts = []
                for h in range(2):
                    lanes = slice(h * LANES, (h + 1) * LANES)
                    soft = p[:, lanes].astype(F32)
                    one = gp[:, lanes]
                    delta = jnp.sum(one * soft, axis=-1, keepdims=True)
                    parts.append(soft * (one - delta))
                gs = jnp.concatenate(parts, 1).astype(BF)
                outs[0].append(dot(gs, pad_heads(k[rows], LANES), 1, 0) * scale)
                outs[1].append(unsplit_heads(dot(gs, q[rows].astype(BF), 0, 0), LANES, group) * scale)
                outs[2].append(unsplit_heads(dot(p, gl, 0, 0), LANES, group))
            for c, o in zip(cols, outs):
                qkv[at, c] = jnp.concatenate(o, 0).astype(BF)

    loop(last, body, first)


def norm_back(src, grad, gain, base, dst, low, sums, rows):
    total, width = grad.shape
    sums[...] = jnp.zeros_like(sums)

    def body(i):
        at = ds(i * rows, rows)
        xn, r = stats(src[at, :].astype(F32))
        g = grad[at, :]
        e = g * gain
        inner = e - jnp.mean(e, axis=-1, keepdims=True) - xn * jnp.mean(e * xn, axis=-1, keepdims=True)
        res = base[at, :] + r * inner
        if dst is not None:
            dst[at, :] = res
        low[at, :] = res.astype(BF)
        sums[...] += jnp.sum((g * xn).reshape(rows // SUB, SUB, width), axis=0)

    loop(total // rows, body)


def gain_row(gains, which):
    return gains[which : which + 1, :]


class Sizes:
    def __init__(self, mesh, video, in_weight):
        self.depth = mesh.shape["wide"] // 2
        self.narrow = mesh.shape["narrow"]
        self.slots, self.patches, self.width = video.shape[1:]
        self.hidden = in_weight.shape[2]
        self.tokens = self.slots * self.patches
        self.group = self.slots * SUB
        devices = 2 * self.depth * self.narrow
        w = self.width // devices
        self.shards = {
            "qkv": (w, 3 * self.width),
            "out": (w, self.width),
            "in": (w, self.hidden),
            "down": (self.hidden // devices, self.width),
        }
        self.mesh_dims = (self.depth, 2, self.narrow)

    def full(self, name):
        return self.mesh_dims + (TILE_GAIN if name == "gain" else self.shards[name])

    def acts(self, b):
        t, w, f = self.tokens, self.width, self.hidden
        pairs = HEADS // 2
        if b == 0:
            probs = (self.slots, pairs, self.patches, 2 * self.patches)
        else:
            probs = (self.patches // SUB, pairs, self.group, 2 * LANES)
        return {
            "normed": ((t, w), BF),
            "qkv": ((t, 3 * w), BF),
            "probs": (probs, BF),
            "att": ((t, w), BF),
            "middle": ((t, w), F32),
            "mlp": ((t, w), BF),
            "active": ((t, f), BF),
            "slope": ((t, f), BF),
        }


TILE_GAIN = (16, LANES)
NAMES = ("qkv", "out", "in", "down")
ACTS = ("normed", "qkv", "probs", "att", "middle", "mlp", "active", "slope")
GATHER_ORDER = [("gain", 0)] + [(name, b) for b in range(2) for name in NAMES]
SCATTER_ORDER = [(name, b) for b in (1, 0) for name in ("down", "in", "out", "qkv")] + [("gain", 0)]
ROWS = 64


def keys_of_weights():
    return [(name, b) for b in range(2) for name in NAMES]


def keys_of_acts():
    return [(name, b) for b in range(2) for name in ACTS]


def forward_kernel(sz, plan, *refs):
    refs = list(refs)

    def grab(n):
        taken, refs[:n] = refs[:n], []
        return taken

    video, frames, gain_tile = grab(3)
    shard = dict(zip(NAMES, grab(4)))
    (out,) = grab(1)
    (gains,) = grab(1)
    h1_hbm, = grab(1)
    acts_hbm = dict(zip(keys_of_acts(), grab(16)))
    full_hbm = dict(zip(keys_of_weights(), grab(8)))
    acts = dict(zip(keys_of_acts(), grab(16)))
    full = dict(zip(GATHER_ORDER, grab(9)))
    h1, result, bias, send, recv, local = grab(6)
    assert not refs

    place = Place(sz.depth)
    place.greet()
    gathers = {}
    for k, key in enumerate(GATHER_ORDER):
        gathers[key] = Gather(place, full[key], send.at[k], recv.at[k])
    saved = []

    def save(src, dst):
        copy = pltpu.make_async_copy(src, dst, local.at[len(saved)])
        copy.start()
        saved.append(copy)

    def comm(key, step):
        if step == 0:
            own = (place.z, place.c, place.n)
            if key[0] == "gain":
                full[key][own] = gain_tile[...]
            else:
                full[key][own] = shard[key[0]][key[1]].astype(BF)
        gathers[key].step(step)
        if step == 4 and key[0] != "gain":
            save(full[key], full_hbm[key])

    count = (frames[0] + 1) // 2
    t, w = sz.tokens, sz.width

    def stage_gain():
        make_bias(bias, count, sz.slots)
        tile = jnp.sum(full[("gain", 0)][...].astype(F32).reshape(-1, 16, LANES), axis=0)
        for g in range(4):
            rows = [tile[g * 4 + r : g * 4 + r + 1, :] for r in range(w // LANES)]
            gains[g : g + 1, :] = jnp.concatenate(rows, 1)

    def stages(b):
        a = {name: acts[(name, b)] for name in ACTS}
        h = video if b == 0 else h1

        def keep(*names):
            for name in names:
                save(a[name], acts_hbm[(name, b)])

        def norm1():
            norm_into(h, gain_row(gains, 2 * b), a["normed"], ROWS)
            keep("normed")

        def qkv(first, last):
            def body(j):
                at = ds(j * TILE, TILE)
                a["qkv"][:, at] = dot(a["normed"][...], wide_rows(full[("qkv", b)], w, at), 1, 0).astype(BF)

            loop(last, body, first)
            if last * TILE == 3 * w:
                keep("qkv")

        def attend(first, last):
            if b == 0:
                spatial_forward(a["qkv"], a["probs"], a["att"], sz.patches, w, first, last)
                end = sz.slots
            else:
                temporal_forward(a["qkv"], a["probs"], a["att"], bias, sz.slots, w, first, last)
                end = sz.patches // (2 * SUB)
            if last == end:
                keep("probs", "att")

        def project():
            def body(j):
                at = ds(j * TILE, TILE)
                new = dot(a["att"][...], wide_rows(full[("out", b)], w, at), 1, 0)
                a["middle"][:, at] = h[:, at].astype(F32) + new

            loop(w // TILE, body)
            keep("middle")

        def norm2():
            norm_into(a["middle"], gain_row(gains, 2 * b + 1), a["mlp"], ROWS)
            keep("mlp")

        def expand(first, last):
            def body(j):
                at = ds(j * TILE, TILE)
                active, slope = gelu_pair(dot(a["mlp"][...], wide_rows(full[("in", b)], w, at), 1, 0))
                a["active"][:, at] = active.astype(BF)
                a["slope"][:, at] = slope.astype(BF)

            loop(last, body, first)
            if last * TILE == sz.hidden:
                keep("active", "slope")

        def contract():
            def body(j):
                at = ds(j * TILE, TILE)
                new = a["middle"][:, at] + dot(a["active"][...], wide_rows(full[("down", b)], sz.hidden, at), 1, 0)
                if b == 0:
                    new = new.reshape(sz.slots, sz.patches // SUB, SUB, TILE)
                    for s in range(sz.slots):
                        h1_view[:, s * SUB : (s + 1) * SUB, at] = new[s]
                else:
                    result[:, at] = new

            loop(w // TILE, body)
            if b == 0:
                save(h1, h1_hbm)

        def write():
            valid = lax.broadcasted_iota(jnp.int32, (sz.slots, 1, 1), 0) < count

            def body(i):
                rows = result[ds(i * 2 * sz.group, 2 * sz.group), :]
                rows = rows.reshape(2, sz.slots, SUB, w)
                rows = jnp.concatenate([rows[0], rows[1]], axis=1)
                out[:, ds(i * 2 * SUB, 2 * SUB), :] = jnp.where(valid, rows, 0.0).astype(BF)

            loop(sz.patches // (2 * SUB), body)

        n_q, n_f = 3 * w // TILE, sz.hidden // TILE
        n_a = sz.slots if b == 0 else sz.patches // (2 * SUB)
        cuts = [n_a * i // 4 for i in range(5)]
        todo = [norm1, lambda: qkv(0, n_q // 2), lambda: qkv(n_q // 2, n_q)]
        todo += [functools.partial(attend, cuts[i], cuts[i + 1]) for i in range(4)]
        todo += [project, norm2]
        todo += [functools.partial(expand, n_f * i // 4, n_f * (i + 1) // 4) for i in range(4)]
        todo += [contract]
        if b == 1:
            todo += [write]
        return todo

    h1_view = h1.reshape(sz.patches // SUB, sz.group, w)
    work = iter([stage_gain] + stages(0) + stages(1))
    for op in plan:
        if op is None:
            next(work)()
        else:
            comm(GATHER_ORDER[op[0]], op[1])
    assert next(work, None) is None
    for gather in gathers.values():
        gather.finish()
    for copy in saved:
        copy.wait()


FORWARD_NEEDS = {0: 0, 1: 2, 2: 8, 3: 10, 4: 14, 5: 16, 6: 22, 7: 24, 8: 28}
FORWARD_STAGES = 30


def forward_plan():
    plan = []
    for k in range(9):
        for s in range(5):
            plan.append((k, s))
    return plan + [None] * FORWARD_STAGES


def backward_kernel(sz, plan, *refs):
    refs = list(refs)

    def grab(n):
        taken, refs[:n] = refs[:n], []
        return taken

    video, cotangent, frames, gains = grab(4)
    (h1_hbm,) = grab(1)
    acts_hbm = dict(zip(keys_of_acts(), grab(16)))
    full_hbm = dict(zip(keys_of_weights(), grab(8)))
    (grad_video,) = grab(1)
    outs = dict(zip(NAMES, grab(4)))
    (gain_out,) = grab(1)
    acts = dict(zip(ACTS, grab(8)))
    probs1, h1 = grab(2)
    full = dict(zip(keys_of_weights(), grab(8)))
    grads = dict(zip([(name, 1) for name in NAMES] + [("gain", 0)], grab(5)))
    landing = {key: grab(4) for key in SCATTER_ORDER}
    grad, grad_mid, grad_norm, low, grad_att, sums = grab(6)
    send, recv, local_w, local_a = grab(4)
    assert not refs
    for name in NAMES:
        grads[(name, 0)] = full[(name, 1)]

    place = Place(sz.depth)
    t, w = sz.tokens, sz.width
    count = (frames[0] + 1) // 2
    fetched = {}

    def fetch(key, src, dst, sem):
        copy = pltpu.make_async_copy(src, dst, sem)
        copy.start()
        fetched[key] = copy

    def ready(*keys):
        for key in keys:
            if key in fetched:
                fetched.pop(key).wait()

    def act(name, b):
        return probs1 if (name, b) == ("probs", 1) else acts[name]

    def fetch_act(name, b):
        i = ACTS.index(name)
        fetch(("act", name, b), acts_hbm[(name, b)], act(name, b), local_a.at[b, i])

    def fetch_full(name, b):
        i = NAMES.index(name)
        fetch(("full", name, b), full_hbm[(name, b)], full[(name, b)], local_w.at[b, i])

    fetch_act("active", 1)
    fetch_full("down", 1)
    fetch_act("slope", 1)
    fetch_act("mlp", 1)
    fetch_full("in", 1)
    fetch_act("middle", 1)
    fetch_act("att", 1)
    fetch_full("out", 1)
    fetch_act("qkv", 1)
    fetch_act("probs", 1)
    fetch_act("probs", 0)
    fetch_act("normed", 1)
    fetch_full("qkv", 1)
    fetch(("h1",), h1_hbm, h1, local_w.at[0, 4])
    for name in ("down", "in", "out", "qkv"):
        fetch_full(name, 0)

    def outs_of(key):
        return gain_out if key[0] == "gain" else outs[key[0]].at[key[1]]

    place.greet()
    scatters = {}
    for k, key in enumerate(SCATTER_ORDER):
        scatters[key] = Scatter(place, grads[key], *landing[key], outs_of(key), send.at[k], recv.at[k])

    def start():
        valid = lax.broadcasted_iota(jnp.int32, (sz.slots, 1, 1), 0) < count

        def body(i):
            rows = cotangent[:, ds(i * 2 * SUB, 2 * SUB), :].astype(F32)
            rows = jnp.where(valid, rows, 0.0)
            both = [rows[:, half * SUB : (half + 1) * SUB, :].reshape(sz.group, w) for half in range(2)]
            rows = jnp.concatenate(both, 0)
            at = ds(i * 2 * sz.group, 2 * sz.group)
            grad[at, :] = rows
            low[at, :] = rows.astype(BF)

        loop(sz.patches // (2 * SUB), body)

    def put_gain(which):
        row = jnp.sum(sums[...], axis=0, keepdims=True)
        per = w // LANES
        tile = jnp.concatenate([row[:, r * LANES : (r + 1) * LANES] for r in range(per)], 0)
        gain_rows[which * per : (which + 1) * per, :] = tile

    gain_rows = gain_out

    def stages(b):
        a = {name: act(name, b) for name in ACTS}
        key = lambda *names: [("act", name, b) for name in names]
        part = sz.narrow * sz.shards["down"][0]

        def again(*names):
            if b == 1:
                for name in names:
                    fetch_act(name, 0)

        def down_grad(first, last):
            ready(*key("active"))

            def body(j):
                g = dot(a["active"][:, ds(j * part, part)], low[...], 0, 0).astype(BF)
                grads[("down", b)][j // 2, j % 2] = g.reshape(sz.narrow, part // sz.narrow, w)

            loop(last, body, first)
            if last * part == sz.hidden:
                again("active")

        def hidden_grad(first, last):
            ready(("full", "down", b), *key("slope", "mlp"))

            def body(j):
                at = ds(j * part, part)
                rows = full[("down", b)][j // 2, j % 2].reshape(part, w)
                g = dot(low[...], rows, 1, 1) * a["slope"][:, at].astype(F32)
                g = g.astype(BF)
                a["slope"][:, at] = g
                grads[("in", b)][:, :, :, :, at] = dot(a["mlp"][...], g, 0, 0).astype(BF).reshape(
                    sz.mesh_dims + (sz.shards["in"][0], part)
                )

            loop(last, body, first)
            if last * part == sz.hidden:
                again("mlp")

        def back_rows(src, weight, put):
            zs = sz.depth // 2

            def body(j):
                rows = weight[ds(j * zs, zs)]
                rows = rows.reshape(w // 2, rows.shape[-1])
                put(ds(j * (w // 2), w // 2), dot(src[...], rows, 1, 1))

            loop(2, body)

        def mlp_back():
            ready(("full", "in", b))

            def put(at, x):
                grad_norm[:, at] = x

            back_rows(a["slope"], full[("in", b)], put)
            again("slope")

        def norm2_back():
            ready(*key("middle"))
            norm_back(a["middle"], grad_norm, gain_row(gains, 2 * b + 1), grad, grad_mid, low, sums, ROWS)
            put_gain(2 * b + 1)
            again("middle")

        def out_grad():
            ready(*key("att"))

            def body(j):
                at = ds(j * TILE, TILE)
                g = dot(a["att"][...], low[:, at], 0, 0).astype(BF)
                grads[("out", b)][:, :, :, :, at] = g.reshape(sz.mesh_dims + (sz.shards["out"][0], TILE))

            loop(w // TILE, body)
            again("att")

        def att_back():
            ready(("full", "out", b))

            def put(at, x):
                grad_att[:, at] = x.astype(BF)

            back_rows(low, full[("out", b)], put)

        def attend(first, last):
            ready(*key("qkv", "probs"))
            if b == 0:
                spatial_backward(a["qkv"], a["probs"], grad_att, sz.patches, w, first, last)
            else:
                temporal_backward(a["qkv"], a["probs"], grad_att, sz.slots, w, first, last)

        def qkv_grad(first, last):
            ready(*key("normed"))

            def body(j):
                at = ds(j * TILE, TILE)
                g = dot(a["normed"][...], a["qkv"][:, at], 0, 0).astype(BF)
                grads[("qkv", b)][:, :, :, :, at] = g.reshape(sz.mesh_dims + (sz.shards["qkv"][0], TILE))

            loop(last, body, first)
            if last * TILE == 3 * w:
                again("normed")

        def qkv_back():
            ready(("full", "qkv", b))

            def put(at, x):
                grad_norm[:, at] = x

            back_rows(a["qkv"], full[("qkv", b)], put)
            again("qkv")

        def norm1_back():
            if b == 1:
                ready(("h1",))
            src = h1 if b == 1 else video
            if b == 1:
                norm_back(src, grad_norm, gain_row(gains, 2), grad_mid, grad, low, sums, ROWS)
            else:
                norm_back(src, grad_norm, gain_row(gains, 0), grad_mid, None, grad_video, sums, ROWS)
            put_gain(2 * b)

        def reorder():
            view = grad.reshape(sz.patches // SUB, sz.group, w)

            def body(s):
                rows = view[:, ds(s * SUB, SUB), :].reshape(sz.patches, w)
                at = ds(s * sz.patches, sz.patches)
                grad_norm[at, :] = rows
                low[at, :] = rows.astype(BF)

            loop(sz.slots, body)
            loop(sz.slots, lambda s: move(ds(s * sz.patches, sz.patches)))

        def move(at):
            grad[at, :] = grad_norm[at, :]

        n_q, n_f = 3 * w // TILE, sz.hidden // part
        n_a = sz.slots if b == 0 else sz.patches // (2 * SUB)
        cuts = [n_a * i // 4 for i in range(5)]
        todo = []
        if b == 1:
            todo += [start]
        todo += [functools.partial(down_grad, n_f * i // 2, n_f * (i + 1) // 2) for i in range(2)]
        todo += [functools.partial(hidden_grad, n_f * i // 4, n_f * (i + 1) // 4) for i in range(4)]
        todo += [mlp_back, norm2_back, out_grad, att_back]
        todo += [functools.partial(attend, cuts[i], cuts[i + 1]) for i in range(4)]
        todo += [functools.partial(qkv_grad, n_q * i // 2, n_q * (i + 1) // 2) for i in range(2)]
        todo += [qkv_back, norm1_back]
        if b == 1:
            todo += [reorder]
        return todo

    def spread_gain():
        tile = gain_out[...]
        grads[("gain", 0)][...] = jnp.broadcast_to(tile, sz.full("gain"))

    work = iter(stages(1) + stages(0) + [spread_gain])
    for op in plan:
        if op is None:
            next(work)()
        else:
            scatters[SCATTER_ORDER[op[0]]].step(op[1])
    assert next(work, None) is None
    for scatter in scatters.values():
        scatter.finish()


BACKWARD_STAGES = 39


def backward_plan():
    plan = [None] * BACKWARD_STAGES
    for k in range(9):
        for s in range(5):
            plan.append((k, s))
    return plan


def gain_tile(attn_gain, mlp_gain, index):
    own = jnp.stack([attn_gain[0], mlp_gain[0], attn_gain[1], mlp_gain[1]])
    per = LANES // own.shape[1]
    values = jnp.repeat(jnp.tile(own, (1, per)), 4, axis=0)
    row = lax.broadcasted_iota(jnp.int32, values.shape, 0) % 4
    lane = lax.broadcasted_iota(jnp.int32, values.shape, 1) // own.shape[1]
    return jnp.where(row * per + lane == index, values, 0.0).astype(BF)


def by_kernels(mesh, sz):
    vmem = pl.BlockSpec(memory_space=pltpu.VMEM)
    smem = pl.BlockSpec(memory_space=pltpu.SMEM)
    anyw = pl.BlockSpec(memory_space=pl.ANY)
    shape = jax.ShapeDtypeStruct
    t, w = sz.tokens, sz.width
    act_shapes = [shape(*sz.acts(b)[name]) for b in range(2) for name in ACTS]
    full_shapes = [shape(sz.full(name), BF) for name, _ in keys_of_weights()]
    h1_shape = shape((t, w), F32)
    params = dict(has_side_effects=True, vmem_limit_bytes=VMEM_LIMIT)

    def landing(key):
        full = sz.full(key[0])
        kind = F32 if key[0] == "gain" else BF
        z, _, n, r, c = full
        return [
            pltpu.VMEM(s, kind) for s in ((z, n, r, c), (2, z, r, c), (z, r, c), (z - 1, r, c))
        ]

    def run(video, frames, cotangent, qkv_weight, out_weight, in_weight, down_weight, attn_gain, mlp_gain):
        index = lax.axis_index("wide") * sz.narrow + lax.axis_index("narrow")
        tile = gain_tile(attn_gain, mlp_gain, index)
        rows = video.reshape(t, w)
        slots = 2 * sz.depth + 6
        out, gains, h1, *rest = pl.pallas_call(
            functools.partial(forward_kernel, sz, forward_plan()),
            out_shape=[shape((sz.slots, sz.patches, w), BF), shape((4, w), F32), h1_shape] + act_shapes + full_shapes,
            in_specs=[vmem, smem] + [vmem] * 5,
            out_specs=[vmem, vmem] + [anyw] * 25,
            scratch_shapes=[pltpu.VMEM(s.shape, s.dtype) for s in act_shapes]
            + [pltpu.VMEM(sz.full(name), BF) for name, _ in GATHER_ORDER]
            + [
                pltpu.VMEM((t, w), F32),
                pltpu.VMEM((t, w), F32),
                pltpu.VMEM((sz.group, LANES), F32),
                pltpu.SemaphoreType.DMA((9, sz.depth + 6)),
                pltpu.SemaphoreType.DMA((9, sz.depth + 6)),
                pltpu.SemaphoreType.DMA((25,)),
            ],
            compiler_params=pltpu.CompilerParams(collective_id=0, **params),
        )(rows, frames, tile, qkv_weight, out_weight, in_weight, down_weight)
        acts0 = sz.acts(0)
        res = pl.pallas_call(
            functools.partial(backward_kernel, sz, backward_plan()),
            out_shape=[shape((t, w), BF)]
            + [shape((2,) + sz.shards[name], F32) for name in NAMES]
            + [shape(TILE_GAIN, F32)],
            in_specs=[vmem, vmem, smem, vmem] + [anyw] * 25,
            out_specs=[vmem] * 6,
            scratch_shapes=[pltpu.VMEM(*acts0[name]) for name in ACTS]
            + [pltpu.VMEM(*sz.acts(1)["probs"]), pltpu.VMEM((t, w), F32)]
            + [pltpu.VMEM(sz.full(name), BF) for name, _ in keys_of_weights()]
            + [pltpu.VMEM(sz.full(name), BF) for name in NAMES]
            + [pltpu.VMEM(sz.full("gain"), F32)]
            + [buffer for key in SCATTER_ORDER for buffer in landing(key)]
            + [
                pltpu.VMEM((t, w), F32),
                pltpu.VMEM((t, w), F32),
                pltpu.VMEM((t, w), F32),
                pltpu.VMEM((t, w), BF),
                pltpu.VMEM((t, w), BF),
                pltpu.VMEM((SUB, w), F32),
                pltpu.SemaphoreType.DMA((9, sz.depth + 3)),
                pltpu.SemaphoreType.DMA((9, sz.depth + 3)),
                pltpu.SemaphoreType.DMA((2, 5)),
                pltpu.SemaphoreType.DMA((2, 8)),
            ],
            compiler_params=pltpu.CompilerParams(collective_id=1, **params),
        )(rows, cotangent.reshape(sz.slots, sz.patches, w), frames, gains, h1, *rest)
        grad_video, *grads, gain_sums = res
        per = w // LANES
        own = attn_gain.shape[1]
        gain_sums = gain_sums.reshape(4, per * (LANES // own), own)
        mine = lax.dynamic_index_in_dim(gain_sums, index, 1, keepdims=False)
        return (
            out.reshape(video.shape),
            grad_video.reshape(video.shape),
            *grads,
            mine[0::2],
            mine[1::2],
        )

    return run


def norm_rows(inputs, scaling):
    centre = jnp.mean(inputs, axis=-1, keepdims=True)
    centred = inputs - centre
    spread = jnp.mean(centred * centred, axis=-1, keepdims=True)
    return centred * lax.rsqrt(spread + EPS) * scaling


def project(rows_in, matrix):
    return jnp.einsum("cspd,de->cspe", rows_in, matrix, preferred_element_type=jnp.float32)


def project_back(rows_in, matrix):
    return jnp.einsum("cspe,de->cspd", rows_in, matrix, preferred_element_type=jnp.float32)


def weight_grad(left, right):
    return jnp.einsum("cspd,cspe->de", left, right, preferred_element_type=jnp.float32)


def pair_scores(first, second, which_block):
    if which_block == 0:
        return jnp.einsum("csphe,csqhe->cshpq", first, second, preferred_element_type=jnp.float32)
    return jnp.einsum("csphe,ctphe->cphst", first, second, preferred_element_type=jnp.float32)


def pair_mix(weighting, second, which_block):
    if which_block == 0:
        return jnp.einsum(
            "cshpq,csqhe->csphe", weighting, second, preferred_element_type=jnp.float32
        )
    return jnp.einsum("cphst,ctphe->csphe", weighting, second, preferred_element_type=jnp.float32)


def pair_back(weighting, first, which_block):
    if which_block == 0:
        return jnp.einsum(
            "cshpq,csphe->csqhe", weighting, first, preferred_element_type=jnp.float32
        )
    return jnp.einsum("cphst,csphe->ctphe", weighting, first, preferred_element_type=jnp.float32)


def masked_scores(queries, key_rows, which_block, allowed):
    head_size = queries.shape[-1]
    scores = pair_scores(queries, key_rows, which_block) * head_size ** (-0.5)
    if which_block == 1:
        scores = jnp.where(allowed[:, None, None], scores, -1000000000.0)
    return scores


def block_forward(inputs, weights, which_block, allowed):
    qkv_matrix, out_matrix, in_matrix, down_matrix, attn_scaling, mlp_scaling = weights
    full_shape = inputs.shape
    head_size = full_shape[-1] // HEADS
    normed, norm_pull = jax.vjp(norm_rows, inputs, attn_scaling.astype(jnp.float32))
    normed_low = normed.astype(jnp.bfloat16)
    qkv_rows = project(normed_low, qkv_matrix).astype(jnp.bfloat16)
    split = qkv_rows.reshape(full_shape[:3] + (3, HEADS, head_size))
    queries = split[:, :, :, 0]
    key_rows = split[:, :, :, 1]
    value_rows = split[:, :, :, 2]
    scores = masked_scores(queries, key_rows, which_block, allowed)
    row_max = jnp.max(scores, axis=-1, keepdims=True)
    shifted = jnp.exp(scores - row_max)
    row_sum = jnp.sum(shifted, axis=-1, keepdims=True)
    log_total = row_max + jnp.log(row_sum)
    probs_low = (shifted / row_sum).astype(jnp.bfloat16)
    attended = pair_mix(probs_low, value_rows, which_block).reshape(full_shape).astype(jnp.bfloat16)
    middle = inputs + project(attended, out_matrix)
    normed_mlp, mlp_pull = jax.vjp(norm_rows, middle, mlp_scaling.astype(jnp.float32))
    normed_mlp_low = normed_mlp.astype(jnp.bfloat16)
    hidden = project(normed_mlp_low, in_matrix)
    active, gelu_pull = jax.vjp(jax.nn.gelu, hidden)
    active_low = active.astype(jnp.bfloat16)
    result = middle + project(active_low, down_matrix)
    stored = (
        norm_pull,
        normed_low,
        queries,
        key_rows,
        value_rows,
        log_total,
        attended,
        mlp_pull,
        normed_mlp_low,
        gelu_pull,
        active_low,
    )
    return (result, stored)


def block_backward(gradient, stored, weights, which_block, allowed):
    qkv_matrix, out_matrix, in_matrix, down_matrix, attn_scaling, mlp_scaling = weights
    (
        norm_pull,
        normed_low,
        queries,
        key_rows,
        value_rows,
        log_total,
        attended,
        mlp_pull,
        normed_mlp_low,
        gelu_pull,
        active_low,
    ) = stored
    full_shape = gradient.shape
    head_size = queries.shape[-1]
    result_low = gradient.astype(jnp.bfloat16)
    grad_down_w = weight_grad(active_low, result_low)
    grad_active = project_back(result_low, down_matrix)
    grad_hidden = gelu_pull(grad_active)[0].astype(jnp.bfloat16)
    grad_in_w = weight_grad(normed_mlp_low, grad_hidden)
    grad_normed_mlp = project_back(grad_hidden, in_matrix)
    middle_part, grad_mlp_scaling = mlp_pull(grad_normed_mlp)
    grad_middle = gradient + middle_part
    middle_low = grad_middle.astype(jnp.bfloat16)
    grad_out_w = weight_grad(attended, middle_low)
    grad_attended = project_back(middle_low, out_matrix).astype(jnp.bfloat16)
    grad_attended = grad_attended.reshape(queries.shape)
    scores = masked_scores(queries, key_rows, which_block, allowed)
    soft_probs = jnp.exp(scores - log_total)
    grad_probs = pair_scores(grad_attended, value_rows, which_block)
    row_delta = jnp.sum(grad_probs * soft_probs, axis=-1, keepdims=True)
    grad_scores = (soft_probs * (grad_probs - row_delta)).astype(jnp.bfloat16)
    score_scale = head_size ** (-0.5)
    grad_queries = pair_mix(grad_scores, key_rows, which_block) * score_scale
    grad_keys = pair_back(grad_scores, queries, which_block) * score_scale
    grad_values = pair_back(soft_probs.astype(jnp.bfloat16), grad_attended, which_block)
    grad_qkv_rows = jnp.stack([grad_queries, grad_keys, grad_values], axis=3).astype(jnp.bfloat16)
    grad_qkv_rows = grad_qkv_rows.reshape(full_shape[:3] + (3 * full_shape[-1],))
    grad_qkv_w = weight_grad(normed_low, grad_qkv_rows)
    grad_normed = project_back(grad_qkv_rows, qkv_matrix)
    input_part, grad_attn_scaling = norm_pull(grad_normed)
    grad_input = grad_middle + input_part
    return (
        grad_input,
        (grad_qkv_w, grad_out_w, grad_in_w, grad_down_w, grad_attn_scaling, grad_mlp_scaling),
    )


def block_shards(qkv_weight, out_weight, in_weight, down_weight, attn_gain, mlp_gain, block_index):
    return (
        qkv_weight[block_index].astype(jnp.bfloat16),
        out_weight[block_index].astype(jnp.bfloat16),
        in_weight[block_index].astype(jnp.bfloat16),
        down_weight[block_index].astype(jnp.bfloat16),
        attn_gain[block_index].astype(jnp.bfloat16),
        mlp_gain[block_index].astype(jnp.bfloat16),
    )


def by_einsums(
    video, frames, cotangent, qkv_weight, out_weight, in_weight, down_weight, attn_gain, mlp_gain
):
    axes = ("wide", "narrow")
    slot_counts = (frames + 1) // 2
    positions = jnp.arange(video.shape[1], dtype=jnp.int32)
    allowed = (positions[None, None, :] <= positions[None, :, None]) & (
        positions[None, None, :] < slot_counts[:, None, None]
    )
    valid_slot = (positions[None, :] < slot_counts[:, None]).astype(jnp.float32)[:, :, None, None]
    weights = (qkv_weight, out_weight, in_weight, down_weight, attn_gain, mlp_gain)
    full = [
        tuple(lax.all_gather(part, axes, axis=0, tiled=True) for part in block_shards(*weights, b))
        for b in range(2)
    ]
    spatial_out, spatial_stored = block_forward(video.astype(jnp.float32), full[0], 0, allowed)
    temporal_out, temporal_stored = block_forward(spatial_out, full[1], 1, allowed)
    output = (temporal_out * valid_slot).astype(jnp.bfloat16)
    gradient = cotangent.astype(jnp.float32) * valid_slot
    grad_between, temporal_grads = block_backward(gradient, temporal_stored, full[1], 1, allowed)
    grad_start, spatial_grads = block_backward(grad_between, spatial_stored, full[0], 0, allowed)
    summed = [
        lax.psum_scatter(jnp.stack(pair), axes, scatter_dimension=1, tiled=True)
        for pair in zip(spatial_grads, temporal_grads)
    ]
    return (output, grad_start.astype(jnp.bfloat16), *summed)


def solution(mesh):
    both = ("wide", "narrow")
    clips = P(both, None, None, None)
    rows = P(None, both, None)
    in_specs = (clips, P(both), clips, rows, rows, rows, rows, P(None, both), P(None, both))
    out_specs = (clips, clips, rows, rows, rows, rows, P(None, both), P(None, both))

    def shards(*args):
        sz = Sizes(mesh, args[0], args[5])
        whole_tiles = all(rows % 16 == 0 for rows, _ in sz.shards.values())
        if whole_tiles and sz.narrow == 4 and args[0].shape[0] == 1:
            return by_kernels(mesh, sz)(*args)
        return by_einsums(*args)

    return jax.shard_map(shards, mesh=mesh, in_specs=in_specs, out_specs=out_specs, check_vma=False)
```

```python
import functools

import jax
import jax.numpy as jnp
from jax import lax
from jax.experimental import pallas as pl
from jax.experimental.pallas import tpu as pltpu
from jax.sharding import PartitionSpec as P

HEADS = 8
EPS = 1e-05
BF = jnp.bfloat16
F32 = jnp.float32
MESH = pl.DeviceIdType.MESH
VMEM_LIMIT = 62 * 2**20


def dot(a, b, ca, cb):
    return lax.dot_general(a, b, (((ca,), (cb,)), ((), ())), preferred_element_type=F32)


def ds(start, size):
    if isinstance(start, int):
        return pl.ds(start, size)
    return pl.ds(pl.multiple_of(start, size), size)


def loop(count, body, first=0):
    if count - first == 1:
        body(first)
        return

    def step(i, carry):
        body(i)
        return carry

    lax.fori_loop(first, count, step, 0)


class Place:
    def __init__(self, depth):
        self.depth = depth
        self.w = lax.axis_index("wide")
        self.n = lax.axis_index("narrow")
        self.z = self.w // 2
        self.c = self.w % 2
        first = 1 + self.c
        self.na = self.flip(self.n, first)
        self.nb = self.flip(self.n, 3 - first)
        self.nab = 3 - self.n

    @staticmethod
    def flip(n, step):
        bit = (n // step) % 2
        return n + step - 2 * step * bit

    def sib(self):
        return (self.z * 2 + 1 - self.c, self.n)

    def a(self):
        return (self.w, self.na)

    def b(self):
        return (self.w, self.nb)

    def along(self, d):
        return (lax.rem(self.z + d, self.depth) * 2 + self.c, self.n)

    def zat(self, d):
        return lax.rem(self.z + d, self.depth)

    def greet(self):
        bar = pltpu.get_barrier_semaphore()
        targets = [self.sib(), self.a(), self.b()] + [self.along(d) for d in range(1, self.depth)]
        for t in targets:
            pl.semaphore_signal(bar, inc=1, device_id=t, device_id_type=MESH)
        pl.semaphore_wait(bar, len(targets))


def remote(src, dst, send, recv, target):
    return pltpu.make_async_remote_copy(src, dst, send, recv, device_id=target, device_id_type=MESH)


class Gather:
    def __init__(self, place, full, send, recv, early_a):
        self.p, self.full, self.send, self.recv, self.early_a = place, full, send, recv, early_a
        self.started = []
        self.slot_a = 2 * place.depth - 2
        self.slot_b = self.slot_a + 1
        self.slot_sib = self.slot_b + 2

    @staticmethod
    def semaphores(depth):
        return 2 * depth + 5

    def go(self, slot, index, target):
        view = self.full.at[index]
        copy = remote(view, view, self.send.at[slot], self.recv.at[slot], target)
        copy.start()
        self.started.append(copy)

    def take(self, slot, index):
        view = self.full.at[index]
        remote(view, view, self.send.at[slot], self.recv.at[slot], self.p.sib()).wait_recv()

    def column(self, n, core=None):
        return (slice(None), self.p.c if core is None else core, n)

    def along(self, first, n):
        p = self.p
        for d in range(1, p.depth):
            self.go(first + d - 1, (p.z, p.c, n), p.along(d))

    def take_along(self, first, n):
        p = self.p
        for d in range(1, p.depth):
            self.take(first + d - 1, (p.zat(p.depth - d), p.c, n))

    def sibling(self, slot, n):
        self.go(self.slot_sib + slot, self.column(n), self.p.sib())

    def step0(self):
        p = self.p
        if self.early_a:
            self.go(self.slot_a, (p.z, p.c, p.n), p.a())
        self.along(0, p.n)

    def step1(self):
        p = self.p
        if self.early_a:
            self.take(self.slot_a, (p.z, p.c, p.na))
            self.along(p.depth - 1, p.na)
        else:
            self.take_along(0, p.n)
            self.go(self.slot_a, self.column(p.n), p.a())
            self.go(self.slot_b, self.column(p.n), p.b())
            self.sibling(0, p.n)

    def step2(self):
        p = self.p
        if self.early_a:
            self.take_along(0, p.n)
            self.go(self.slot_b, self.column(p.n), p.b())
            self.sibling(0, p.n)
            self.take_along(p.depth - 1, p.na)
        else:
            self.take(self.slot_a, self.column(p.na))
        self.go(self.slot_b + 1, self.column(p.na), p.b())
        self.sibling(1, p.na)

    def step3(self):
        p = self.p
        self.take(self.slot_b, self.column(p.nb))
        self.sibling(2, p.nb)
        self.take(self.slot_b + 1, self.column(p.nab))
        self.sibling(3, p.nab)

    def step4(self):
        p = self.p
        for slot, n in enumerate((p.n, p.nb, p.na, p.nab)):
            self.take(self.slot_sib + slot, self.column(n, 1 - p.c))

    def finish(self):
        for copy in self.started:
            copy.wait_send()

    def step(self, i):
        (self.step0, self.step1, self.step2, self.step3, self.step4)[i]()


class Scatter:
    def __init__(self, place, full, from_sib, from_b, from_a, from_z, out, send, recv, late_a):
        self.p, self.full, self.out, self.send, self.recv = place, full, out, send, recv
        self.from_sib, self.from_b, self.from_a, self.from_z = from_sib, from_b, from_a, from_z
        self.late_a = late_a
        self.started = []

    @staticmethod
    def semaphores(depth):
        return 2 * depth + 2

    @staticmethod
    def landing(full, late_a):
        z, _, n, r, c = full
        a = (1, r, c) if late_a else (z, r, c)
        return [(z, n, r, c), (2, z, r, c), a, ((2 if late_a else 1) * (z - 1), r, c)]

    def go(self, slot, src, dst, target):
        copy = remote(src, dst, self.send.at[slot], self.recv.at[slot], target)
        copy.start()
        self.started.append(copy)

    def take(self, slot, view):
        remote(view, view, self.send.at[slot], self.recv.at[slot], self.p.sib()).wait_recv()

    def add(self, n, part):
        c = self.p.c
        for z in range(self.p.depth):
            self.full[z, c, n] = self.full[z, c, n] + part(z)

    def along(self, first, n):
        p = self.p
        for d in range(1, p.depth):
            slot = first + d - 1
            self.go(4 + slot, self.full.at[p.zat(d), p.c, n], self.from_z.at[slot], p.along(d))

    def sum_along(self, first, n):
        p = self.p
        total = self.full[p.z, p.c, n].astype(F32)
        for d in range(1, p.depth):
            slot = first + d - 1
            self.take(4 + slot, self.from_z.at[slot])
            total = total + self.from_z[slot].astype(F32)
        return total

    def step0(self):
        self.go(0, self.full.at[:, 1 - self.p.c], self.from_sib, self.p.sib())

    def step1(self):
        p = self.p
        self.take(0, self.from_sib)
        for slot, n in ((1, p.nab), (2, p.nb)):
            self.add(n, lambda z, n=n: self.from_sib[z, n])
            self.go(slot, self.full.at[:, p.c, n], self.from_b.at[slot - 1], p.b())
        for n in (p.na, p.n):
            self.add(n, lambda z, n=n: self.from_sib[z, n])

    def step2(self):
        p = self.p
        self.take(1, self.from_b.at[0])
        self.add(p.na, lambda z: self.from_b[0, z])
        if self.late_a:
            self.along(p.depth - 1, p.na)
        else:
            self.go(3, self.full.at[:, p.c, p.na], self.from_a, p.a())
        self.take(2, self.from_b.at[1])
        self.add(p.n, lambda z: self.from_b[1, z])
        if self.late_a:
            self.along(0, p.n)

    def step3(self):
        p = self.p
        if self.late_a:
            self.full[p.z, p.c, p.na] = self.sum_along(p.depth - 1, p.na).astype(self.full.dtype)
            self.go(3, self.full.at[p.z, p.c, p.na], self.from_a.at[0], p.a())
            self.out[...] = self.sum_along(0, p.n)
        else:
            self.take(3, self.from_a)
            self.add(p.n, lambda z: self.from_a[z])
            self.along(0, p.n)

    def step4(self):
        p = self.p
        if self.late_a:
            self.take(3, self.from_a.at[0])
            self.out[...] = self.out[...] + self.from_a[0].astype(F32)
        else:
            self.out[...] = self.sum_along(0, p.n)

    def finish(self):
        for copy in self.started:
            copy.wait_send()

    def step(self, i):
        (self.step0, self.step1, self.step2, self.step3, self.step4)[i]()


def stats(x):
    centre = jnp.mean(x, axis=-1, keepdims=True)
    centred = x - centre
    spread = jnp.mean(centred * centred, axis=-1, keepdims=True)
    r = lax.rsqrt(spread + EPS)
    return centred * r, r


def norm_into(src, gain, dst, rows):
    total = src.shape[0]

    def body(i):
        at = ds(i * rows, rows)
        xn, _ = stats(src[at, :].astype(F32))
        dst[at, :] = (xn * gain).astype(BF)

    loop(total // rows, body)


def halves(shape):
    return lax.broadcasted_iota(jnp.int32, shape, 1) < shape[1] // 2


def split_heads(x):
    low = halves(x.shape)
    zero = jnp.zeros_like(x)
    return jnp.concatenate([jnp.where(low, x, zero), jnp.where(low, zero, x)], 0)


def head_ones(keys):
    shape = (2 * keys, LANES)
    row = lax.broadcasted_iota(jnp.int32, shape, 0) < keys
    low = lax.broadcasted_iota(jnp.int32, shape, 1) < LANES // 2
    return jnp.where(row == low, 1.0, 0.0).astype(BF)


def unroll(first, last, body):
    for i in range(first, last):
        body(i)


def spatial_forward(qkv, probs, att, patches, width, first, last):
    head = width // HEADS
    scale = head ** -0.5
    pairs = range(HEADS // 2)
    ones = head_ones(patches)

    def body(s):
        at = ds(s * patches, patches)
        parts = []
        for pair in pairs:
            lane = pair * 2 * head
            q = qkv[at, lane : lane + 2 * head]
            parts.append(dot(q, split_heads(qkv[at, width + lane : width + lane + 2 * head]), 1, 1))
        scores = jnp.concatenate(parts, 0) * scale
        low = halves(scores.shape)
        top0 = jnp.max(jnp.where(low, scores, -jnp.inf), axis=-1, keepdims=True)
        top1 = jnp.max(jnp.where(low, -jnp.inf, scores), axis=-1, keepdims=True)
        e = jnp.exp(scores - jnp.where(low, top0, top1))
        e_low = e.astype(BF)
        parts = []
        for pair in pairs:
            lane = pair * 2 * head
            v2 = split_heads(qkv[at, 2 * width + lane : 2 * width + lane + 2 * head])
            rows = slice(pair * patches, (pair + 1) * patches)
            parts.append(dot(e_low[rows], jnp.concatenate([v2, ones], 1), 1, 0))
        both = jnp.concatenate(parts, 0)
        r = 1.0 / both[:, 2 * head :]
        probs[s] = (e * r).astype(BF).reshape(HEADS // 2, patches, 2 * patches)
        new = (both[:, : 2 * head] * r).astype(BF)
        for pair in pairs:
            att[at, pair * 2 * head : (pair + 1) * 2 * head] = new[pair * patches : (pair + 1) * patches]

    unroll(first, last, body)


def pad_heads(x, lanes):
    low = halves(x.shape)
    zero = jnp.zeros_like(x)
    fill = jnp.zeros((lanes - x.shape[0], x.shape[1]), x.dtype)
    return jnp.concatenate([jnp.where(low, x, zero), fill, jnp.where(low, zero, x), fill], 0).astype(BF)


LANES = 128
SUB = 8


def temporal_forward(qkv, probs, att, bias, slots, width, first, last):
    head = width // HEADS
    scale = head ** -0.5
    group = slots * SUB
    pairs = range(HEADS // 2)
    parts_of = [slice(half * group, (half + 1) * group) for half in range(2)]

    def body(i):
        at = ds(i * 2 * group, 2 * group)
        parts = []
        for pair in pairs:
            lane = pair * 2 * head
            q = qkv[at, lane : lane + 2 * head].astype(F32)
            k = qkv[at, width + lane : width + lane + 2 * head].astype(F32)
            for rows in parts_of:
                x = dot(q[rows].astype(BF), pad_heads(k[rows], LANES), 1, 1)
                parts += [x[:, :LANES], x[:, LANES:]]
        scores = jnp.stack(parts, 0) * scale + bias[...][None]
        e = jnp.exp(scores - jnp.max(scores, axis=-1, keepdims=True))
        p = (e / jnp.sum(e, axis=-1, keepdims=True)).astype(BF)
        for pair in pairs:
            lane = pair * 2 * head
            v = qkv[at, 2 * width + lane : 2 * width + lane + 2 * head].astype(F32)
            out = []
            for half, rows in enumerate(parts_of):
                j = (pair * 2 + half) * 2
                both = jnp.concatenate([p[j], p[j + 1]], 1)
                probs[i * 2 + half, pair] = both
                out.append(dot(both, pad_heads(v[rows], LANES), 1, 0))
            att[at, lane : lane + 2 * head] = jnp.concatenate(out, 0).astype(BF)

    unroll(first, last, body)


def make_bias(bias, count, slots):
    group = slots * SUB
    q = lax.broadcasted_iota(jnp.int32, (group, LANES), 0)
    k = lax.broadcasted_iota(jnp.int32, (group, LANES), 1)
    sq, sk = q // SUB, k // SUB
    ok = (q - sq * SUB == k - sk * SUB) & (sk <= sq) & (sk < count)
    bias[...] = jnp.where(ok, 0.0, -1e9)


def gelu_pair(z):
    k0 = 0.7978845608028654
    k1 = k0 * 0.044715
    z2 = z * z
    half = 0.5 + 0.5 * jnp.tanh(z * (k0 + k1 * z2))
    active = z * half
    slope = half + half * (z - active) * (2.0 * k0 + 6.0 * k1 * z2)
    return active, slope


def wide_rows(ref, width, columns=None):
    x = ref[...] if columns is None else ref[:, :, :, :, columns]
    return x.reshape(width, x.shape[-1])


def unsplit_heads(x, second, rows):
    low = halves((rows, x.shape[1]))
    return jnp.where(low, x[:rows], x[second : second + rows])


def spatial_backward(qkv, probs, grad, patches, width, first, last):
    head = width // HEADS
    scale = head ** -0.5
    pairs = range(HEADS // 2)
    rows_of = [slice(pair * patches, (pair + 1) * patches) for pair in pairs]

    def body(s):
        at = ds(s * patches, patches)
        cols = [[slice(t * width + p * 2 * head, t * width + (p + 1) * 2 * head) for t in range(3)] for p in pairs]
        p_low = probs[s].reshape(HEADS // 2 * patches, 2 * patches)
        soft = p_low.astype(F32)
        q = [qkv[at, cols[p][0]] for p in pairs]
        k2 = [split_heads(qkv[at, cols[p][1]]) for p in pairs]
        g = [grad[at, p * 2 * head : (p + 1) * 2 * head] for p in pairs]
        gp = [dot(g[p], split_heads(qkv[at, cols[p][2]]), 1, 1) for p in pairs]
        gv = [dot(p_low[rows_of[p]], g[p], 0, 0) for p in pairs]
        gp = jnp.concatenate(gp, 0)
        low = halves(gp.shape)
        both = gp * soft
        sum0 = jnp.sum(jnp.where(low, both, 0.0), axis=-1, keepdims=True)
        sum1 = jnp.sum(jnp.where(low, 0.0, both), axis=-1, keepdims=True)
        gs = (soft * (gp - jnp.where(low, sum0, sum1))).astype(BF)
        gq = [dot(gs[rows_of[p]], k2[p], 1, 0) for p in pairs]
        gk = [dot(gs[rows_of[p]], q[p], 0, 0) for p in pairs]
        for p in pairs:
            qkv[at, cols[p][0]] = (gq[p] * scale).astype(BF)
            qkv[at, cols[p][1]] = (unsplit_heads(gk[p], patches, patches) * scale).astype(BF)
            qkv[at, cols[p][2]] = unsplit_heads(gv[p], patches, patches).astype(BF)

    unroll(first, last, body)


def temporal_backward(qkv, probs, grad, slots, width, first, last):
    head = width // HEADS
    scale = head ** -0.5
    group = slots * SUB
    pairs = range(HEADS // 2)
    parts_of = [slice(half * group, (half + 1) * group) for half in range(2)]

    def body(i):
        at = ds(i * 2 * group, 2 * group)
        cols = [[slice(t * width + p * 2 * head, t * width + (p + 1) * 2 * head) for t in range(3)] for p in pairs]
        qs, ks, gs_in, ps, gp, soft = [], [], [], [], [], []
        for pair in pairs:
            q, k, v = (qkv[at, c].astype(F32) for c in cols[pair])
            g = grad[at, pair * 2 * head : (pair + 1) * 2 * head].astype(F32)
            for half, rows in enumerate(parts_of):
                qs.append(q[rows].astype(BF))
                ks.append(pad_heads(k[rows], LANES))
                gs_in.append(g[rows].astype(BF))
                p = probs[i * 2 + half, pair]
                ps.append(p)
                x = dot(gs_in[-1], pad_heads(v[rows], LANES), 1, 1)
                wide = p.astype(F32)
                gp += [x[:, :LANES], x[:, LANES:]]
                soft += [wide[:, :LANES], wide[:, LANES:]]
        many = range(len(ps))
        gv = [unsplit_heads(dot(ps[j], gs_in[j], 0, 0), LANES, group) for j in many]
        gp = jnp.stack(gp, 0)
        soft = jnp.stack(soft, 0)
        delta = jnp.sum(gp * soft, axis=-1, keepdims=True)
        gs = (soft * (gp - delta)).astype(BF)
        gs = [jnp.concatenate([gs[2 * j], gs[2 * j + 1]], 1) for j in many]
        gq = [dot(gs[j], ks[j], 1, 0) * scale for j in many]
        gk = [unsplit_heads(dot(gs[j], qs[j], 0, 0), LANES, group) * scale for j in many]
        for pair in pairs:
            for c, outs in zip(cols[pair], (gq, gk, gv)):
                qkv[at, c] = jnp.concatenate(outs[2 * pair : 2 * pair + 2], 0).astype(BF)

    unroll(first, last, body)


def norm_back(src, grad, gain, base, dst, low, sums, rows):
    total, width = grad.shape
    sums[...] = jnp.zeros_like(sums)

    def body(i):
        at = ds(i * rows, rows)
        xn, r = stats(src[at, :].astype(F32))
        g = grad[at, :]
        e = g * gain
        inner = e - jnp.mean(e, axis=-1, keepdims=True) - xn * jnp.mean(e * xn, axis=-1, keepdims=True)
        res = base[at, :] + r * inner
        if dst is not None:
            dst[at, :] = res
        low[at, :] = res.astype(BF)
        sums[...] += jnp.sum((g * xn).reshape(rows // SUB, SUB, width), axis=0)

    loop(total // rows, body)


def gain_row(gains, which):
    return gains[which : which + 1, :]


class Sizes:
    def __init__(self, mesh, video, in_weight):
        self.depth = mesh.shape["wide"] // 2
        self.narrow = mesh.shape["narrow"]
        self.slots, self.patches, self.width = video.shape[1:]
        self.hidden = in_weight.shape[2]
        self.tokens = self.slots * self.patches
        self.group = self.slots * SUB
        devices = 2 * self.depth * self.narrow
        w = self.width // devices
        self.shards = {
            "qkv": (w, 3 * self.width),
            "out": (w, self.width),
            "in": (w, self.hidden),
            "down": (self.hidden // devices, self.width),
        }
        self.mesh_dims = (self.depth, 2, self.narrow)

    def full(self, name):
        return self.mesh_dims + (TILE_GAIN if name == "gain" else self.shards[name])

    def acts(self, b):
        t, w, f = self.tokens, self.width, self.hidden
        pairs = HEADS // 2
        if b == 0:
            probs = (self.slots, pairs, self.patches, 2 * self.patches)
        else:
            probs = (self.patches // SUB, pairs, self.group, 2 * LANES)
        return {
            "normed": ((t, w), BF),
            "qkv": ((t, 3 * w), BF),
            "probs": (probs, BF),
            "att": ((t, w), BF),
            "middle": ((t, w), F32),
            "mlp": ((t, w), BF),
            "active": ((t, f), BF),
            "slope": ((t, f), BF),
        }


TILE_GAIN = (16, LANES)
NAMES = ("qkv", "out", "in", "down")
ACTS = ("normed", "qkv", "probs", "att", "middle", "mlp", "active", "slope")
SPLIT = {"gain": 1, "qkv": 2, "out": 1, "in": 2, "down": 2}


def pieces_of(name, b):
    return [(name, b, i) for i in range(SPLIT[name])]


GAIN = ("gain", 0)
GATHER_ORDER = [(*GAIN, 0)] + [piece for b in range(2) for name in NAMES for piece in pieces_of(name, b)]
SCATTER_ORDER = [
    piece for b in (1, 0) for name in ("down", "in", "out", "qkv") for piece in pieces_of(name, b)
] + [(*GAIN, 0)]


def columns_of(piece, columns):
    name, _, i = piece
    part = columns // SPLIT[name]
    return slice(i * part, (i + 1) * part)


def row_tile(tokens):
    return tokens // 2 if tokens % 32 == 0 else tokens


def keys_of_weights():
    return [(name, b) for b in range(2) for name in NAMES]


def keys_of_acts():
    return [(name, b) for b in range(2) for name in ACTS]


def forward_kernel(sz, plan, types, *refs):
    refs = list(refs)

    def grab(n):
        taken, refs[:n] = refs[:n], []
        return taken

    video, frames, attn_gain, mlp_gain = grab(4)
    shard = dict(zip(NAMES, grab(4)))
    (out,) = grab(1)
    (gains,) = grab(1)
    h1_hbm, = grab(1)
    acts_hbm = dict(zip(keys_of_acts(), grab(16)))
    full_hbm = dict(zip(keys_of_weights(), grab(8)))
    acts = dict(zip(keys_of_acts(), grab(16)))
    full = dict(zip([GAIN] + keys_of_weights(), grab(9)))
    h1, result, bias, send, recv, local = grab(6)
    assert not refs

    place = Place(sz.depth)
    place.greet()
    gathers = {}
    for k, piece in enumerate(GATHER_ORDER):
        view = full[piece[:2]]
        if SPLIT[piece[0]] > 1:
            view = view.at[:, :, :, :, columns_of(piece, view.shape[-1])]
        gathers[piece] = Gather(place, view, send.at[k], recv.at[k], types[k])
    filled = set()
    arrived = set()
    saved = []

    def save(src, dst):
        copy = pltpu.make_async_copy(src, dst, local.at[len(saved)])
        copy.start()
        saved.append(copy)

    def comm(piece, step):
        key = piece[:2]
        if step == 0 and key not in filled:
            filled.add(key)
            own = (place.z, place.c, place.n)
            if key == GAIN:
                full[key][own] = place_gains(attn_gain, mlp_gain, place.w * sz.narrow + place.n)
            else:
                full[key][own] = shard[key[0]][key[1]].astype(BF)
        gathers[piece].step(step)
        if step == 4 and key != GAIN:
            arrived.add(piece)
            if all(part in arrived for part in pieces_of(*key)):
                save(full[key], full_hbm[key])

    count = (frames[0] + 1) // 2
    t, w = sz.tokens, sz.width

    def stage_gain():
        make_bias(bias, count, sz.slots)
        tile = jnp.sum(full[GAIN][...].astype(F32).reshape(-1, 16, LANES), axis=0)
        for g in range(4):
            rows = [tile[g * 4 + r : g * 4 + r + 1, :] for r in range(w // LANES)]
            gains[g : g + 1, :] = jnp.concatenate(rows, 1)

    def stages(b):
        a = {name: acts[(name, b)] for name in ACTS}
        h = video if b == 0 else h1

        def keep(*names):
            for name in names:
                save(a[name], acts_hbm[(name, b)])

        def norm1():
            norm_into(h, gain_row(gains, 2 * b), a["normed"], row_tile(t))
            keep("normed")

        def qkv(first, last):
            at = slice(first, last)
            a["qkv"][:, at] = dot(a["normed"][...], wide_rows(full[("qkv", b)], w, at), 1, 0).astype(BF)
            if last == 3 * w:
                keep("qkv")

        def attend(first, last):
            if b == 0:
                spatial_forward(a["qkv"], a["probs"], a["att"], sz.patches, w, first, last)
                end = sz.slots
            else:
                temporal_forward(a["qkv"], a["probs"], a["att"], bias, sz.slots, w, first, last)
                end = sz.patches // (2 * SUB)
            if last == end:
                keep("probs", "att")

        def project():
            new = dot(a["att"][...], wide_rows(full[("out", b)], w), 1, 0)
            a["middle"][...] = h[...].astype(F32) + new
            keep("middle")

        def norm2():
            norm_into(a["middle"], gain_row(gains, 2 * b + 1), a["mlp"], row_tile(t))
            keep("mlp")

        def expand(first, last):
            at = slice(first, last)
            weight = wide_rows(full[("in", b)], w, at)
            rows = row_tile(t)
            for r in range(0, t, rows):
                active, slope = gelu_pair(dot(a["mlp"][r : r + rows, :], weight, 1, 0))
                a["active"][r : r + rows, at] = active.astype(BF)
                a["slope"][r : r + rows, at] = slope.astype(BF)
            if last == sz.hidden:
                keep("active", "slope")

        def contract(first, last):
            at = slice(first, last)
            new = a["middle"][:, at] + dot(a["active"][...], wide_rows(full[("down", b)], sz.hidden, at), 1, 0)
            if b == 0:
                new = new.reshape(sz.slots, sz.patches // SUB, SUB, last - first)
                for s in range(sz.slots):
                    h1_view[:, s * SUB : (s + 1) * SUB, at] = new[s]
                if last == w:
                    save(h1, h1_hbm)
            else:
                result[:, at] = new

        def write():
            valid = lax.broadcasted_iota(jnp.int32, (sz.slots, 1, 1), 0) < count

            def body(i):
                rows = result[ds(i * 2 * sz.group, 2 * sz.group), :]
                rows = rows.reshape(2, sz.slots, SUB, w)
                rows = jnp.concatenate([rows[0], rows[1]], axis=1)
                out[:, ds(i * 2 * SUB, 2 * SUB), :] = jnp.where(valid, rows, 0.0).astype(BF)

            loop(sz.patches // (2 * SUB), body)

        n_a = sz.slots if b == 0 else sz.patches // (2 * SUB)
        cuts = [-(-n_a * i // 4) for i in range(5)]
        todo = [norm1]
        todo += [functools.partial(qkv, 3 * w * i // 2, 3 * w * (i + 1) // 2) for i in range(2)]
        todo += [functools.partial(attend, cuts[i], cuts[i + 1]) for i in range(4)]
        todo += [project, norm2]
        todo += [functools.partial(expand, sz.hidden * i // 4, sz.hidden * (i + 1) // 4) for i in range(4)]
        todo += [functools.partial(contract, w * i // 2, w * (i + 1) // 2) for i in range(2)]
        if b == 1:
            todo += [write]
        return todo

    h1_view = h1.reshape(sz.patches // SUB, sz.group, w)
    work = iter([stage_gain] + stages(0) + stages(1))
    for op in plan:
        if op < 0:
            next(work)()
        else:
            comm(GATHER_ORDER[op // 8], op % 8)
    assert next(work, None) is None
    for gather in gathers.values():
        gather.finish()
    for copy in saved:
        copy.wait()


FORWARD_STAGES = 32


def backward_kernel(sz, plan, types, *refs):
    refs = list(refs)

    def grab(n):
        taken, refs[:n] = refs[:n], []
        return taken

    video, cotangent, frames, gains = grab(4)
    (h1_hbm,) = grab(1)
    acts_hbm = dict(zip(keys_of_acts(), grab(16)))
    full_hbm = dict(zip(keys_of_weights(), grab(8)))
    (grad_video,) = grab(1)
    outs = dict(zip(NAMES, grab(4)))
    gain_outs = grab(2)
    acts = dict(zip(ACTS, grab(8)))
    probs1, h1 = grab(2)
    full = dict(zip(keys_of_weights(), grab(8)))
    grads = dict(zip([(name, 1) for name in NAMES] + [GAIN], grab(5)))
    landing = {piece: grab(4) for piece in SCATTER_ORDER}
    gain_out, grad, grad_mid, grad_norm, low, grad_att, sums = grab(7)
    send, recv, local_w, local_a = grab(4)
    assert not refs
    for name in NAMES:
        grads[(name, 0)] = full[(name, 1)]

    place = Place(sz.depth)
    t, w = sz.tokens, sz.width
    count = (frames[0] + 1) // 2
    fetched = {}

    def fetch(key, src, dst, sem):
        copy = pltpu.make_async_copy(src, dst, sem)
        copy.start()
        fetched[key] = copy

    def ready(*keys):
        for key in keys:
            if key in fetched:
                fetched.pop(key).wait()

    def act(name, b):
        return probs1 if (name, b) == ("probs", 1) else acts[name]

    def fetch_act(name, b):
        i = ACTS.index(name)
        fetch(("act", name, b), acts_hbm[(name, b)], act(name, b), local_a.at[b, i])

    def fetch_full(name, b):
        i = NAMES.index(name)
        fetch(("full", name, b), full_hbm[(name, b)], full[(name, b)], local_w.at[b, i])

    fetch_act("active", 1)
    fetch_full("down", 1)
    fetch_act("slope", 1)
    fetch_act("mlp", 1)
    fetch_full("in", 1)
    fetch_act("middle", 1)
    fetch_act("att", 1)
    fetch_full("out", 1)
    fetch_act("qkv", 1)
    fetch_act("probs", 1)
    fetch_act("probs", 0)
    fetch_act("normed", 1)
    fetch_full("qkv", 1)
    fetch(("h1",), h1_hbm, h1, local_w.at[0, 4])
    for name in ("down", "in", "out", "qkv"):
        fetch_full(name, 0)

    place.greet()
    scatters = {}
    for k, piece in enumerate(SCATTER_ORDER):
        name, b, _ = piece
        view = grads[(name, b)]
        out = gain_out if name == "gain" else outs[name].at[b]
        if SPLIT[name] > 1:
            out = out.at[:, columns_of(piece, view.shape[-1])]
            view = view.at[:, :, :, :, columns_of(piece, view.shape[-1])]
        scatters[piece] = Scatter(place, view, *landing[piece], out, send.at[k], recv.at[k], types[k])

    def start():
        valid = lax.broadcasted_iota(jnp.int32, (sz.slots, 1, 1), 0) < count

        def body(i):
            rows = cotangent[:, ds(i * 2 * SUB, 2 * SUB), :].astype(F32)
            rows = jnp.where(valid, rows, 0.0)
            both = [rows[:, half * SUB : (half + 1) * SUB, :].reshape(sz.group, w) for half in range(2)]
            rows = jnp.concatenate(both, 0)
            at = ds(i * 2 * sz.group, 2 * sz.group)
            grad[at, :] = rows
            low[at, :] = rows.astype(BF)

        loop(sz.patches // (2 * SUB), body)

    def put_gain(which):
        row = jnp.sum(sums[...], axis=0, keepdims=True)
        per = w // LANES
        tile = jnp.concatenate([row[:, r * LANES : (r + 1) * LANES] for r in range(per)], 0)
        gain_rows[which * per : (which + 1) * per, :] = tile

    gain_rows = gain_out

    def stages(b):
        a = {name: act(name, b) for name in ACTS}
        key = lambda *names: [("act", name, b) for name in names]

        def again(*names):
            if b == 1:
                for name in names:
                    fetch_act(name, 0)

        half = sz.hidden // 2
        z_half = sz.depth // 2

        def down_grad(i):
            ready(*key("active"))
            at = slice(i * w // 2, (i + 1) * w // 2)
            g = dot(a["active"][...], low[:, at], 0, 0).astype(BF)
            grads[("down", b)][:, :, :, :, at] = g.reshape(sz.full("down")[:-1] + (w // 2,))
            if i == 1:
                again("active")

        def hidden_back(i):
            ready(("full", "down", b), *key("slope"))
            at = slice(i * half, (i + 1) * half)
            weight = full[("down", b)][i * z_half : (i + 1) * z_half].reshape(half, w)
            a["slope"][:, at] = (dot(low[...], weight, 1, 1) * a["slope"][:, at].astype(F32)).astype(BF)

        def in_grad(i):
            ready(*key("mlp"))
            at = slice(i * half, (i + 1) * half)
            g = dot(a["mlp"][...], a["slope"][:, at], 0, 0).astype(BF)
            grads[("in", b)][:, :, :, :, at] = g.reshape(sz.full("in")[:-1] + (half,))
            if i == 1:
                again("mlp")

        def back_rows(src, weight, put):
            put(dot(src[...], wide_rows(weight, w), 1, 1))

        def mlp_back():
            ready(("full", "in", b))

            def put(x):
                grad_norm[...] = x

            back_rows(a["slope"], full[("in", b)], put)
            again("slope")

        def norm2_back():
            ready(*key("middle"))
            norm_back(a["middle"], grad_norm, gain_row(gains, 2 * b + 1), grad, grad_mid, low, sums, row_tile(t))
            put_gain(2 * b + 1)
            again("middle")

        def out_grad():
            ready(*key("att"))

            g = dot(a["att"][...], low[...], 0, 0).astype(BF)
            grads[("out", b)][...] = g.reshape(sz.full("out"))
            again("att")

        def att_back():
            ready(("full", "out", b))

            def put(x):
                grad_att[...] = x.astype(BF)

            back_rows(low, full[("out", b)], put)

        def attend(first, last):
            ready(*key("qkv", "probs"))
            if b == 0:
                spatial_backward(a["qkv"], a["probs"], grad_att, sz.patches, w, first, last)
            else:
                temporal_backward(a["qkv"], a["probs"], grad_att, sz.slots, w, first, last)

        def qkv_grad(first, last):
            ready(*key("normed"))
            at = slice(first, last)
            g = dot(a["normed"][...], a["qkv"][:, at], 0, 0).astype(BF)
            grads[("qkv", b)][:, :, :, :, at] = g.reshape(sz.full("qkv")[:-1] + (last - first,))
            if last == 3 * w:
                again("normed")

        def qkv_back():
            ready(("full", "qkv", b))

            def put(x):
                grad_norm[...] = x

            back_rows(a["qkv"], full[("qkv", b)], put)
            again("qkv")

        def norm1_back():
            if b == 1:
                ready(("h1",))
            src = h1 if b == 1 else video
            if b == 1:
                norm_back(src, grad_norm, gain_row(gains, 2), grad_mid, grad, low, sums, row_tile(t))
            else:
                norm_back(src, grad_norm, gain_row(gains, 0), grad_mid, None, low, sums, row_tile(t))
                grad_video[...] = low[...].reshape(grad_video.shape)
            put_gain(2 * b)

        def reorder():
            view = grad.reshape(sz.patches // SUB, sz.group, w)

            def body(s):
                rows = view[:, ds(s * SUB, SUB), :].reshape(sz.patches, w)
                at = ds(s * sz.patches, sz.patches)
                grad_norm[at, :] = rows
                low[at, :] = rows.astype(BF)

            loop(sz.slots, body)
            loop(sz.slots, lambda s: move(ds(s * sz.patches, sz.patches)))

        def move(at):
            grad[at, :] = grad_norm[at, :]

        n_a = sz.slots if b == 0 else sz.patches // (2 * SUB)
        cuts = [-(-n_a * i // 4) for i in range(5)]
        todo = []
        if b == 1:
            todo += [start]
        for piece in (down_grad, hidden_back, in_grad):
            todo += [functools.partial(piece, i) for i in range(2)]
        todo += [mlp_back, norm2_back, out_grad, att_back]
        todo += [functools.partial(attend, cuts[i], cuts[i + 1]) for i in range(4)]
        todo += [functools.partial(qkv_grad, 3 * w * i // 2, 3 * w * (i + 1) // 2) for i in range(2)]
        todo += [qkv_back, norm1_back]
        if b == 1:
            todo += [reorder]
        return todo

    def spread_gain():
        tile = gain_out[...]
        grads[GAIN][...] = jnp.broadcast_to(tile, sz.full("gain"))

    work = iter(stages(1) + stages(0) + [spread_gain])
    for op in plan:
        if op < 0:
            next(work)()
        else:
            scatters[SCATTER_ORDER[op // 8]].step(op % 8)
    assert next(work, None) is None
    pick_gains(gain_out[...], gain_outs, place.w * sz.narrow + place.n)
    for scatter in scatters.values():
        scatter.finish()


BACKWARD_STAGES = 39


def place_gains(attn_gain, mlp_gain, index):
    own = attn_gain.shape[1]
    per = LANES // own
    row = lax.broadcasted_iota(jnp.int32, (TILE_GAIN[0] // 4, LANES), 0)
    lane = lax.broadcasted_iota(jnp.int32, (TILE_GAIN[0] // 4, LANES), 1) // own
    here = row * per + lane == index
    tiles = []
    for b in range(2):
        for ref in (attn_gain, mlp_gain):
            values = jnp.concatenate([ref[b : b + 1, :]] * per, 1)
            tiles.append(jnp.where(here, values, 0.0))
    return jnp.concatenate(tiles, 0).astype(BF)


def pick_gains(tile, outs, index):
    own = outs[0].shape[1]
    per = LANES // own
    rows = TILE_GAIN[0] // 4
    row = lax.broadcasted_iota(jnp.int32, (rows, own), 0)
    for b in range(2):
        for kind, out in enumerate(outs):
            first = (2 * b + kind) * rows
            total = jnp.zeros((rows, own), F32)
            for j in range(per):
                piece = tile[first : first + rows, j * own : (j + 1) * own]
                total = total + jnp.where(row * per + j == index, piece, 0.0)
            out[b : b + 1, :] = jnp.sum(total, axis=0, keepdims=True)


FORWARD_PLAN = (
    0, 24, 8, 16, 32, 56, 64, 40, 72, 80, 48, 96, 1, 25, 49, 88, 104, 2, 9, 26, 17, 33, 81, 10, 27, 18, 57,
    97, 3, 4, -1, 105, 41, -1, 65, 11, 12, -1, 112, 19, 20, -1, 73, -1, 42, 34, -1, 58, -1, -1, 28, -1, -1,
    50, 43, 74, 66, 35, 36, -1, 89, -1, 59, 44, -1, -1, 51, 52, -1, 82, 75, 60, -1, 67, 90, -1, 68, -1, 98,
    76, -1, 83, -1, -1, 113, 106, 91, -1, -1, 84, -1, 114, -1, 99, 92, -1, 107, -1, 100, -1, -1, 115, 108,
    -1, 116, -1, -1,
)
FORWARD_EARLY = (
    0, 0, 0, 0, 0, 0, 1, 0, 0, 0, 1, 0, 1, 1, 1,
)
BACKWARD_PLAN = (
    -1, -1, 0, -1, 8, -1, 1, -1, -1, 16, -1, 24, -1, 17, -1, 2, -1, 32, 9, -1, -1, 25, 18, 33, -1, -1, 10,
    -1, -1, 40, -1, 48, 26, -1, 41, -1, -1, 49, 34, -1, 56, 11, -1, 64, -1, 57, 35, -1, 50, 42, 65, -1, 72,
    -1, 80, 58, 73, -1, 81, 66, -1, -1, 88, -1, 43, 74, -1, -1, 82, -1, -1, -1, 96, 89, 83, -1, 104, 97, 12,
    75, 105, -1, -1, -1, 112, 90, 98, 113, 106, 27, 19, 91, 114, 3, 59, 107, 51, 67, 99, 28, 115, 84, 4, 36,
    52, 20, 44, 60, 68, 76, 92, 100, 108, 116,
)
BACKWARD_LATE = (
    1, 0, 1, 1, 0, 0, 1, 1, 1, 0, 0, 0, 1, 0, 0,
)


def copy_kernel(count, *refs):
    for i in range(count):
        refs[count + i][...] = refs[i][...]


def by_kernels(mesh, sz):
    vmem = pl.BlockSpec(memory_space=pltpu.VMEM)
    smem = pl.BlockSpec(memory_space=pltpu.SMEM)
    anyw = pl.BlockSpec(memory_space=pl.ANY)
    shape = jax.ShapeDtypeStruct
    t, w = sz.tokens, sz.width
    act_shapes = [shape(*sz.acts(b)[name]) for b in range(2) for name in ACTS]
    full_shapes = [shape(sz.full(name), BF) for name, _ in keys_of_weights()]
    h1_shape = shape((t, w), F32)
    clip_shape = shape((sz.slots, sz.patches, w), BF)
    params = dict(has_side_effects=True, vmem_limit_bytes=VMEM_LIMIT)
    items = len(GATHER_ORDER)

    def landing(k, piece):
        full = sz.full(piece[0])
        full = full[:-1] + (full[-1] // SPLIT[piece[0]],)
        kind = F32 if piece[0] == "gain" else BF
        return [pltpu.VMEM(s, kind) for s in Scatter.landing(full, BACKWARD_LATE[k])]

    def run(video, frames, cotangent, qkv_weight, out_weight, in_weight, down_weight, attn_gain, mlp_gain):
        rows = video.reshape(t, w)
        out, gains, h1, *rest = pl.pallas_call(
            functools.partial(forward_kernel, sz, FORWARD_PLAN, FORWARD_EARLY),
            out_shape=[clip_shape, shape((4, w), F32), h1_shape] + act_shapes + full_shapes,
            in_specs=[vmem, smem] + [vmem] * 6,
            out_specs=[vmem, vmem] + [anyw] * 25,
            scratch_shapes=[pltpu.VMEM(s.shape, s.dtype) for s in act_shapes]
            + [pltpu.VMEM(sz.full(name), BF) for name, _ in [GAIN] + keys_of_weights()]
            + [
                pltpu.VMEM((t, w), F32),
                pltpu.VMEM((t, w), F32),
                pltpu.VMEM((sz.group, LANES), F32),
                pltpu.SemaphoreType.DMA((items, Gather.semaphores(sz.depth))),
                pltpu.SemaphoreType.DMA((items, Gather.semaphores(sz.depth))),
                pltpu.SemaphoreType.DMA((25,)),
            ],
            compiler_params=pltpu.CompilerParams(collective_id=0, **params),
        )(rows, frames, attn_gain, mlp_gain, qkv_weight, out_weight, in_weight, down_weight)
        acts0 = sz.acts(0)
        gain_shape = shape(attn_gain.shape, F32)
        res = pl.pallas_call(
            functools.partial(backward_kernel, sz, BACKWARD_PLAN, BACKWARD_LATE),
            out_shape=[clip_shape]
            + [shape((2,) + sz.shards[name], F32) for name in NAMES]
            + [gain_shape, gain_shape],
            in_specs=[vmem, vmem, smem, vmem] + [anyw] * 25,
            out_specs=[vmem] * 7,
            scratch_shapes=[pltpu.VMEM(*acts0[name]) for name in ACTS]
            + [pltpu.VMEM(*sz.acts(1)["probs"]), pltpu.VMEM((t, w), F32)]
            + [pltpu.VMEM(sz.full(name), BF) for name, _ in keys_of_weights()]
            + [pltpu.VMEM(sz.full(name), BF) for name in NAMES]
            + [pltpu.VMEM(sz.full("gain"), F32)]
            + [buffer for k, piece in enumerate(SCATTER_ORDER) for buffer in landing(k, piece)]
            + [
                pltpu.VMEM(TILE_GAIN, F32),
                pltpu.VMEM((t, w), F32),
                pltpu.VMEM((t, w), F32),
                pltpu.VMEM((t, w), F32),
                pltpu.VMEM((t, w), BF),
                pltpu.VMEM((t, w), BF),
                pltpu.VMEM((SUB, w), F32),
                pltpu.SemaphoreType.DMA((items, Scatter.semaphores(sz.depth))),
                pltpu.SemaphoreType.DMA((items, Scatter.semaphores(sz.depth))),
                pltpu.SemaphoreType.DMA((2, 5)),
                pltpu.SemaphoreType.DMA((2, 8)),
            ],
            compiler_params=pltpu.CompilerParams(collective_id=1, **params),
        )(rows, cotangent.reshape(clip_shape.shape), frames, gains, h1, *rest)
        res = [out] + list(res)
        res = pl.pallas_call(
            functools.partial(copy_kernel, len(res)),
            out_shape=[shape(x.shape, x.dtype) for x in res],
            in_specs=[vmem] * len(res),
            out_specs=[vmem] * len(res),
        )(*res)
        return (res[0].reshape(video.shape), res[1].reshape(video.shape), *res[2:])

    return run


def norm_rows(inputs, scaling):
    centre = jnp.mean(inputs, axis=-1, keepdims=True)
    centred = inputs - centre
    spread = jnp.mean(centred * centred, axis=-1, keepdims=True)
    return centred * lax.rsqrt(spread + EPS) * scaling


def project(rows_in, matrix):
    return jnp.einsum("cspd,de->cspe", rows_in, matrix, preferred_element_type=jnp.float32)


def project_back(rows_in, matrix):
    return jnp.einsum("cspe,de->cspd", rows_in, matrix, preferred_element_type=jnp.float32)


def weight_grad(left, right):
    return jnp.einsum("cspd,cspe->de", left, right, preferred_element_type=jnp.float32)


def pair_scores(first, second, which_block):
    if which_block == 0:
        return jnp.einsum("csphe,csqhe->cshpq", first, second, preferred_element_type=jnp.float32)
    return jnp.einsum("csphe,ctphe->cphst", first, second, preferred_element_type=jnp.float32)


def pair_mix(weighting, second, which_block):
    if which_block == 0:
        return jnp.einsum(
            "cshpq,csqhe->csphe", weighting, second, preferred_element_type=jnp.float32
        )
    return jnp.einsum("cphst,ctphe->csphe", weighting, second, preferred_element_type=jnp.float32)


def pair_back(weighting, first, which_block):
    if which_block == 0:
        return jnp.einsum(
            "cshpq,csphe->csqhe", weighting, first, preferred_element_type=jnp.float32
        )
    return jnp.einsum("cphst,csphe->ctphe", weighting, first, preferred_element_type=jnp.float32)


def masked_scores(queries, key_rows, which_block, allowed):
    head_size = queries.shape[-1]
    scores = pair_scores(queries, key_rows, which_block) * head_size ** (-0.5)
    if which_block == 1:
        scores = jnp.where(allowed[:, None, None], scores, -1000000000.0)
    return scores


def block_forward(inputs, weights, which_block, allowed):
    qkv_matrix, out_matrix, in_matrix, down_matrix, attn_scaling, mlp_scaling = weights
    full_shape = inputs.shape
    head_size = full_shape[-1] // HEADS
    normed, norm_pull = jax.vjp(norm_rows, inputs, attn_scaling.astype(jnp.float32))
    normed_low = normed.astype(jnp.bfloat16)
    qkv_rows = project(normed_low, qkv_matrix).astype(jnp.bfloat16)
    split = qkv_rows.reshape(full_shape[:3] + (3, HEADS, head_size))
    queries = split[:, :, :, 0]
    key_rows = split[:, :, :, 1]
    value_rows = split[:, :, :, 2]
    scores = masked_scores(queries, key_rows, which_block, allowed)
    row_max = jnp.max(scores, axis=-1, keepdims=True)
    shifted = jnp.exp(scores - row_max)
    row_sum = jnp.sum(shifted, axis=-1, keepdims=True)
    log_total = row_max + jnp.log(row_sum)
    probs_low = (shifted / row_sum).astype(jnp.bfloat16)
    attended = pair_mix(probs_low, value_rows, which_block).reshape(full_shape).astype(jnp.bfloat16)
    middle = inputs + project(attended, out_matrix)
    normed_mlp, mlp_pull = jax.vjp(norm_rows, middle, mlp_scaling.astype(jnp.float32))
    normed_mlp_low = normed_mlp.astype(jnp.bfloat16)
    hidden = project(normed_mlp_low, in_matrix)
    active, gelu_pull = jax.vjp(jax.nn.gelu, hidden)
    active_low = active.astype(jnp.bfloat16)
    result = middle + project(active_low, down_matrix)
    stored = (
        norm_pull,
        normed_low,
        queries,
        key_rows,
        value_rows,
        log_total,
        attended,
        mlp_pull,
        normed_mlp_low,
        gelu_pull,
        active_low,
    )
    return (result, stored)


def block_backward(gradient, stored, weights, which_block, allowed):
    qkv_matrix, out_matrix, in_matrix, down_matrix, attn_scaling, mlp_scaling = weights
    (
        norm_pull,
        normed_low,
        queries,
        key_rows,
        value_rows,
        log_total,
        attended,
        mlp_pull,
        normed_mlp_low,
        gelu_pull,
        active_low,
    ) = stored
    full_shape = gradient.shape
    head_size = queries.shape[-1]
    result_low = gradient.astype(jnp.bfloat16)
    grad_down_w = weight_grad(active_low, result_low)
    grad_active = project_back(result_low, down_matrix)
    grad_hidden = gelu_pull(grad_active)[0].astype(jnp.bfloat16)
    grad_in_w = weight_grad(normed_mlp_low, grad_hidden)
    grad_normed_mlp = project_back(grad_hidden, in_matrix)
    middle_part, grad_mlp_scaling = mlp_pull(grad_normed_mlp)
    grad_middle = gradient + middle_part
    middle_low = grad_middle.astype(jnp.bfloat16)
    grad_out_w = weight_grad(attended, middle_low)
    grad_attended = project_back(middle_low, out_matrix).astype(jnp.bfloat16)
    grad_attended = grad_attended.reshape(queries.shape)
    scores = masked_scores(queries, key_rows, which_block, allowed)
    soft_probs = jnp.exp(scores - log_total)
    grad_probs = pair_scores(grad_attended, value_rows, which_block)
    row_delta = jnp.sum(grad_probs * soft_probs, axis=-1, keepdims=True)
    grad_scores = (soft_probs * (grad_probs - row_delta)).astype(jnp.bfloat16)
    score_scale = head_size ** (-0.5)
    grad_queries = pair_mix(grad_scores, key_rows, which_block) * score_scale
    grad_keys = pair_back(grad_scores, queries, which_block) * score_scale
    grad_values = pair_back(soft_probs.astype(jnp.bfloat16), grad_attended, which_block)
    grad_qkv_rows = jnp.stack([grad_queries, grad_keys, grad_values], axis=3).astype(jnp.bfloat16)
    grad_qkv_rows = grad_qkv_rows.reshape(full_shape[:3] + (3 * full_shape[-1],))
    grad_qkv_w = weight_grad(normed_low, grad_qkv_rows)
    grad_normed = project_back(grad_qkv_rows, qkv_matrix)
    input_part, grad_attn_scaling = norm_pull(grad_normed)
    grad_input = grad_middle + input_part
    return (
        grad_input,
        (grad_qkv_w, grad_out_w, grad_in_w, grad_down_w, grad_attn_scaling, grad_mlp_scaling),
    )


def block_shards(qkv_weight, out_weight, in_weight, down_weight, attn_gain, mlp_gain, block_index):
    return (
        qkv_weight[block_index].astype(jnp.bfloat16),
        out_weight[block_index].astype(jnp.bfloat16),
        in_weight[block_index].astype(jnp.bfloat16),
        down_weight[block_index].astype(jnp.bfloat16),
        attn_gain[block_index].astype(jnp.bfloat16),
        mlp_gain[block_index].astype(jnp.bfloat16),
    )


def by_einsums(
    video, frames, cotangent, qkv_weight, out_weight, in_weight, down_weight, attn_gain, mlp_gain
):
    axes = ("wide", "narrow")
    slot_counts = (frames + 1) // 2
    positions = jnp.arange(video.shape[1], dtype=jnp.int32)
    allowed = (positions[None, None, :] <= positions[None, :, None]) & (
        positions[None, None, :] < slot_counts[:, None, None]
    )
    valid_slot = (positions[None, :] < slot_counts[:, None]).astype(jnp.float32)[:, :, None, None]
    weights = (qkv_weight, out_weight, in_weight, down_weight, attn_gain, mlp_gain)
    full = [
        tuple(lax.all_gather(part, axes, axis=0, tiled=True) for part in block_shards(*weights, b))
        for b in range(2)
    ]
    spatial_out, spatial_stored = block_forward(video.astype(jnp.float32), full[0], 0, allowed)
    temporal_out, temporal_stored = block_forward(spatial_out, full[1], 1, allowed)
    output = (temporal_out * valid_slot).astype(jnp.bfloat16)
    gradient = cotangent.astype(jnp.float32) * valid_slot
    grad_between, temporal_grads = block_backward(gradient, temporal_stored, full[1], 1, allowed)
    grad_start, spatial_grads = block_backward(grad_between, spatial_stored, full[0], 0, allowed)
    summed = [
        lax.psum_scatter(jnp.stack(pair), axes, scatter_dimension=1, tiled=True)
        for pair in zip(spatial_grads, temporal_grads)
    ]
    return (output, grad_start.astype(jnp.bfloat16), *summed)


def solution(mesh):
    both = ("wide", "narrow")
    clips = P(both, None, None, None)
    rows = P(None, both, None)
    in_specs = (clips, P(both), clips, rows, rows, rows, rows, P(None, both), P(None, both))
    out_specs = (clips, clips, rows, rows, rows, rows, P(None, both), P(None, both))

    def shards(*args):
        sz = Sizes(mesh, args[0], args[5])
        whole_tiles = all(rows % 16 == 0 for rows, _ in sz.shards.values())
        if whole_tiles and sz.narrow == 4 and args[0].shape[0] == 1:
            return by_kernels(mesh, sz)(*args)
        return by_einsums(*args)

    return jax.shard_map(shards, mesh=mesh, in_specs=in_specs, out_specs=out_specs, check_vma=False)
```

```python
import functools

import jax
import jax.numpy as jnp
from jax import lax
from jax.experimental import pallas as pl
from jax.experimental.pallas import tpu as pltpu
from jax.sharding import PartitionSpec as P

HEADS = 8
EPS = 1e-05
BF = jnp.bfloat16
F32 = jnp.float32
MESH = pl.DeviceIdType.MESH
VMEM_LIMIT = 62 * 2**20


def dot(a, b, ca, cb):
    return lax.dot_general(a, b, (((ca,), (cb,)), ((), ())), preferred_element_type=F32)


def ds(start, size):
    if isinstance(start, int):
        return pl.ds(start, size)
    return pl.ds(pl.multiple_of(start, size), size)


def loop(count, body, first=0):
    if count - first == 1:
        body(first)
        return

    def step(i, carry):
        body(i)
        return carry

    lax.fori_loop(first, count, step, 0)


class Place:
    def __init__(self, depth):
        self.depth = depth
        self.w = lax.axis_index("wide")
        self.n = lax.axis_index("narrow")
        self.z = self.w // 2
        self.c = self.w % 2
        first = 1 + self.c
        self.na = self.flip(self.n, first)
        self.nb = self.flip(self.n, 3 - first)
        self.nab = 3 - self.n

    @staticmethod
    def flip(n, step):
        bit = (n // step) % 2
        return n + step - 2 * step * bit

    def sib(self):
        return (self.z * 2 + 1 - self.c, self.n)

    def a(self):
        return (self.w, self.na)

    def b(self):
        return (self.w, self.nb)

    def along(self, d):
        return (lax.rem(self.z + d, self.depth) * 2 + self.c, self.n)

    def zat(self, d):
        return lax.rem(self.z + d, self.depth)

    def greet(self):
        bar = pltpu.get_barrier_semaphore()
        targets = [self.sib(), self.a(), self.b()] + [self.along(d) for d in range(1, self.depth)]
        for t in targets:
            pl.semaphore_signal(bar, inc=1, device_id=t, device_id_type=MESH)
        pl.semaphore_wait(bar, len(targets))


def remote(src, dst, send, recv, target):
    return pltpu.make_async_remote_copy(src, dst, send, recv, device_id=target, device_id_type=MESH)


class Gather:
    def __init__(self, place, full, send, recv, early_a):
        self.p, self.full, self.send, self.recv, self.early_a = place, full, send, recv, early_a
        self.sent = set()

    @staticmethod
    def semaphores(early_a):
        return 4 + early_a

    Z, A, B, SIB, ZA = range(5)

    def go(self, slot, index, target):
        view = self.full.at[index]
        remote(view, view, self.send.at[slot], self.recv.at[slot], target).start()
        self.sent.add(slot)

    def take(self, slot):
        view = self.bytes_of(slot)
        remote(view, view, self.send.at[slot], self.recv.at[slot], self.p.sib()).wait_recv()

    def bytes_of(self, slot):
        p, full = self.p, self.full
        if slot in (self.Z, self.ZA):
            return full.at[0 : p.depth - 1, p.c, p.n]
        if slot == self.A:
            return full.at[p.z, p.c, p.n] if self.early_a else full.at[:, p.c, p.n]
        if slot == self.B:
            return full.at[:, p.c, 0:2]
        return full.at[:, p.c]

    def column(self, n):
        return (slice(None), self.p.c, n)

    def along(self, slot, n):
        p = self.p
        for d in range(1, p.depth):
            self.go(slot, (p.z, p.c, n), p.along(d))

    def step0(self):
        p = self.p
        if self.early_a:
            self.go(self.A, (p.z, p.c, p.n), p.a())
        self.along(self.Z, p.n)

    def step1(self):
        p = self.p
        if self.early_a:
            self.take(self.A)
            self.along(self.ZA, p.na)
        else:
            self.take(self.Z)
            self.go(self.A, self.column(p.n), p.a())
            self.go(self.B, self.column(p.n), p.b())
            self.go(self.SIB, self.column(p.n), p.sib())

    def step2(self):
        p = self.p
        if self.early_a:
            self.take(self.Z)
            self.go(self.B, self.column(p.n), p.b())
            self.go(self.SIB, self.column(p.n), p.sib())
            self.take(self.ZA)
        else:
            self.take(self.A)
        self.go(self.B, self.column(p.na), p.b())
        self.go(self.SIB, self.column(p.na), p.sib())

    def step3(self):
        p = self.p
        self.take(self.B)
        self.go(self.SIB, self.column(p.nb), p.sib())
        self.go(self.SIB, self.column(p.nab), p.sib())

    def step4(self):
        self.take(self.SIB)

    def finish(self):
        for slot in sorted(self.sent):
            view = self.bytes_of(slot)
            remote(view, view, self.send.at[slot], self.recv.at[slot], self.p.sib()).wait_send()
        self.sent = set()

    def step(self, i):
        (self.step0, self.step1, self.step2, self.step3, self.step4)[i]()


class Scatter:
    def __init__(self, place, full, from_sib, from_b, from_a, from_z, out, send, recv, late_a):
        self.p, self.full, self.out, self.send, self.recv = place, full, out, send, recv
        self.from_sib, self.from_b, self.from_a, self.from_z = from_sib, from_b, from_a, from_z
        self.late_a = late_a
        self.sent = set()

    @staticmethod
    def semaphores(late_a):
        return 4 + late_a, 5 + late_a

    @staticmethod
    def landing(full, late_a):
        z, _, n, r, c = full
        a = (1, r, c) if late_a else (z, r, c)
        return [(z, n, r, c), (2, z, r, c), a, ((2 if late_a else 1) * (z - 1), r, c)]

    SIB, A, B, Z, B1, ZA = 0, 1, 2, 3, 4, 5

    def sending(self, slot):
        return 4 if slot == self.ZA else self.B if slot == self.B1 else slot

    def go(self, slot, src, dst, target):
        out = self.sending(slot)
        remote(src, dst, self.send.at[out], self.recv.at[slot], target).start()
        self.sent.add(out)

    def take(self, slot, view):
        remote(view, view, self.send.at[0], self.recv.at[slot], self.p.sib()).wait_recv()

    def add(self, n, part):
        c = self.p.c
        for z in range(self.p.depth):
            self.full[z, c, n] = self.full[z, c, n] + part(z)

    def along(self, second, n):
        p = self.p
        for d in range(1, p.depth):
            land = self.from_z.at[second * (p.depth - 1) + d - 1]
            self.go(self.ZA if second else self.Z, self.full.at[p.zat(d), p.c, n], land, p.along(d))

    def sum_along(self, second, n):
        p = self.p
        first = second * (p.depth - 1)
        self.take(self.ZA if second else self.Z, self.from_z.at[first : first + p.depth - 1])
        total = self.full[p.z, p.c, n].astype(F32)
        for d in range(1, p.depth):
            total = total + self.from_z[first + d - 1].astype(F32)
        return total

    def step0(self):
        self.go(self.SIB, self.full.at[:, 1 - self.p.c], self.from_sib, self.p.sib())

    def step1(self):
        p = self.p
        self.take(self.SIB, self.from_sib)
        for slot, half, n in ((self.B, 0, p.nab), (self.B1, 1, p.nb)):
            self.add(n, lambda z, n=n: self.from_sib[z, n])
            self.go(slot, self.full.at[:, p.c, n], self.from_b.at[half], p.b())
        for n in (p.na, p.n):
            self.add(n, lambda z, n=n: self.from_sib[z, n])

    def step2(self):
        p = self.p
        self.take(self.B, self.from_b.at[0])
        self.add(p.na, lambda z: self.from_b[0, z])
        if self.late_a:
            self.along(1, p.na)
        else:
            self.go(self.A, self.full.at[:, p.c, p.na], self.from_a, p.a())
        self.take(self.B1, self.from_b.at[1])
        self.add(p.n, lambda z: self.from_b[1, z])
        if self.late_a:
            self.along(0, p.n)

    def step3(self):
        p = self.p
        if self.late_a:
            self.full[p.z, p.c, p.na] = self.sum_along(1, p.na).astype(self.full.dtype)
            self.go(self.A, self.full.at[p.z, p.c, p.na], self.from_a.at[0], p.a())
            self.out[...] = self.sum_along(0, p.n)
        else:
            self.take(self.A, self.from_a)
            self.add(p.n, lambda z: self.from_a[z])
            self.along(0, p.n)

    def step4(self):
        p = self.p
        if self.late_a:
            self.take(self.A, self.from_a.at[0])
            self.out[...] = self.out[...] + self.from_a[0].astype(F32)
        else:
            self.out[...] = self.sum_along(0, p.n)

    def finish(self):
        p, full = self.p, self.full
        views = {
            self.SIB: full.at[:, p.c],
            self.A: full.at[p.z, p.c, p.n] if self.late_a else full.at[:, p.c, p.n],
            self.B: full.at[:, p.c, 0:2],
            self.Z: full.at[0 : p.depth - 1, p.c, p.n],
            4: full.at[0 : p.depth - 1, p.c, p.n],
        }
        for slot in sorted(self.sent):
            view = views[slot]
            remote(view, view, self.send.at[slot], self.recv.at[0], p.sib()).wait_send()
        self.sent = set()

    def step(self, i):
        (self.step0, self.step1, self.step2, self.step3, self.step4)[i]()


def stats(x):
    centre = jnp.mean(x, axis=-1, keepdims=True)
    centred = x - centre
    spread = jnp.mean(centred * centred, axis=-1, keepdims=True)
    r = lax.rsqrt(spread + EPS)
    return centred * r, r


def norm_into(src, gain, dst, rows):
    total = src.shape[0]

    def body(i):
        at = ds(i * rows, rows)
        xn, _ = stats(src[at, :].astype(F32))
        dst[at, :] = (xn * gain).astype(BF)

    loop(total // rows, body)


def halves(shape):
    return lax.broadcasted_iota(jnp.int32, shape, 1) < shape[1] // 2


def split_heads(x):
    low = halves(x.shape)
    zero = jnp.zeros_like(x)
    return jnp.concatenate([jnp.where(low, x, zero), jnp.where(low, zero, x)], 0)


def head_ones(keys):
    shape = (2 * keys, LANES)
    row = lax.broadcasted_iota(jnp.int32, shape, 0) < keys
    low = lax.broadcasted_iota(jnp.int32, shape, 1) < LANES // 2
    return jnp.where(row == low, 1.0, 0.0).astype(BF)


def unroll(first, last, body):
    for i in range(first, last):
        body(i)


def spatial_forward(qkv, probs, att, patches, width, first, last):
    head = width // HEADS
    scale = head ** -0.5
    pairs = range(HEADS // 2)
    ones = head_ones(patches)

    def body(s):
        at = ds(s * patches, patches)
        parts = []
        for pair in pairs:
            lane = pair * 2 * head
            q = qkv[at, lane : lane + 2 * head]
            parts.append(dot(q, split_heads(qkv[at, width + lane : width + lane + 2 * head]), 1, 1))
        scores = jnp.concatenate(parts, 0) * scale
        low = halves(scores.shape)
        top0 = jnp.max(jnp.where(low, scores, -jnp.inf), axis=-1, keepdims=True)
        top1 = jnp.max(jnp.where(low, -jnp.inf, scores), axis=-1, keepdims=True)
        e = jnp.exp(scores - jnp.where(low, top0, top1))
        e_low = e.astype(BF)
        parts = []
        for pair in pairs:
            lane = pair * 2 * head
            v2 = split_heads(qkv[at, 2 * width + lane : 2 * width + lane + 2 * head])
            rows = slice(pair * patches, (pair + 1) * patches)
            parts.append(dot(e_low[rows], jnp.concatenate([v2, ones], 1), 1, 0))
        both = jnp.concatenate(parts, 0)
        r = 1.0 / both[:, 2 * head :]
        probs[s] = (e * r).astype(BF).reshape(HEADS // 2, patches, 2 * patches)
        new = (both[:, : 2 * head] * r).astype(BF)
        for pair in pairs:
            att[at, pair * 2 * head : (pair + 1) * 2 * head] = new[pair * patches : (pair + 1) * patches]

    unroll(first, last, body)


def pad_heads(x, lanes):
    low = halves(x.shape)
    zero = jnp.zeros_like(x)
    fill = jnp.zeros((lanes - x.shape[0], x.shape[1]), x.dtype)
    return jnp.concatenate([jnp.where(low, x, zero), fill, jnp.where(low, zero, x), fill], 0).astype(BF)


LANES = 128
SUB = 8


def temporal_forward(qkv, probs, att, bias, slots, width, first, last):
    head = width // HEADS
    scale = head ** -0.5
    group = slots * SUB
    pairs = range(HEADS // 2)
    parts_of = [slice(half * group, (half + 1) * group) for half in range(2)]

    def body(i):
        at = ds(i * 2 * group, 2 * group)
        parts = []
        for pair in pairs:
            lane = pair * 2 * head
            q = qkv[at, lane : lane + 2 * head].astype(F32)
            k = qkv[at, width + lane : width + lane + 2 * head].astype(F32)
            for rows in parts_of:
                x = dot(q[rows].astype(BF), pad_heads(k[rows], LANES), 1, 1)
                parts += [x[:, :LANES], x[:, LANES:]]
        scores = jnp.stack(parts, 0) * scale + bias[...][None]
        e = jnp.exp(scores - jnp.max(scores, axis=-1, keepdims=True))
        p = (e / jnp.sum(e, axis=-1, keepdims=True)).astype(BF)
        for pair in pairs:
            lane = pair * 2 * head
            v = qkv[at, 2 * width + lane : 2 * width + lane + 2 * head].astype(F32)
            out = []
            for half, rows in enumerate(parts_of):
                j = (pair * 2 + half) * 2
                both = jnp.concatenate([p[j], p[j + 1]], 1)
                probs[i * 2 + half, pair] = both
                out.append(dot(both, pad_heads(v[rows], LANES), 1, 0))
            att[at, lane : lane + 2 * head] = jnp.concatenate(out, 0).astype(BF)

    unroll(first, last, body)


def make_bias(bias, count, slots):
    group = slots * SUB
    q = lax.broadcasted_iota(jnp.int32, (group, LANES), 0)
    k = lax.broadcasted_iota(jnp.int32, (group, LANES), 1)
    sq, sk = q // SUB, k // SUB
    ok = (q - sq * SUB == k - sk * SUB) & (sk <= sq) & (sk < count)
    bias[...] = jnp.where(ok, 0.0, -1e9)


def gelu_pair(z):
    k0 = 0.7978845608028654
    k1 = k0 * 0.044715
    z2 = z * z
    half = 0.5 + 0.5 * jnp.tanh(z * (k0 + k1 * z2))
    active = z * half
    slope = half + half * (z - active) * (2.0 * k0 + 6.0 * k1 * z2)
    return active, slope


def wide_rows(ref, width, columns=None):
    x = ref[...] if columns is None else ref[:, :, :, :, columns]
    return x.reshape(width, x.shape[-1])


def unsplit_heads(x, second, rows):
    low = halves((rows, x.shape[1]))
    return jnp.where(low, x[:rows], x[second : second + rows])


def spatial_backward(qkv, probs, grad, patches, width, first, last):
    head = width // HEADS
    scale = head ** -0.5
    pairs = range(HEADS // 2)
    rows_of = [slice(pair * patches, (pair + 1) * patches) for pair in pairs]

    def body(s):
        at = ds(s * patches, patches)
        cols = [[slice(t * width + p * 2 * head, t * width + (p + 1) * 2 * head) for t in range(3)] for p in pairs]
        p_low = probs[s].reshape(HEADS // 2 * patches, 2 * patches)
        soft = p_low.astype(F32)
        q = [qkv[at, cols[p][0]] for p in pairs]
        k2 = [split_heads(qkv[at, cols[p][1]]) for p in pairs]
        g = [grad[at, p * 2 * head : (p + 1) * 2 * head] for p in pairs]
        gp = [dot(g[p], split_heads(qkv[at, cols[p][2]]), 1, 1) for p in pairs]
        gv = [dot(p_low[rows_of[p]], g[p], 0, 0) for p in pairs]
        gp = jnp.concatenate(gp, 0)
        low = halves(gp.shape)
        both = gp * soft
        sum0 = jnp.sum(jnp.where(low, both, 0.0), axis=-1, keepdims=True)
        sum1 = jnp.sum(jnp.where(low, 0.0, both), axis=-1, keepdims=True)
        gs = (soft * (gp - jnp.where(low, sum0, sum1))).astype(BF)
        gq = [dot(gs[rows_of[p]], k2[p], 1, 0) for p in pairs]
        gk = [dot(gs[rows_of[p]], q[p], 0, 0) for p in pairs]
        for p in pairs:
            qkv[at, cols[p][0]] = (gq[p] * scale).astype(BF)
            qkv[at, cols[p][1]] = (unsplit_heads(gk[p], patches, patches) * scale).astype(BF)
            qkv[at, cols[p][2]] = unsplit_heads(gv[p], patches, patches).astype(BF)

    unroll(first, last, body)


def temporal_backward(qkv, probs, grad, slots, width, first, last):
    head = width // HEADS
    scale = head ** -0.5
    group = slots * SUB
    pairs = range(HEADS // 2)
    parts_of = [slice(half * group, (half + 1) * group) for half in range(2)]

    def body(i):
        at = ds(i * 2 * group, 2 * group)
        cols = [[slice(t * width + p * 2 * head, t * width + (p + 1) * 2 * head) for t in range(3)] for p in pairs]
        qs, ks, gs_in, ps, gp, soft = [], [], [], [], [], []
        for pair in pairs:
            q, k, v = (qkv[at, c].astype(F32) for c in cols[pair])
            g = grad[at, pair * 2 * head : (pair + 1) * 2 * head].astype(F32)
            for half, rows in enumerate(parts_of):
                qs.append(q[rows].astype(BF))
                ks.append(pad_heads(k[rows], LANES))
                gs_in.append(g[rows].astype(BF))
                p = probs[i * 2 + half, pair]
                ps.append(p)
                x = dot(gs_in[-1], pad_heads(v[rows], LANES), 1, 1)
                wide = p.astype(F32)
                gp += [x[:, :LANES], x[:, LANES:]]
                soft += [wide[:, :LANES], wide[:, LANES:]]
        many = range(len(ps))
        gv = [unsplit_heads(dot(ps[j], gs_in[j], 0, 0), LANES, group) for j in many]
        gp = jnp.stack(gp, 0)
        soft = jnp.stack(soft, 0)
        delta = jnp.sum(gp * soft, axis=-1, keepdims=True)
        gs = (soft * (gp - delta)).astype(BF)
        gs = [jnp.concatenate([gs[2 * j], gs[2 * j + 1]], 1) for j in many]
        gq = [dot(gs[j], ks[j], 1, 0) * scale for j in many]
        gk = [unsplit_heads(dot(gs[j], qs[j], 0, 0), LANES, group) * scale for j in many]
        for pair in pairs:
            for c, outs in zip(cols[pair], (gq, gk, gv)):
                qkv[at, c] = jnp.concatenate(outs[2 * pair : 2 * pair + 2], 0).astype(BF)

    unroll(first, last, body)


def norm_back(src, grad, gain, base, dst, low, sums, rows):
    total, width = grad.shape
    sums[...] = jnp.zeros_like(sums)

    def body(i):
        at = ds(i * rows, rows)
        xn, r = stats(src[at, :].astype(F32))
        g = grad[at, :]
        e = g * gain
        inner = e - jnp.mean(e, axis=-1, keepdims=True) - xn * jnp.mean(e * xn, axis=-1, keepdims=True)
        res = base[at, :] + r * inner
        if dst is not None:
            dst[at, :] = res
        low[at, :] = res.astype(BF)
        sums[...] += jnp.sum((g * xn).reshape(rows // SUB, SUB, width), axis=0)

    loop(total // rows, body)


def gain_row(gains, which):
    return gains[which : which + 1, :]


class Sizes:
    def __init__(self, mesh, video, in_weight):
        self.depth = mesh.shape["wide"] // 2
        self.narrow = mesh.shape["narrow"]
        self.slots, self.patches, self.width = video.shape[1:]
        self.hidden = in_weight.shape[2]
        self.tokens = self.slots * self.patches
        self.group = self.slots * SUB
        devices = 2 * self.depth * self.narrow
        w = self.width // devices
        self.shards = {
            "qkv": (w, 3 * self.width),
            "out": (w, self.width),
            "in": (w, self.hidden),
            "down": (self.hidden // devices, self.width),
        }
        self.mesh_dims = (self.depth, 2, self.narrow)

    def full(self, name):
        return self.mesh_dims + (TILE_GAIN if name == "gain" else self.shards[name])

    def acts(self, b):
        t, w, f = self.tokens, self.width, self.hidden
        pairs = HEADS // 2
        if b == 0:
            probs = (self.slots, pairs, self.patches, 2 * self.patches)
        else:
            probs = (self.patches // SUB, pairs, self.group, 2 * LANES)
        return {
            "normed": ((t, w), BF),
            "qkv": ((t, 3 * w), BF),
            "probs": (probs, BF),
            "att": ((t, w), BF),
            "middle": ((t, w), F32),
            "mlp": ((t, w), BF),
            "active": ((t, f), BF),
            "slope": ((t, f), BF),
        }


TILE_GAIN = (16, LANES)
NAMES = ("qkv", "out", "in", "down")
ACTS = ("normed", "qkv", "probs", "att", "middle", "mlp", "active", "slope")
SPLIT = {"gain": 1, "qkv": 2, "out": 1, "in": 2, "down": 2}


def pieces_of(name, b):
    return [(name, b, i) for i in range(SPLIT[name])]


GAIN = ("gain", 0)
GATHER_ORDER = [(*GAIN, 0)] + [piece for b in range(2) for name in NAMES for piece in pieces_of(name, b)]
SCATTER_ORDER = [
    piece for b in (1, 0) for name in ("down", "in", "out", "qkv") for piece in pieces_of(name, b)
] + [(*GAIN, 0)]


def columns_of(piece, columns):
    name, _, i = piece
    part = columns // SPLIT[name]
    return slice(i * part, (i + 1) * part)


def row_tile(tokens):
    return tokens // 2 if tokens % 32 == 0 else tokens


def keys_of_weights():
    return [(name, b) for b in range(2) for name in NAMES]


KEPT = ("normed", "qkv", "att", "middle", "mlp", "active", "slope")


def layer_kernel(sz, *refs):
    refs = list(refs)

    def grab(n):
        taken, refs[:n] = refs[:n], []
        return taken

    video, cotangent, frames, attn_gain, mlp_gain = grab(5)
    shard = dict(zip(NAMES, grab(4)))
    out, grad_video = grab(2)
    outs = dict(zip(NAMES, grab(4)))
    gain_outs = grab(2)
    acts_hbm = dict(zip(KEPT, grab(len(KEPT))))
    acts = dict(zip(ACTS, grab(8)))
    probs1, h1 = grab(2)
    full = dict(zip([GAIN] + keys_of_weights(), grab(9)))
    grads = dict(zip([(name, 1) for name in NAMES] + [GAIN], grab(5)))
    landing = {piece: grab(4) for piece in SCATTER_ORDER}
    gains, bias, gain_out, grad, grad_mid, grad_norm, low, grad_att, sums = grab(9)
    gather_send, gather_recv, scatter_send, scatter_recv, local = grab(5)
    assert not refs
    result = grad_mid
    for name in NAMES:
        grads[(name, 0)] = full[(name, 1)]

    place = Place(sz.depth)
    place.greet()

    def part_of(ref, piece, columns):
        if SPLIT[piece[0]] == 1:
            return ref
        return ref.at[(slice(None),) * (len(ref.shape) - 1) + (columns_of(piece, columns),)]

    gathers = {}
    at = 0
    for k, piece in enumerate(GATHER_ORDER):
        n = Gather.semaphores(FORWARD_EARLY[k])
        ref = full[piece[:2]]
        sems = [sem.at[at : at + n] for sem in (gather_send, gather_recv)]
        gathers[piece] = Gather(place, part_of(ref, piece, ref.shape[-1]), *sems, FORWARD_EARLY[k])
        at += n
    scatters = {}
    at_send = at_recv = 0
    for k, piece in enumerate(SCATTER_ORDER):
        n_send, n_recv = Scatter.semaphores(BACKWARD_LATE[k])
        ref = grads[piece[:2]]
        columns = ref.shape[-1]
        target = gain_out if piece[:2] == GAIN else outs[piece[0]].at[piece[1]]
        sems = [scatter_send.at[at_send : at_send + n_send], scatter_recv.at[at_recv : at_recv + n_recv]]
        scatters[piece] = Scatter(
            place,
            part_of(ref, piece, columns),
            *landing[piece],
            part_of(target, piece, columns),
            *sems,
            BACKWARD_LATE[k],
        )
        at_send += n_send
        at_recv += n_recv
    filled = set()

    def gather_step(piece, step):
        key = piece[:2]
        if step == 0 and key not in filled:
            filled.add(key)
            own = (place.z, place.c, place.n)
            if key == GAIN:
                full[key][own] = place_gains(attn_gain, mlp_gain, place.w * sz.narrow + place.n)
            else:
                full[key][own] = shard[key[0]][key[1]].astype(BF)
        gathers[piece].step(step)

    moving = {}

    def move(name, src, dst):
        copy = pltpu.make_async_copy(src, dst, local.at[KEPT.index(name)])
        copy.start()
        moving[name] = copy

    def settle(*names):
        for name in names:
            if name in moving:
                moving.pop(name).wait()

    def act(name, b):
        return probs1 if (name, b) == ("probs", 1) else acts[name]

    def keep(b, *names):
        for name in names:
            if b == 0 and name in KEPT:
                move(name, acts[name], acts_hbm[name])

    def fetch(b, *names):
        for name in names:
            if b == 1 and name in KEPT:
                settle(name)
                move(name, acts_hbm[name], acts[name])

    count = (frames[0] + 1) // 2
    t, w = sz.tokens, sz.width

    def stage_gain():
        make_bias(bias, count, sz.slots)
        tile = jnp.sum(full[GAIN][...].astype(F32).reshape(-1, 16, LANES), axis=0)
        for g in range(4):
            rows = [tile[g * 4 + r : g * 4 + r + 1, :] for r in range(w // LANES)]
            gains[g : g + 1, :] = jnp.concatenate(rows, 1)

    def forward_stages(b):
        a = {name: act(name, b) for name in ACTS}
        h = video if b == 0 else h1

        def norm1():
            settle("normed")
            norm_into(h, gain_row(gains, 2 * b), a["normed"], row_tile(t))
            keep(b, "normed")

        def qkv(first, last):
            settle("qkv")
            at = slice(first, last)
            a["qkv"][:, at] = dot(a["normed"][...], wide_rows(full[("qkv", b)], w, at), 1, 0).astype(BF)
            if last == 3 * w:
                keep(b, "qkv")

        def attend(first, last):
            settle("att")
            if b == 0:
                spatial_forward(a["qkv"], a["probs"], a["att"], sz.patches, w, first, last)
                end = sz.slots
            else:
                temporal_forward(a["qkv"], a["probs"], a["att"], bias, sz.slots, w, first, last)
                end = sz.patches // (2 * SUB)
            if last == end:
                keep(b, "probs", "att")

        def project():
            settle("middle")
            new = dot(a["att"][...], wide_rows(full[("out", b)], w), 1, 0)
            a["middle"][...] = h[...].astype(F32) + new
            keep(b, "middle")

        def norm2():
            settle("mlp")
            norm_into(a["middle"], gain_row(gains, 2 * b + 1), a["mlp"], row_tile(t))
            keep(b, "mlp")

        def expand(first, last):
            at = slice(first, last)
            settle("active", "slope")
            weight = wide_rows(full[("in", b)], w, at)
            rows = row_tile(t)
            for r in range(0, t, rows):
                active, slope = gelu_pair(dot(a["mlp"][r : r + rows, :], weight, 1, 0))
                a["active"][r : r + rows, at] = active.astype(BF)
                a["slope"][r : r + rows, at] = slope.astype(BF)
            if last == sz.hidden:
                keep(b, "active", "slope")

        def contract(first, last):
            at = slice(first, last)
            new = a["middle"][:, at] + dot(a["active"][...], wide_rows(full[("down", b)], sz.hidden, at), 1, 0)
            if b == 0:
                new = new.reshape(sz.slots, sz.patches // SUB, SUB, last - first)
                for s in range(sz.slots):
                    h1_view[:, s * SUB : (s + 1) * SUB, at] = new[s]
            else:
                result[:, at] = new

        def write():
            valid = lax.broadcasted_iota(jnp.int32, (sz.slots, 1, 1), 0) < count

            def body(i):
                rows = result[ds(i * 2 * sz.group, 2 * sz.group), :]
                rows = rows.reshape(2, sz.slots, SUB, w)
                rows = jnp.concatenate([rows[0], rows[1]], axis=1)
                out[:, ds(i * 2 * SUB, 2 * SUB), :] = jnp.where(valid, rows, 0.0).astype(BF)

            loop(sz.patches // (2 * SUB), body)

        n_a = sz.slots if b == 0 else sz.patches // (2 * SUB)
        cuts = [-(-n_a * i // 4) for i in range(5)]
        todo = [norm1]
        todo += [functools.partial(qkv, 3 * w * i // 2, 3 * w * (i + 1) // 2) for i in range(2)]
        todo += [functools.partial(attend, cuts[i], cuts[i + 1]) for i in range(4)]
        todo += [project, norm2]
        todo += [functools.partial(expand, sz.hidden * i // 4, sz.hidden * (i + 1) // 4) for i in range(4)]
        todo += [functools.partial(contract, w * i // 2, w * (i + 1) // 2) for i in range(2)]
        if b == 1:
            todo += [write]
        return todo

    h1_view = h1.reshape(sz.patches // SUB, sz.group, w)

    def start():
        valid = lax.broadcasted_iota(jnp.int32, (sz.slots, 1, 1), 0) < count

        def body(i):
            rows = cotangent[:, ds(i * 2 * SUB, 2 * SUB), :].astype(F32)
            rows = jnp.where(valid, rows, 0.0)
            both = [rows[:, half * SUB : (half + 1) * SUB, :].reshape(sz.group, w) for half in range(2)]
            rows = jnp.concatenate(both, 0)
            at = ds(i * 2 * sz.group, 2 * sz.group)
            grad[at, :] = rows
            low[at, :] = rows.astype(BF)

        loop(sz.patches // (2 * SUB), body)

    def put_gain(which):
        row = jnp.sum(sums[...], axis=0, keepdims=True)
        per = w // LANES
        tile = jnp.concatenate([row[:, r * LANES : (r + 1) * LANES] for r in range(per)], 0)
        gain_rows[which * per : (which + 1) * per, :] = tile

    gain_rows = gain_out

    def backward_stages(b):
        a = {name: act(name, b) for name in ACTS}

        half = sz.hidden // 2
        z_half = sz.depth // 2

        def down_grad(i):
            settle("active")
            if b == 0 and i == 0:
                for gather in gathers.values():
                    gather.finish()
            at = slice(i * w // 2, (i + 1) * w // 2)
            g = dot(a["active"][...], low[:, at], 0, 0).astype(BF)
            grads[("down", b)][:, :, :, :, at] = g.reshape(sz.full("down")[:-1] + (w // 2,))
            if i == 1:
                fetch(b, "active")

        def hidden_back(i):
            settle("slope")
            at = slice(i * half, (i + 1) * half)
            weight = full[("down", b)][i * z_half : (i + 1) * z_half].reshape(half, w)
            a["slope"][:, at] = (dot(low[...], weight, 1, 1) * a["slope"][:, at].astype(F32)).astype(BF)

        def in_grad(i):
            settle("mlp")
            at = slice(i * half, (i + 1) * half)
            g = dot(a["mlp"][...], a["slope"][:, at], 0, 0).astype(BF)
            grads[("in", b)][:, :, :, :, at] = g.reshape(sz.full("in")[:-1] + (half,))
            if i == 1:
                fetch(b, "mlp")

        def back_rows(src, weight, put):
            put(dot(src[...], wide_rows(weight, w), 1, 1))

        def mlp_back():

            def put(x):
                grad_norm[...] = x

            back_rows(a["slope"], full[("in", b)], put)
            fetch(b, "slope")

        def norm2_back():
            settle("middle")
            norm_back(a["middle"], grad_norm, gain_row(gains, 2 * b + 1), grad, grad_mid, low, sums, row_tile(t))
            put_gain(2 * b + 1)
            fetch(b, "middle")

        def out_grad():
            settle("att")

            g = dot(a["att"][...], low[...], 0, 0).astype(BF)
            grads[("out", b)][...] = g.reshape(sz.full("out"))
            fetch(b, "att")

        def att_back():

            def put(x):
                grad_att[...] = x.astype(BF)

            back_rows(low, full[("out", b)], put)

        def attend(first, last):
            settle("qkv", "probs")
            if b == 0:
                spatial_backward(a["qkv"], a["probs"], grad_att, sz.patches, w, first, last)
            else:
                temporal_backward(a["qkv"], a["probs"], grad_att, sz.slots, w, first, last)

        def qkv_grad(first, last):
            settle("normed")
            at = slice(first, last)
            g = dot(a["normed"][...], a["qkv"][:, at], 0, 0).astype(BF)
            grads[("qkv", b)][:, :, :, :, at] = g.reshape(sz.full("qkv")[:-1] + (last - first,))
            if last == 3 * w:
                fetch(b, "normed")

        def qkv_back():

            def put(x):
                grad_norm[...] = x

            back_rows(a["qkv"], full[("qkv", b)], put)
            fetch(b, "qkv")

        def norm1_back():
            src = h1 if b == 1 else video
            if b == 1:
                norm_back(src, grad_norm, gain_row(gains, 2), grad_mid, grad, low, sums, row_tile(t))
            else:
                norm_back(src, grad_norm, gain_row(gains, 0), grad_mid, None, low, sums, row_tile(t))
                grad_video[...] = low[...].reshape(grad_video.shape)
            put_gain(2 * b)

        def reorder():
            view = grad.reshape(sz.patches // SUB, sz.group, w)

            def body(s):
                rows = view[:, ds(s * SUB, SUB), :].reshape(sz.patches, w)
                at = ds(s * sz.patches, sz.patches)
                grad_norm[at, :] = rows
                low[at, :] = rows.astype(BF)

            loop(sz.slots, body)
            grad[...] = grad_norm[...]

        n_a = sz.slots if b == 0 else sz.patches // (2 * SUB)
        cuts = [-(-n_a * i // 4) for i in range(5)]
        todo = []
        if b == 1:
            todo += [start]
        for piece in (down_grad, hidden_back, in_grad):
            todo += [functools.partial(piece, i) for i in range(2)]
        todo += [mlp_back, norm2_back, out_grad, att_back]
        todo += [functools.partial(attend, cuts[i], cuts[i + 1]) for i in range(4)]
        todo += [functools.partial(qkv_grad, 3 * w * i // 2, 3 * w * (i + 1) // 2) for i in range(2)]
        todo += [qkv_back, norm1_back]
        if b == 1:
            todo += [reorder]
        return todo

    def spread_gain():
        tile = gain_out[...]
        grads[GAIN][...] = jnp.broadcast_to(tile, sz.full("gain"))

    work = iter([stage_gain] + forward_stages(0) + forward_stages(1))
    for op in FORWARD_PLAN:
        if op < 0:
            next(work)()
        else:
            gather_step(GATHER_ORDER[op // 8], op % 8)
    assert next(work, None) is None
    work = iter(backward_stages(1) + backward_stages(0) + [spread_gain])
    for op in BACKWARD_PLAN:
        if op < 0:
            next(work)()
        else:
            scatters[SCATTER_ORDER[op // 8]].step(op % 8)
    assert next(work, None) is None
    pick_gains(gain_out[...], gain_outs, place.w * sz.narrow + place.n)
    settle(*KEPT)
    for scatter in scatters.values():
        scatter.finish()


BACKWARD_STAGES = 39


def place_gains(attn_gain, mlp_gain, index):
    own = attn_gain.shape[1]
    per = LANES // own
    row = lax.broadcasted_iota(jnp.int32, (TILE_GAIN[0] // 4, LANES), 0)
    lane = lax.broadcasted_iota(jnp.int32, (TILE_GAIN[0] // 4, LANES), 1) // own
    here = row * per + lane == index
    tiles = []
    for b in range(2):
        for ref in (attn_gain, mlp_gain):
            values = jnp.concatenate([ref[b : b + 1, :]] * per, 1)
            tiles.append(jnp.where(here, values, 0.0))
    return jnp.concatenate(tiles, 0).astype(BF)


def pick_gains(tile, outs, index):
    own = outs[0].shape[1]
    per = LANES // own
    rows = TILE_GAIN[0] // 4
    row = lax.broadcasted_iota(jnp.int32, (rows, own), 0)
    for b in range(2):
        for kind, out in enumerate(outs):
            first = (2 * b + kind) * rows
            total = jnp.zeros((rows, own), F32)
            for j in range(per):
                piece = tile[first : first + rows, j * own : (j + 1) * own]
                total = total + jnp.where(row * per + j == index, piece, 0.0)
            out[b : b + 1, :] = jnp.sum(total, axis=0, keepdims=True)


FORWARD_PLAN = (
    0, 24, 1, 80, 16, 25, 2, 81, 8, 32, 17, 3, 26, 82, 9, 48, 56, 33, 4, -1, 40, 18, -1, 72, 49, 41, 10, 34,
    57, 50, 27, 64, 88, 11, 12, -1, 73, 19, 20, -1, 96, 42, 58, 35, -1, 36, 89, 65, -1, -1, -1, 83, 66, 97,
    74, 51, 28, -1, -1, 104, 43, -1, -1, 44, -1, 90, 59, 105, -1, 52, -1, 112, 67, 60, -1, 75, -1, 98, 68,
    -1, 76, -1, -1, -1, 91, 106, 84, 113, -1, -1, -1, 99, 114, -1, 92, -1, -1, 100, -1, 107, -1, 115, 108,
    -1, 116, -1, -1,
)
FORWARD_EARLY = (
    0, 0, 0, 0, 0, 1, 0, 0, 0, 0, 0, 1, 1, 1, 1,
)
BACKWARD_PLAN = (
    -1, -1, 0, -1, 8, -1, 1, -1, 9, -1, 16, -1, 24, -1, 2, 25, -1, 17, -1, 32, -1, -1, -1, 10, 33, -1, -1,
    26, -1, 40, -1, 48, -1, 41, 49, 18, -1, -1, -1, 56, 34, -1, 64, 57, -1, 65, 27, -1, -1, 72, 35, -1, 80,
    42, 50, -1, -1, 81, -1, 88, 73, -1, 43, -1, -1, 58, -1, 82, 28, 89, -1, -1, 96, 66, 97, -1, 104, 74, 59,
    -1, 11, 105, 67, -1, 98, -1, 112, 75, 113, 90, 3, 99, 106, 12, 19, 36, 51, 68, 114, 83, 91, 107, 115, 4,
    20, 44, 52, 60, 76, 84, 92, 100, 108, 116,
)
BACKWARD_LATE = (
    1, 1, 1, 0, 0, 0, 1, 0, 0, 0, 1, 0, 0, 0, 0,
)


def copy_kernel(count, *refs):
    sems = refs[-1]
    refs = refs[:-1]
    down = [pltpu.make_async_copy(refs[i], refs[2 * count + i], sems.at[i]) for i in range(count)]
    up = [pltpu.make_async_copy(refs[2 * count + i], refs[count + i], sems.at[i]) for i in range(count)]
    for copy in down:
        copy.start()
    for i in range(count):
        down[i].wait()
        up[i].start()
    for copy in up:
        copy.wait()


def by_kernels(mesh, sz):
    vmem = pl.BlockSpec(memory_space=pltpu.VMEM)
    smem = pl.BlockSpec(memory_space=pltpu.SMEM)
    anyw = pl.BlockSpec(memory_space=pl.ANY)
    shape = jax.ShapeDtypeStruct
    t, w = sz.tokens, sz.width
    acts0 = sz.acts(0)
    clip_shape = shape((sz.slots, sz.patches, w), BF)
    dma = pltpu.SemaphoreType.DMA

    def landing(k, piece):
        full = sz.full(piece[0])
        full = full[:-1] + (full[-1] // SPLIT[piece[0]],)
        kind = F32 if piece[0] == "gain" else BF
        return [pltpu.VMEM(s, kind) for s in Scatter.landing(full, BACKWARD_LATE[k])]

    def run(video, frames, cotangent, qkv_weight, out_weight, in_weight, down_weight, attn_gain, mlp_gain):
        gain_shape = shape(attn_gain.shape, F32)
        shapes = [clip_shape, clip_shape]
        shapes += [shape((2,) + sz.shards[name], F32) for name in NAMES]
        shapes += [gain_shape, gain_shape]
        n_gather = sum(Gather.semaphores(early) for early in FORWARD_EARLY)
        n_scatter = [sum(Scatter.semaphores(late)[i] for late in BACKWARD_LATE) for i in range(2)]
        res = pl.pallas_call(
            functools.partial(layer_kernel, sz),
            out_shape=shapes + [shape(*acts0[name]) for name in KEPT],
            in_specs=[vmem, vmem, smem] + [vmem] * 6,
            out_specs=[vmem] * len(shapes) + [anyw] * len(KEPT),
            scratch_shapes=[pltpu.VMEM(*acts0[name]) for name in ACTS]
            + [pltpu.VMEM(*sz.acts(1)["probs"]), pltpu.VMEM((t, w), F32)]
            + [pltpu.VMEM(sz.full(name), BF) for name, _ in [GAIN] + keys_of_weights()]
            + [pltpu.VMEM(sz.full(name), BF) for name in NAMES]
            + [pltpu.VMEM(sz.full("gain"), F32)]
            + [buffer for k, piece in enumerate(SCATTER_ORDER) for buffer in landing(k, piece)]
            + [
                pltpu.VMEM((4, w), F32),
                pltpu.VMEM((sz.group, LANES), F32),
                pltpu.VMEM(TILE_GAIN, F32),
                pltpu.VMEM((t, w), F32),
                pltpu.VMEM((t, w), F32),
                pltpu.VMEM((t, w), F32),
                pltpu.VMEM((t, w), BF),
                pltpu.VMEM((t, w), BF),
                pltpu.VMEM((SUB, w), F32),
                dma((n_gather,)),
                dma((n_gather,)),
                dma((n_scatter[0],)),
                dma((n_scatter[1],)),
                dma((len(KEPT),)),
            ],
            compiler_params=pltpu.CompilerParams(
                collective_id=0, has_side_effects=True, vmem_limit_bytes=VMEM_LIMIT
            ),
        )(
            video.reshape(t, w),
            cotangent.reshape(clip_shape.shape),
            frames,
            attn_gain,
            mlp_gain,
            qkv_weight,
            out_weight,
            in_weight,
            down_weight,
        )
        res = list(res)[: len(shapes)]
        res = pl.pallas_call(
            functools.partial(copy_kernel, len(res)),
            out_shape=shapes,
            in_specs=[anyw] * len(res),
            out_specs=[anyw] * len(res),
            scratch_shapes=[pltpu.VMEM(x.shape, x.dtype) for x in shapes] + [dma((len(res),))],
        )(*res)
        return (res[0].reshape(video.shape), res[1].reshape(video.shape), *res[2:])

    return run


def norm_rows(inputs, scaling):
    centre = jnp.mean(inputs, axis=-1, keepdims=True)
    centred = inputs - centre
    spread = jnp.mean(centred * centred, axis=-1, keepdims=True)
    return centred * lax.rsqrt(spread + EPS) * scaling


def project(rows_in, matrix):
    return jnp.einsum("cspd,de->cspe", rows_in, matrix, preferred_element_type=jnp.float32)


def project_back(rows_in, matrix):
    return jnp.einsum("cspe,de->cspd", rows_in, matrix, preferred_element_type=jnp.float32)


def weight_grad(left, right):
    return jnp.einsum("cspd,cspe->de", left, right, preferred_element_type=jnp.float32)


def pair_scores(first, second, which_block):
    if which_block == 0:
        return jnp.einsum("csphe,csqhe->cshpq", first, second, preferred_element_type=jnp.float32)
    return jnp.einsum("csphe,ctphe->cphst", first, second, preferred_element_type=jnp.float32)


def pair_mix(weighting, second, which_block):
    if which_block == 0:
        return jnp.einsum(
            "cshpq,csqhe->csphe", weighting, second, preferred_element_type=jnp.float32
        )
    return jnp.einsum("cphst,ctphe->csphe", weighting, second, preferred_element_type=jnp.float32)


def pair_back(weighting, first, which_block):
    if which_block == 0:
        return jnp.einsum(
            "cshpq,csphe->csqhe", weighting, first, preferred_element_type=jnp.float32
        )
    return jnp.einsum("cphst,csphe->ctphe", weighting, first, preferred_element_type=jnp.float32)


def masked_scores(queries, key_rows, which_block, allowed):
    head_size = queries.shape[-1]
    scores = pair_scores(queries, key_rows, which_block) * head_size ** (-0.5)
    if which_block == 1:
        scores = jnp.where(allowed[:, None, None], scores, -1000000000.0)
    return scores


def block_forward(inputs, weights, which_block, allowed):
    qkv_matrix, out_matrix, in_matrix, down_matrix, attn_scaling, mlp_scaling = weights
    full_shape = inputs.shape
    head_size = full_shape[-1] // HEADS
    normed, norm_pull = jax.vjp(norm_rows, inputs, attn_scaling.astype(jnp.float32))
    normed_low = normed.astype(jnp.bfloat16)
    qkv_rows = project(normed_low, qkv_matrix).astype(jnp.bfloat16)
    split = qkv_rows.reshape(full_shape[:3] + (3, HEADS, head_size))
    queries = split[:, :, :, 0]
    key_rows = split[:, :, :, 1]
    value_rows = split[:, :, :, 2]
    scores = masked_scores(queries, key_rows, which_block, allowed)
    row_max = jnp.max(scores, axis=-1, keepdims=True)
    shifted = jnp.exp(scores - row_max)
    row_sum = jnp.sum(shifted, axis=-1, keepdims=True)
    log_total = row_max + jnp.log(row_sum)
    probs_low = (shifted / row_sum).astype(jnp.bfloat16)
    attended = pair_mix(probs_low, value_rows, which_block).reshape(full_shape).astype(jnp.bfloat16)
    middle = inputs + project(attended, out_matrix)
    normed_mlp, mlp_pull = jax.vjp(norm_rows, middle, mlp_scaling.astype(jnp.float32))
    normed_mlp_low = normed_mlp.astype(jnp.bfloat16)
    hidden = project(normed_mlp_low, in_matrix)
    active, gelu_pull = jax.vjp(jax.nn.gelu, hidden)
    active_low = active.astype(jnp.bfloat16)
    result = middle + project(active_low, down_matrix)
    stored = (
        norm_pull,
        normed_low,
        queries,
        key_rows,
        value_rows,
        log_total,
        attended,
        mlp_pull,
        normed_mlp_low,
        gelu_pull,
        active_low,
    )
    return (result, stored)


def block_backward(gradient, stored, weights, which_block, allowed):
    qkv_matrix, out_matrix, in_matrix, down_matrix, attn_scaling, mlp_scaling = weights
    (
        norm_pull,
        normed_low,
        queries,
        key_rows,
        value_rows,
        log_total,
        attended,
        mlp_pull,
        normed_mlp_low,
        gelu_pull,
        active_low,
    ) = stored
    full_shape = gradient.shape
    head_size = queries.shape[-1]
    result_low = gradient.astype(jnp.bfloat16)
    grad_down_w = weight_grad(active_low, result_low)
    grad_active = project_back(result_low, down_matrix)
    grad_hidden = gelu_pull(grad_active)[0].astype(jnp.bfloat16)
    grad_in_w = weight_grad(normed_mlp_low, grad_hidden)
    grad_normed_mlp = project_back(grad_hidden, in_matrix)
    middle_part, grad_mlp_scaling = mlp_pull(grad_normed_mlp)
    grad_middle = gradient + middle_part
    middle_low = grad_middle.astype(jnp.bfloat16)
    grad_out_w = weight_grad(attended, middle_low)
    grad_attended = project_back(middle_low, out_matrix).astype(jnp.bfloat16)
    grad_attended = grad_attended.reshape(queries.shape)
    scores = masked_scores(queries, key_rows, which_block, allowed)
    soft_probs = jnp.exp(scores - log_total)
    grad_probs = pair_scores(grad_attended, value_rows, which_block)
    row_delta = jnp.sum(grad_probs * soft_probs, axis=-1, keepdims=True)
    grad_scores = (soft_probs * (grad_probs - row_delta)).astype(jnp.bfloat16)
    score_scale = head_size ** (-0.5)
    grad_queries = pair_mix(grad_scores, key_rows, which_block) * score_scale
    grad_keys = pair_back(grad_scores, queries, which_block) * score_scale
    grad_values = pair_back(soft_probs.astype(jnp.bfloat16), grad_attended, which_block)
    grad_qkv_rows = jnp.stack([grad_queries, grad_keys, grad_values], axis=3).astype(jnp.bfloat16)
    grad_qkv_rows = grad_qkv_rows.reshape(full_shape[:3] + (3 * full_shape[-1],))
    grad_qkv_w = weight_grad(normed_low, grad_qkv_rows)
    grad_normed = project_back(grad_qkv_rows, qkv_matrix)
    input_part, grad_attn_scaling = norm_pull(grad_normed)
    grad_input = grad_middle + input_part
    return (
        grad_input,
        (grad_qkv_w, grad_out_w, grad_in_w, grad_down_w, grad_attn_scaling, grad_mlp_scaling),
    )


def block_shards(qkv_weight, out_weight, in_weight, down_weight, attn_gain, mlp_gain, block_index):
    return (
        qkv_weight[block_index].astype(jnp.bfloat16),
        out_weight[block_index].astype(jnp.bfloat16),
        in_weight[block_index].astype(jnp.bfloat16),
        down_weight[block_index].astype(jnp.bfloat16),
        attn_gain[block_index].astype(jnp.bfloat16),
        mlp_gain[block_index].astype(jnp.bfloat16),
    )


def by_einsums(
    video, frames, cotangent, qkv_weight, out_weight, in_weight, down_weight, attn_gain, mlp_gain
):
    axes = ("wide", "narrow")
    slot_counts = (frames + 1) // 2
    positions = jnp.arange(video.shape[1], dtype=jnp.int32)
    allowed = (positions[None, None, :] <= positions[None, :, None]) & (
        positions[None, None, :] < slot_counts[:, None, None]
    )
    valid_slot = (positions[None, :] < slot_counts[:, None]).astype(jnp.float32)[:, :, None, None]
    weights = (qkv_weight, out_weight, in_weight, down_weight, attn_gain, mlp_gain)
    full = [
        tuple(lax.all_gather(part, axes, axis=0, tiled=True) for part in block_shards(*weights, b))
        for b in range(2)
    ]
    spatial_out, spatial_stored = block_forward(video.astype(jnp.float32), full[0], 0, allowed)
    temporal_out, temporal_stored = block_forward(spatial_out, full[1], 1, allowed)
    output = (temporal_out * valid_slot).astype(jnp.bfloat16)
    gradient = cotangent.astype(jnp.float32) * valid_slot
    grad_between, temporal_grads = block_backward(gradient, temporal_stored, full[1], 1, allowed)
    grad_start, spatial_grads = block_backward(grad_between, spatial_stored, full[0], 0, allowed)
    summed = [
        lax.psum_scatter(jnp.stack(pair), axes, scatter_dimension=1, tiled=True)
        for pair in zip(spatial_grads, temporal_grads)
    ]
    return (output, grad_start.astype(jnp.bfloat16), *summed)


def solution(mesh):
    both = ("wide", "narrow")
    clips = P(both, None, None, None)
    rows = P(None, both, None)
    in_specs = (clips, P(both), clips, rows, rows, rows, rows, P(None, both), P(None, both))
    out_specs = (clips, clips, rows, rows, rows, rows, P(None, both), P(None, both))

    def shards(*args):
        sz = Sizes(mesh, args[0], args[5])
        whole_tiles = all(rows % 16 == 0 for rows, _ in sz.shards.values())
        if whole_tiles and sz.narrow == 4 and args[0].shape[0] == 1:
            return by_kernels(mesh, sz)(*args)
        return by_einsums(*args)

    return jax.shard_map(shards, mesh=mesh, in_specs=in_specs, out_specs=out_specs, check_vma=False)
```

```python
import functools

import jax
import jax.numpy as jnp
from jax import lax
from jax.experimental import pallas as pl
from jax.experimental.pallas import tpu as pltpu
from jax.sharding import PartitionSpec as P

HEADS = 8
EPS = 1e-05
BF = jnp.bfloat16
F32 = jnp.float32
MESH = pl.DeviceIdType.MESH
VMEM_LIMIT = 62 * 2**20


def dot(a, b, ca, cb):
    return lax.dot_general(a, b, (((ca,), (cb,)), ((), ())), preferred_element_type=F32)


def ds(start, size):
    if isinstance(start, int):
        return pl.ds(start, size)
    return pl.ds(pl.multiple_of(start, size), size)


def loop(count, body, first=0):
    if count - first == 1:
        body(first)
        return

    def step(i, carry):
        body(i)
        return carry

    lax.fori_loop(first, count, step, 0)


class Place:
    def __init__(self):
        self.w = lax.axis_index("wide")
        self.n = lax.axis_index("narrow")
        self.z = self.w // 2
        self.c = self.w % 2
        first = 1 + self.c
        self.na = self.flip(self.n, first)
        self.nb = self.flip(self.n, 3 - first)
        self.nab = 3 - self.n
        self.z1 = self.flip(self.z, 1)
        self.z2 = self.flip(self.z, 2)
        self.z3 = 3 - self.z
        self.others = (self.z1, self.z2, self.z3)
        self.end = (self.z == 0) | (self.z == 3)
        self.middle = (self.z == 1) | (self.z == 2)

    @staticmethod
    def flip(n, step):
        bit = (n // step) % 2
        return n + step - 2 * step * bit

    def sib(self):
        return (self.z * 2 + 1 - self.c, self.n)

    def a(self):
        return (self.w, self.na)

    def b(self):
        return (self.w, self.nb)

    def chip(self, z):
        return (z * 2 + self.c, self.n)

    def greet(self):
        targets = [self.sib(), self.a(), self.b()] + [self.chip(z) for z in self.others]
        for t in targets:
            pl.semaphore_signal(pltpu.get_barrier_semaphore(), inc=1, device_id=t, device_id_type=MESH)
        return len(targets)

    def met(self, count):
        pl.semaphore_wait(pltpu.get_barrier_semaphore(), count)


def remote(src, dst, send, recv, target):
    return pltpu.make_async_remote_copy(src, dst, send, recv, device_id=target, device_id_type=MESH)


class Gather:
    def __init__(self, place, full, send, recv, way):
        self.p, self.full, self.send, self.recv, self.way = place, full, send, recv, way
        self.sent = set()

    A, B, SIB, Z, ZA = range(5)
    @staticmethod
    def semaphores(way):
        return (5, 7) if way == 1 else (4, 5)

    @staticmethod
    def near_far(which):
        return (3, 4) if which == 0 else (5, 6)

    def go(self, out, into, index, target):
        view = self.full.at[index]
        remote(view, view, self.send.at[out], self.recv.at[into], target).start()
        self.sent.add(out)

    def take(self, slot, view):
        remote(view, view, self.send.at[0], self.recv.at[slot], self.p.sib()).wait_recv()

    def shards(self, count):
        p = self.p
        return self.full.at[p.z, p.c, p.n] if count == 1 else self.full.at[0:count, p.c, p.n]

    def pass_on(self, slot, index):
        p = self.p
        self.go(slot, slot, index, {self.A: p.a, self.B: p.b, self.SIB: p.sib}[slot]())

    def others(self, n, slots):
        p = self.p
        for z in p.others:
            for slot in slots:
                self.pass_on(slot, (z, p.c, n))

    def column(self, n, slots):
        for slot in slots:
            self.pass_on(slot, (slice(None), self.p.c, n))

    def along(self, which, n):
        p = self.p
        near, far = self.near_far(which)
        own = (p.z, p.c, n)
        self.go(self.Z + which, far, own, p.chip(p.z2))
        self.go(self.Z + which, near, own, p.chip(p.z1))

        @pl.when(p.middle)
        def _():
            self.go(self.Z + which, near, own, p.chip(p.z3))

    def relay(self, which, n):
        p = self.p
        near, far = self.near_far(which)
        self.take(far, self.shards(1))

        @pl.when(p.middle)
        def _():
            self.go(self.Z + which, near, (p.z2, p.c, n), p.chip(p.z1))

    def take_near(self, which):
        self.take(self.near_far(which)[0], self.shards(2))

    def steps(self):
        p = self.p
        A, B, SIB = self.A, self.B, self.SIB

        def start():
            own = (p.z, p.c, p.n)
            self.pass_on(A, own)
            self.pass_on(B, own)
            self.along(0, p.n)
            self.pass_on(SIB, own)

        def own_relay():
            self.relay(0, p.n)

        def own_column():
            self.take_near(0)
            self.others(p.n, (A, B, SIB))

        def column_of_a():
            self.take(A, self.shards(self.full.shape[0]))
            self.column(p.na, (B, SIB))

        def shard_of_a():
            self.take(A, self.shards(1))
            self.along(1, p.na)
            self.pass_on(B, (p.z, p.c, p.na))
            self.pass_on(SIB, (p.z, p.c, p.na))

        def own_column_late():
            self.take_near(0)
            self.others(p.n, (B, SIB))
            self.relay(1, p.na)

        def column_of_a_late():
            self.take_near(1)
            self.others(p.na, (B, SIB))

        def from_b():
            self.take(B, self.full.at[:, p.c, 0:2])
            self.column(p.nb, (SIB,))
            self.column(p.nab, (SIB,))

        def from_sib():
            self.take(SIB, self.full.at[:, p.c])

        def start_row():
            self.pass_on(A, (p.z, p.c, p.n))
            self.pass_on(B, (p.z, p.c, p.n))

        def shard_of_a_on():
            self.take(A, self.shards(1))
            self.pass_on(B, (p.z, p.c, p.na))

        near, far = self.near_far(0)
        row = (p.z, p.c)

        def row_along():
            self.take(B, self.shards(2))
            self.go(self.Z, far, row, p.chip(p.z2))
            self.go(self.Z, near, row, p.chip(p.z1))

            @pl.when(p.middle)
            def _():
                self.go(self.Z, near, row, p.chip(p.z3))

        def row_relay():
            self.take(far, self.full.at[p.z, p.c])

            @pl.when(p.middle)
            def _():
                self.go(self.Z, near, (p.z2, p.c), p.chip(p.z1))

        def rows_over():
            self.take(near, self.full.at[0:2, p.c])
            self.pass_on(SIB, (slice(None), p.c))

        if self.way == 2:
            return [start_row, shard_of_a_on, row_along, row_relay, rows_over, from_sib]
        if self.way == 1:
            return [start, shard_of_a, own_relay, own_column_late, column_of_a_late, from_b, from_sib]
        return [start, own_relay, own_column, column_of_a, from_b, from_sib]

    def finish(self):
        p, full = self.p, self.full
        if not self.sent:
            return

        def sent(slot, view):
            remote(view, view, self.send.at[slot], self.recv.at[0], p.sib()).wait_send()

        sent(self.A, self.shards(full.shape[0] if self.way == 0 else 1))
        sent(self.B, self.shards(2) if self.way == 2 else full.at[:, p.c, 0:2])
        sent(self.SIB, full.at[:, p.c])
        for which in range(2 if self.way == 1 else 1):

            @pl.when(p.middle)
            def _(which=which):
                sent(self.Z + which, full.at[:, p.c] if self.way == 2 else self.shards(4))

            @pl.when(p.end)
            def _(which=which):
                sent(self.Z + which, full.at[0:2, p.c] if self.way == 2 else self.shards(2))

        self.sent = set()

    def step(self, i):
        self.steps()[i]()


class Scatter:
    def __init__(self, place, full, from_sib, from_b, from_a, from_z, out, send, recv, way):
        self.p, self.full, self.out, self.send, self.recv = place, full, out, send, recv
        self.from_sib, self.from_b, self.from_a, self.from_z = from_sib, from_b, from_a, from_z
        self.way = way
        self.sent = set()

    @staticmethod
    def semaphores(way):
        return (5, 8) if way == 1 else (4, 6)

    @staticmethod
    def landing(full, way):
        z, _, n, r, c = full
        if way == 2:
            return [(z, n, r, c), (2, 1, r, c), (1, r, c), (4, n, r, c)]
        if way == 1:
            return [(z, n, r, c), (2, z, r, c), (1, r, c), (8, r, c)]
        return [(z, n, r, c), (2, z, r, c), (z, r, c), (4, r, c)]

    SIB, A, B, Z, ZA = range(5)
    B1 = 3

    @staticmethod
    def sum_relay(which):
        return (4, 5) if which == 0 else (6, 7)

    def go(self, out, into, src, dst, target):
        remote(src, dst, self.send.at[out], self.recv.at[into], target).start()
        self.sent.add(out)

    def take(self, slot, view):
        remote(view, view, self.send.at[0], self.recv.at[slot], self.p.sib()).wait_recv()

    def add(self, n, part):
        c = self.p.c
        for z in range(self.full.shape[0]):
            self.full[z, c, n] = self.full[z, c, n] + part(z)


    def along(self, which, n):
        p = self.p
        total, relay = self.sum_relay(which)

        def send(z, target, land, into):
            self.go(self.Z + which, into, self.full.at[z, p.c, n], self.from_z.at[4 * which + land], p.chip(target))

        @pl.when(p.end)
        def _():
            send(p.z3, p.z1, 3, relay)
            send(p.z2, p.z2, 1, total)

        @pl.when(p.middle)
        def _():
            send(p.z3, p.z3, 2, total)

        send(p.z1, p.z1, 0, total)

    def relay(self, which, n):
        p = self.p
        total, relay = self.sum_relay(which)

        @pl.when(p.middle)
        def _():
            land = self.from_z.at[4 * which + 3]
            self.take(relay, land)
            self.full[p.z2, p.c, n] = self.full[p.z2, p.c, n] + self.from_z[4 * which + 3]
            view = self.full.at[p.z2, p.c, n]
            self.go(self.Z + which, total, view, self.from_z.at[4 * which + 1], p.chip(p.z2))

    def sum_along(self, which, n, put):
        p = self.p
        total, _ = self.sum_relay(which)
        first = 4 * which

        def add_up(count):
            self.take(total, self.from_z.at[first : first + count])
            x = self.full[p.z, p.c, n].astype(F32)
            for i in range(count):
                x = x + self.from_z[first + i].astype(F32)
            put(x)

        @pl.when(p.end)
        def _():
            add_up(2)

        @pl.when(p.middle)
        def _():
            add_up(3)

    def steps(self):
        p = self.p

        def start():
            self.go(self.SIB, self.SIB, self.full.at[:, 1 - p.c], self.from_sib, p.sib())

        def other_core():
            self.take(self.SIB, self.from_sib)
            for slot, half, n in ((self.B, 0, p.nab), (self.B1, 1, p.nb)):
                self.add(n, lambda z, n=n: self.from_sib[z, n])
                self.go(self.B, slot, self.full.at[:, p.c, n], self.from_b.at[half], p.b())
            for n in (p.na, p.n):
                self.add(n, lambda z, n=n: self.from_sib[z, n])

        def partner_b():
            self.take(self.B, self.from_b.at[0])
            self.add(p.na, lambda z: self.from_b[0, z])
            if self.way == 1:
                self.along(1, p.na)
            else:
                self.go(self.A, self.A, self.full.at[:, p.c, p.na], self.from_a, p.a())
            self.take(self.B1, self.from_b.at[1])
            self.add(p.n, lambda z: self.from_b[1, z])
            if self.way == 1:
                self.along(0, p.n)

        def partner_a():
            self.take(self.A, self.from_a)
            self.add(p.n, lambda z: self.from_a[z])
            self.along(0, p.n)

        def relay():
            self.relay(0, p.n)

        def store(x):
            self.out[...] = x

        def end():
            self.sum_along(0, p.n, store)

        def relay_both():
            self.relay(1, p.na)
            self.relay(0, p.n)

        def to_a():
            def put(x):
                self.full[p.z, p.c, p.na] = x.astype(self.full.dtype)

            self.sum_along(1, p.na, put)
            self.go(self.A, self.A, self.full.at[p.z, p.c, p.na], self.from_a.at[0], p.a())
            self.sum_along(0, p.n, store)

        def end_a():
            self.take(self.A, self.from_a.at[0])
            self.out[...] = self.out[...] + self.from_a[0].astype(F32)

        total, relayed = self.sum_relay(0)

        def row(z, target, land, into):
            self.go(self.Z, into, self.full.at[z, p.c], self.from_z.at[land], p.chip(target))

        def rows_along():
            self.take(self.SIB, self.from_sib)
            for n in range(self.full.shape[2]):
                self.add(n, lambda z, n=n: self.from_sib[z, n])

            @pl.when(p.end)
            def _():
                row(p.z3, p.z1, 3, relayed)
                row(p.z2, p.z2, 1, total)

            @pl.when(p.middle)
            def _():
                row(p.z3, p.z3, 2, total)

            row(p.z1, p.z1, 0, total)

        def row_relay():
            @pl.when(p.middle)
            def _():
                self.take(relayed, self.from_z.at[3])
                for n in range(self.full.shape[2]):
                    self.full[p.z2, p.c, n] = self.full[p.z2, p.c, n] + self.from_z[3, n]
                row(p.z2, p.z2, 1, total)

        def row_to_b():
            def add_up(count):
                self.take(total, self.from_z.at[0:count])
                for n in range(self.full.shape[2]):
                    x = self.full[p.z, p.c, n].astype(F32)
                    for i in range(count):
                        x = x + self.from_z[i, n].astype(F32)
                    self.full[p.z, p.c, n] = x.astype(self.full.dtype)

            @pl.when(p.end)
            def _():
                add_up(2)

            @pl.when(p.middle)
            def _():
                add_up(3)

            for slot, half, n in ((self.B, 0, p.nab), (self.B1, 1, p.nb)):
                self.go(self.B, slot, self.full.at[p.z, p.c, n], self.from_b.at[half, 0], p.b())

        def shard_to_a():
            self.take(self.B, self.from_b.at[0, 0])
            self.full[p.z, p.c, p.na] = self.full[p.z, p.c, p.na] + self.from_b[0, 0]
            self.go(self.A, self.A, self.full.at[p.z, p.c, p.na], self.from_a.at[0], p.a())
            self.take(self.B1, self.from_b.at[1, 0])
            self.out[...] = self.full[p.z, p.c, p.n].astype(F32) + self.from_b[1, 0].astype(F32)

        if self.way == 2:
            return [start, rows_along, row_relay, row_to_b, shard_to_a, end_a]
        if self.way == 1:
            return [start, other_core, partner_b, relay_both, to_a, end_a]
        return [start, other_core, partner_b, partner_a, relay, end]

    def finish(self):
        p, full = self.p, self.full
        if not self.sent:
            return
        one, all_z, some = full.at[p.z, p.c, p.n], full.at[:, p.c, p.n], full.at[0:3, p.c, p.n]
        views = {
            self.SIB: full.at[:, p.c],
            self.A: all_z if self.way == 0 else one,
            self.B: full.at[0:2, p.c, p.n] if self.way == 2 else full.at[:, p.c, 0:2],
            self.Z: full.at[0:3, p.c] if self.way == 2 else some,
            self.ZA: some,
        }
        for slot in sorted(self.sent):
            view = views[slot]
            remote(view, view, self.send.at[slot], self.recv.at[0], p.sib()).wait_send()
        self.sent = set()

    def step(self, i):
        self.steps()[i]()


def stats(x):
    centre = jnp.mean(x, axis=-1, keepdims=True)
    centred = x - centre
    spread = jnp.mean(centred * centred, axis=-1, keepdims=True)
    r = lax.rsqrt(spread + EPS)
    return centred * r, r


def norm_into(src, gain, dst, rows):
    total = src.shape[0]

    def body(i):
        at = ds(i * rows, rows)
        xn, _ = stats(src[at, :].astype(F32))
        dst[at, :] = (xn * gain).astype(BF)

    loop(total // rows, body)


def halves(shape):
    return lax.broadcasted_iota(jnp.int32, shape, 1) < shape[1] // 2


def split_heads(x):
    low = halves(x.shape)
    zero = jnp.zeros_like(x)
    return jnp.concatenate([jnp.where(low, x, zero), jnp.where(low, zero, x)], 0)


def head_ones(keys):
    shape = (2 * keys, LANES)
    row = lax.broadcasted_iota(jnp.int32, shape, 0) < keys
    low = lax.broadcasted_iota(jnp.int32, shape, 1) < LANES // 2
    return jnp.where(row == low, 1.0, 0.0).astype(BF)


def unroll(first, last, body):
    for i in range(first, last):
        body(i)


def spatial_forward(qkv, probs, att, patches, width, first, last):
    head = width // HEADS
    scale = head ** -0.5
    pairs = range(HEADS // 2)
    ones = head_ones(patches)

    def body(s):
        at = ds(s * patches, patches)
        parts = []
        for pair in pairs:
            lane = pair * 2 * head
            q = qkv[at, lane : lane + 2 * head]
            parts.append(dot(q, split_heads(qkv[at, width + lane : width + lane + 2 * head]), 1, 1))
        scores = jnp.concatenate(parts, 0) * scale
        low = halves(scores.shape)
        top0 = jnp.max(jnp.where(low, scores, -jnp.inf), axis=-1, keepdims=True)
        top1 = jnp.max(jnp.where(low, -jnp.inf, scores), axis=-1, keepdims=True)
        e = jnp.exp(scores - jnp.where(low, top0, top1))
        e_low = e.astype(BF)
        parts = []
        for pair in pairs:
            lane = pair * 2 * head
            v2 = split_heads(qkv[at, 2 * width + lane : 2 * width + lane + 2 * head])
            rows = slice(pair * patches, (pair + 1) * patches)
            parts.append(dot(e_low[rows], jnp.concatenate([v2, ones], 1), 1, 0))
        both = jnp.concatenate(parts, 0)
        r = 1.0 / both[:, 2 * head :]
        probs[s] = (e * r).astype(BF).reshape(HEADS // 2, patches, 2 * patches)
        new = (both[:, : 2 * head] * r).astype(BF)
        for pair in pairs:
            att[at, pair * 2 * head : (pair + 1) * 2 * head] = new[pair * patches : (pair + 1) * patches]

    unroll(first, last, body)


def pad_heads(x, lanes):
    low = halves(x.shape)
    zero = jnp.zeros_like(x)
    fill = jnp.zeros((lanes - x.shape[0], x.shape[1]), x.dtype)
    return jnp.concatenate([jnp.where(low, x, zero), fill, jnp.where(low, zero, x), fill], 0).astype(BF)


LANES = 128
SUB = 8


def temporal_forward(qkv, probs, att, bias, slots, width, first, last):
    head = width // HEADS
    scale = head ** -0.5
    group = slots * SUB
    pairs = range(HEADS // 2)
    parts_of = [slice(half * group, (half + 1) * group) for half in range(2)]

    def body(i):
        at = ds(i * 2 * group, 2 * group)
        parts = []
        for pair in pairs:
            lane = pair * 2 * head
            q = qkv[at, lane : lane + 2 * head].astype(F32)
            k = qkv[at, width + lane : width + lane + 2 * head].astype(F32)
            for rows in parts_of:
                x = dot(q[rows].astype(BF), pad_heads(k[rows], LANES), 1, 1)
                parts += [x[:, :LANES], x[:, LANES:]]
        scores = jnp.stack(parts, 0) * scale + bias[...][None]
        e = jnp.exp(scores - jnp.max(scores, axis=-1, keepdims=True))
        p = (e / jnp.sum(e, axis=-1, keepdims=True)).astype(BF)
        for pair in pairs:
            lane = pair * 2 * head
            v = qkv[at, 2 * width + lane : 2 * width + lane + 2 * head].astype(F32)
            out = []
            for half, rows in enumerate(parts_of):
                j = (pair * 2 + half) * 2
                both = jnp.concatenate([p[j], p[j + 1]], 1)
                probs[i * 2 + half, pair] = both
                out.append(dot(both, pad_heads(v[rows], LANES), 1, 0))
            att[at, lane : lane + 2 * head] = jnp.concatenate(out, 0).astype(BF)

    unroll(first, last, body)


def make_bias(bias, count, slots):
    group = slots * SUB
    q = lax.broadcasted_iota(jnp.int32, (group, LANES), 0)
    k = lax.broadcasted_iota(jnp.int32, (group, LANES), 1)
    sq, sk = q // SUB, k // SUB
    ok = (q - sq * SUB == k - sk * SUB) & (sk <= sq) & (sk < count)
    bias[...] = jnp.where(ok, 0.0, -1e9)


def gelu_pair(z):
    k0 = 0.7978845608028654
    k1 = k0 * 0.044715
    z2 = z * z
    half = 0.5 + 0.5 * jnp.tanh(z * (k0 + k1 * z2))
    active = z * half
    slope = half + half * (z - active) * (2.0 * k0 + 6.0 * k1 * z2)
    return active, slope


def wide_rows(ref, width, columns=None):
    x = ref[...] if columns is None else ref[:, :, :, :, columns]
    return x.reshape(width, x.shape[-1])


def unsplit_heads(x, second, rows):
    low = halves((rows, x.shape[1]))
    return jnp.where(low, x[:rows], x[second : second + rows])


def spatial_backward(qkv, probs, grad, patches, width, first, last):
    head = width // HEADS
    scale = head ** -0.5
    pairs = range(HEADS // 2)
    rows_of = [slice(pair * patches, (pair + 1) * patches) for pair in pairs]

    def body(s):
        at = ds(s * patches, patches)
        cols = [[slice(t * width + p * 2 * head, t * width + (p + 1) * 2 * head) for t in range(3)] for p in pairs]
        p_low = probs[s].reshape(HEADS // 2 * patches, 2 * patches)
        soft = p_low.astype(F32)
        q = [qkv[at, cols[p][0]] for p in pairs]
        k2 = [split_heads(qkv[at, cols[p][1]]) for p in pairs]
        g = [grad[at, p * 2 * head : (p + 1) * 2 * head] for p in pairs]
        gp = [dot(g[p], split_heads(qkv[at, cols[p][2]]), 1, 1) for p in pairs]
        gv = [dot(p_low[rows_of[p]], g[p], 0, 0) for p in pairs]
        gp = jnp.concatenate(gp, 0)
        low = halves(gp.shape)
        both = gp * soft
        sum0 = jnp.sum(jnp.where(low, both, 0.0), axis=-1, keepdims=True)
        sum1 = jnp.sum(jnp.where(low, 0.0, both), axis=-1, keepdims=True)
        gs = (soft * (gp - jnp.where(low, sum0, sum1))).astype(BF)
        gq = [dot(gs[rows_of[p]], k2[p], 1, 0) for p in pairs]
        gk = [dot(gs[rows_of[p]], q[p], 0, 0) for p in pairs]
        for p in pairs:
            qkv[at, cols[p][0]] = (gq[p] * scale).astype(BF)
            qkv[at, cols[p][1]] = (unsplit_heads(gk[p], patches, patches) * scale).astype(BF)
            qkv[at, cols[p][2]] = unsplit_heads(gv[p], patches, patches).astype(BF)

    unroll(first, last, body)


def temporal_backward(qkv, probs, grad, slots, width, first, last):
    head = width // HEADS
    scale = head ** -0.5
    group = slots * SUB
    pairs = range(HEADS // 2)
    parts_of = [slice(half * group, (half + 1) * group) for half in range(2)]

    def body(i):
        at = ds(i * 2 * group, 2 * group)
        cols = [[slice(t * width + p * 2 * head, t * width + (p + 1) * 2 * head) for t in range(3)] for p in pairs]
        qs, ks, gs_in, ps, gp, soft = [], [], [], [], [], []
        for pair in pairs:
            q, k, v = (qkv[at, c].astype(F32) for c in cols[pair])
            g = grad[at, pair * 2 * head : (pair + 1) * 2 * head].astype(F32)
            for half, rows in enumerate(parts_of):
                qs.append(q[rows].astype(BF))
                ks.append(pad_heads(k[rows], LANES))
                gs_in.append(g[rows].astype(BF))
                p = probs[i * 2 + half, pair]
                ps.append(p)
                x = dot(gs_in[-1], pad_heads(v[rows], LANES), 1, 1)
                wide = p.astype(F32)
                gp += [x[:, :LANES], x[:, LANES:]]
                soft += [wide[:, :LANES], wide[:, LANES:]]
        many = range(len(ps))
        gv = [unsplit_heads(dot(ps[j], gs_in[j], 0, 0), LANES, group) for j in many]
        gp = jnp.stack(gp, 0)
        soft = jnp.stack(soft, 0)
        delta = jnp.sum(gp * soft, axis=-1, keepdims=True)
        gs = (soft * (gp - delta)).astype(BF)
        gs = [jnp.concatenate([gs[2 * j], gs[2 * j + 1]], 1) for j in many]
        gq = [dot(gs[j], ks[j], 1, 0) * scale for j in many]
        gk = [unsplit_heads(dot(gs[j], qs[j], 0, 0), LANES, group) * scale for j in many]
        for pair in pairs:
            for c, outs in zip(cols[pair], (gq, gk, gv)):
                qkv[at, c] = jnp.concatenate(outs[2 * pair : 2 * pair + 2], 0).astype(BF)

    unroll(first, last, body)


def norm_back(src, grad, gain, base, dst, low, sums, rows):
    total, width = grad.shape
    sums[...] = jnp.zeros_like(sums)

    def body(i):
        at = ds(i * rows, rows)
        xn, r = stats(src[at, :].astype(F32))
        g = grad[at, :]
        e = g * gain
        inner = e - jnp.mean(e, axis=-1, keepdims=True) - xn * jnp.mean(e * xn, axis=-1, keepdims=True)
        res = base[at, :] + r * inner
        if dst is not None:
            dst[at, :] = res
        low[at, :] = res.astype(BF)
        sums[...] += jnp.sum((g * xn).reshape(rows // SUB, SUB, width), axis=0)

    loop(total // rows, body)


def gain_row(gains, which):
    return gains[which : which + 1, :]


class Sizes:
    def __init__(self, mesh, video, in_weight):
        self.depth = mesh.shape["wide"] // 2
        self.narrow = mesh.shape["narrow"]
        self.slots, self.patches, self.width = video.shape[1:]
        self.hidden = in_weight.shape[2]
        self.tokens = self.slots * self.patches
        self.group = self.slots * SUB
        devices = 2 * self.depth * self.narrow
        w = self.width // devices
        self.shards = {
            "qkv": (w, 3 * self.width),
            "out": (w, self.width),
            "in": (w, self.hidden),
            "down": (self.hidden // devices, self.width),
        }
        self.mesh_dims = (self.depth, 2, self.narrow)

    def full(self, name):
        return self.mesh_dims + (TILE_GAIN if name == "gain" else self.shards[name])

    def acts(self, b):
        t, w, f = self.tokens, self.width, self.hidden
        pairs = HEADS // 2
        if b == 0:
            probs = (self.slots, pairs, self.patches, 2 * self.patches)
        else:
            probs = (self.patches // SUB, pairs, self.group, 2 * LANES)
        return {
            "normed": ((t, w), BF),
            "qkv": ((t, 3 * w), BF),
            "probs": (probs, BF),
            "att": ((t, w), BF),
            "middle": ((t, w), F32),
            "mlp": ((t, w), BF),
            "active": ((t, f), BF),
            "slope": ((t, f), BF),
        }


TILE_GAIN = (16, LANES)
NAMES = ("qkv", "out", "in", "down")
ACTS = ("normed", "qkv", "probs", "att", "middle", "mlp", "active", "slope")
SPLIT = {"gain": 1, "qkv": 2, "out": 1, "in": 2, "down": 2}


def pieces_of(name, b):
    return [(name, b, i) for i in range(SPLIT[name])]


GAIN = ("gain", 0)
GATHER_ORDER = [(*GAIN, 0)] + [piece for b in range(2) for name in NAMES for piece in pieces_of(name, b)]
SCATTER_ORDER = [
    piece for b in (1, 0) for name in ("down", "in", "out", "qkv") for piece in pieces_of(name, b)
] + [(*GAIN, 0)]


def columns_of(piece, columns):
    name, _, i = piece
    part = columns // SPLIT[name]
    return slice(i * part, (i + 1) * part)


def row_tile(tokens):
    return tokens // 2 if tokens % 32 == 0 else tokens


def keys_of_weights():
    return [(name, b) for b in range(2) for name in NAMES]


KEPT = ("normed", "qkv", "att", "middle", "mlp", "active", "slope")


def layer_kernel(sz, *refs):
    refs = list(refs)

    def grab(n):
        taken, refs[:n] = refs[:n], []
        return taken

    video, cotangent, frames, attn_gain, mlp_gain = grab(5)
    shard = dict(zip(NAMES, grab(4)))
    out, grad_video = grab(2)
    outs = dict(zip(NAMES, grab(4)))
    gain_outs = grab(2)
    acts_hbm = dict(zip(KEPT, grab(len(KEPT))))
    acts = dict(zip(ACTS, grab(8)))
    probs1, h1 = grab(2)
    full = dict(zip([GAIN] + keys_of_weights(), grab(9)))
    grads = dict(zip([(name, 1) for name in NAMES] + [GAIN], grab(5)))
    landing = {piece: grab(4) for piece in SCATTER_ORDER}
    gains, bias, gain_out, grad, grad_mid, grad_norm, low, grad_att, sums = grab(9)
    gather_send, gather_recv, scatter_send, scatter_recv, local = grab(5)
    assert not refs
    for name in NAMES:
        grads[(name, 0)] = full[(name, 1)]

    place = Place()
    met = place.greet()

    def part_of(ref, piece, columns):
        if SPLIT[piece[0]] == 1:
            return ref
        return ref.at[(slice(None),) * (len(ref.shape) - 1) + (columns_of(piece, columns),)]

    gathers = {}
    at_send = at_recv = 0
    for k, piece in enumerate(GATHER_ORDER):
        n_send, n_recv = Gather.semaphores(GATHER_WAYS[k])
        ref = full[piece[:2]]
        sems = [gather_send.at[at_send : at_send + n_send], gather_recv.at[at_recv : at_recv + n_recv]]
        gathers[piece] = Gather(place, part_of(ref, piece, ref.shape[-1]), *sems, GATHER_WAYS[k])
        at_send += n_send
        at_recv += n_recv
    scatters = {}
    at_send = at_recv = 0
    for k, piece in enumerate(SCATTER_ORDER):
        n_send, n_recv = Scatter.semaphores(SCATTER_WAYS[k])
        ref = grads[piece[:2]]
        columns = ref.shape[-1]
        target = gain_out if piece[:2] == GAIN else outs[piece[0]].at[piece[1]]
        sems = [scatter_send.at[at_send : at_send + n_send], scatter_recv.at[at_recv : at_recv + n_recv]]
        scatters[piece] = Scatter(
            place,
            part_of(ref, piece, columns),
            *landing[piece],
            part_of(target, piece, columns),
            *sems,
            SCATTER_WAYS[k],
        )
        at_send += n_send
        at_recv += n_recv
    own = (place.z, place.c, place.n)
    full[GAIN][own] = place_gains(attn_gain, mlp_gain, place.w * sz.narrow + place.n)
    for key in keys_of_weights():
        full[key][own] = shard[key[0]][key[1]].astype(BF)
    place.met(met)

    moving = {}

    def move(name, src, dst):
        copy = pltpu.make_async_copy(src, dst, local.at[KEPT.index(name)])
        copy.start()
        moving[name] = copy

    def settle(*names):
        for name in names:
            if name in moving:
                moving.pop(name).wait()

    def act(name, b):
        return probs1 if (name, b) == ("probs", 1) else acts[name]

    def keep(b, *names):
        for name in names:
            if b == 0 and name in KEPT:
                move(name, acts[name], acts_hbm[name])

    def fetch(b, *names):
        for name in names:
            if b == 1 and name in KEPT:
                settle(name)
                move(name, acts_hbm[name], acts[name])

    count = (frames[0] + 1) // 2
    t, w = sz.tokens, sz.width

    def stage_gain():
        make_bias(bias, count, sz.slots)
        tile = jnp.sum(full[GAIN][...].astype(F32).reshape(-1, 16, LANES), axis=0)
        for g in range(4):
            rows = [tile[g * 4 + r : g * 4 + r + 1, :] for r in range(w // LANES)]
            gains[g : g + 1, :] = jnp.concatenate(rows, 1)

    def forward_stages(b):
        a = {name: act(name, b) for name in ACTS}
        h = video if b == 0 else h1

        def norm1():
            settle("normed")
            norm_into(h, gain_row(gains, 2 * b), a["normed"], row_tile(t))
            keep(b, "normed")

        def qkv(first, last):
            settle("qkv")
            at = slice(first, last)
            a["qkv"][:, at] = dot(a["normed"][...], wide_rows(full[("qkv", b)], w, at), 1, 0).astype(BF)
            if last == 3 * w:
                keep(b, "qkv")

        def attend(first, last):
            settle("att")
            if b == 0:
                spatial_forward(a["qkv"], a["probs"], a["att"], sz.patches, w, first, last)
                end = sz.slots
            else:
                temporal_forward(a["qkv"], a["probs"], a["att"], bias, sz.slots, w, first, last)
                end = sz.patches // (2 * SUB)
            if last == end:
                keep(b, "probs", "att")

        def project():
            settle("middle")
            new = dot(a["att"][...], wide_rows(full[("out", b)], w), 1, 0)
            a["middle"][...] = h[...].astype(F32) + new
            keep(b, "middle")

        def norm2():
            settle("mlp")
            norm_into(a["middle"], gain_row(gains, 2 * b + 1), a["mlp"], row_tile(t))
            keep(b, "mlp")

        def expand(first, last):
            at = slice(first, last)
            settle("active", "slope")
            weight = wide_rows(full[("in", b)], w, at)
            rows = row_tile(t)
            for r in range(0, t, rows):
                active, slope = gelu_pair(dot(a["mlp"][r : r + rows, :], weight, 1, 0))
                a["active"][r : r + rows, at] = active.astype(BF)
                a["slope"][r : r + rows, at] = slope.astype(BF)
            if last == sz.hidden:
                keep(b, "active", "slope")

        def contract(first, last):
            at = slice(first, last)
            new = a["middle"][:, at] + dot(a["active"][...], wide_rows(full[("down", b)], sz.hidden, at), 1, 0)
            if b == 0:
                new = new.reshape(sz.slots, sz.patches // SUB, SUB, last - first)
                for s in range(sz.slots):
                    h1_view[:, s * SUB : (s + 1) * SUB, at] = new[s]
            else:
                valid = lax.broadcasted_iota(jnp.int32, (sz.slots, 1, 1), 0) < count
                new = new.reshape(sz.patches // (2 * SUB), 2, sz.slots, SUB, last - first)
                for i in range(sz.patches // (2 * SUB)):
                    rows = jnp.concatenate([new[i, 0], new[i, 1]], axis=1)
                    out[:, i * 2 * SUB : (i + 1) * 2 * SUB, at] = jnp.where(valid, rows, 0.0).astype(BF)
                if last == w:
                    fetch(b, "active", "middle")

        n_a = sz.slots if b == 0 else sz.patches // (2 * SUB)
        cuts = [-(-n_a * i // 4) for i in range(5)]
        todo = [norm1]
        todo += [functools.partial(qkv, 3 * w * i // 2, 3 * w * (i + 1) // 2) for i in range(2)]
        todo += [functools.partial(attend, cuts[i], cuts[i + 1]) for i in range(4)]
        todo += [project, norm2]
        todo += [functools.partial(expand, sz.hidden * i // 4, sz.hidden * (i + 1) // 4) for i in range(4)]
        last = [functools.partial(contract, w * i // 2, w * (i + 1) // 2) for i in range(2)]
        return todo, last

    h1_view = h1.reshape(sz.patches // SUB, sz.group, w)

    def start():
        valid = lax.broadcasted_iota(jnp.int32, (sz.slots, 1, 1), 0) < count

        def body(i):
            rows = cotangent[:, ds(i * 2 * SUB, 2 * SUB), :].astype(F32)
            rows = jnp.where(valid, rows, 0.0)
            both = [rows[:, half * SUB : (half + 1) * SUB, :].reshape(sz.group, w) for half in range(2)]
            rows = jnp.concatenate(both, 0)
            at = ds(i * 2 * sz.group, 2 * sz.group)
            grad[at, :] = rows
            low[at, :] = rows.astype(BF)

        loop(sz.patches // (2 * SUB), body)

    def put_gain(which):
        row = jnp.sum(sums[...], axis=0, keepdims=True)
        per = w // LANES
        tile = jnp.concatenate([row[:, r * LANES : (r + 1) * LANES] for r in range(per)], 0)
        gain_rows[which * per : (which + 1) * per, :] = tile

    gain_rows = gain_out

    def backward_stages(b):
        a = {name: act(name, b) for name in ACTS}

        half = sz.hidden // 2
        z_half = sz.depth // 2

        def down_grad(i):
            settle("active")
            if b == 0 and i == 0:
                for gather in gathers.values():
                    gather.finish()
            at = slice(i * w // 2, (i + 1) * w // 2)
            g = dot(a["active"][...], low[:, at], 0, 0).astype(BF)
            grads[("down", b)][:, :, :, :, at] = g.reshape(sz.full("down")[:-1] + (w // 2,))

        def hidden_back(i):
            settle("slope")
            at = slice(i * half, (i + 1) * half)
            weight = full[("down", b)][i * z_half : (i + 1) * z_half].reshape(half, w)
            a["slope"][:, at] = (dot(low[...], weight, 1, 1) * a["slope"][:, at].astype(F32)).astype(BF)

        def in_grad(i):
            settle("mlp")
            at = slice(i * half, (i + 1) * half)
            g = dot(a["mlp"][...], a["slope"][:, at], 0, 0).astype(BF)
            grads[("in", b)][:, :, :, :, at] = g.reshape(sz.full("in")[:-1] + (half,))
            if i == 1:
                fetch(b, "mlp")

        def back_rows(src, weight, put):
            put(dot(src[...], wide_rows(weight, w), 1, 1))

        def mlp_back():

            def put(x):
                grad_norm[...] = x

            back_rows(a["slope"], full[("in", b)], put)
            fetch(b, "slope")

        def norm2_back():
            settle("middle")
            norm_back(a["middle"], grad_norm, gain_row(gains, 2 * b + 1), grad, grad_mid, low, sums, row_tile(t))
            put_gain(2 * b + 1)

        def out_grad():
            settle("att")

            g = dot(a["att"][...], low[...], 0, 0).astype(BF)
            grads[("out", b)][...] = g.reshape(sz.full("out"))
            fetch(b, "att")

        def att_back():

            def put(x):
                grad_att[...] = x.astype(BF)

            back_rows(low, full[("out", b)], put)

        def attend(first, last):
            settle("qkv", "probs")
            if b == 0:
                spatial_backward(a["qkv"], a["probs"], grad_att, sz.patches, w, first, last)
            else:
                temporal_backward(a["qkv"], a["probs"], grad_att, sz.slots, w, first, last)

        def qkv_grad(first, last):
            settle("normed")
            at = slice(first, last)
            g = dot(a["normed"][...], a["qkv"][:, at], 0, 0).astype(BF)
            grads[("qkv", b)][:, :, :, :, at] = g.reshape(sz.full("qkv")[:-1] + (last - first,))
            if last == 3 * w:
                fetch(b, "normed")

        def qkv_back():

            def put(x):
                grad_norm[...] = x

            back_rows(a["qkv"], full[("qkv", b)], put)
            fetch(b, "qkv")

        def norm1_back():
            src = h1 if b == 1 else video
            if b == 1:
                norm_back(src, grad_norm, gain_row(gains, 2), grad_mid, grad, low, sums, row_tile(t))
            else:
                norm_back(src, grad_norm, gain_row(gains, 0), grad_mid, None, low, sums, row_tile(t))
                grad_video[...] = low[...].reshape(grad_video.shape)
            put_gain(2 * b)

        def reorder():
            view = grad.reshape(sz.patches // SUB, sz.group, w)

            def body(s):
                rows = view[:, ds(s * SUB, SUB), :].reshape(sz.patches, w)
                at = ds(s * sz.patches, sz.patches)
                grad_norm[at, :] = rows
                low[at, :] = rows.astype(BF)

            loop(sz.slots, body)
            grad[...] = grad_norm[...]

        n_a = sz.slots if b == 0 else sz.patches // (2 * SUB)
        cuts = [-(-n_a * i // 4) for i in range(5)]
        todo = []
        for piece in (down_grad, hidden_back, in_grad):
            todo += [functools.partial(piece, i) for i in range(2)]
        todo += [mlp_back, norm2_back, out_grad, att_back]
        todo += [functools.partial(attend, cuts[i], cuts[i + 1]) for i in range(4)]
        todo += [functools.partial(qkv_grad, 3 * w * i // 2, 3 * w * (i + 1) // 2) for i in range(2)]
        if b == 1:
            todo += output
        todo += [qkv_back, norm1_back]
        if b == 1:
            todo += [reorder]
        return todo

    def spread_gain():
        tile = gain_out[...]
        grads[GAIN][...] = jnp.broadcast_to(tile, sz.full("gain"))

    first, last = forward_stages(0)
    second, output = forward_stages(1)
    work = [start, stage_gain] + first + last + second
    work = iter(work + backward_stages(1) + backward_stages(0) + [spread_gain])
    steps = [gathers[piece] for piece in GATHER_ORDER] + [scatters[piece] for piece in SCATTER_ORDER]
    for op in PLAN:
        if op < 0:
            next(work)()
        else:
            steps[op // 8].step(op % 8)
    assert next(work, None) is None
    pick_gains(gain_out[...], gain_outs, place.w * sz.narrow + place.n)
    settle(*KEPT)
    for scatter in scatters.values():
        scatter.finish()


def place_gains(attn_gain, mlp_gain, index):
    own = attn_gain.shape[1]
    per = LANES // own
    row = lax.broadcasted_iota(jnp.int32, (TILE_GAIN[0] // 4, LANES), 0)
    lane = lax.broadcasted_iota(jnp.int32, (TILE_GAIN[0] // 4, LANES), 1) // own
    here = row * per + lane == index
    tiles = []
    for b in range(2):
        for ref in (attn_gain, mlp_gain):
            values = jnp.concatenate([ref[b : b + 1, :]] * per, 1)
            tiles.append(jnp.where(here, values, 0.0))
    return jnp.concatenate(tiles, 0).astype(BF)


def pick_gains(tile, outs, index):
    own = outs[0].shape[1]
    per = LANES // own
    rows = TILE_GAIN[0] // 4
    row = lax.broadcasted_iota(jnp.int32, (rows, own), 0)
    for b in range(2):
        for kind, out in enumerate(outs):
            first = (2 * b + kind) * rows
            total = jnp.zeros((rows, own), F32)
            for j in range(per):
                piece = tile[first : first + rows, j * own : (j + 1) * own]
                total = total + jnp.where(row * per + j == index, piece, 0.0)
            out[b : b + 1, :] = jnp.sum(total, axis=0, keepdims=True)


PLAN = (
    112, 8, 48, 0, 24, 16, 1, 9, 64, 40, 104, 17, 88, 113, 49, 2, 10, 41, 25, 32, 72, 80, 18, 65, 3, 33, 96,
    26, 56, 11, 19, -1, 27, 57, 73, 81, 4, 42, 50, 34, 12, 5, -1, -1, 13, -1, 20, 21, -1, 58, 28, -1, 35, 89,
    97, 74, 51, -1, 66, -1, 43, 59, -1, 29, -1, -1, 75, 82, 90, 36, 37, -1, -1, 67, 44, 52, 98, 45, -1, 105,
    -1, 60, 83, 114, 91, 53, -1, 61, -1, 68, 99, 106, 76, -1, 69, -1, 77, -1, -1, -1, 84, -1, -1, 92, 115,
    107, 85, -1, -1, 100, 93, -1, -1, 101, -1, -1, 108, 116, -1, 120, -1, 128, 109, 117, -1, -1, 129, 121,
    -1, 136, -1, 144, -1, -1, -1, 152, 145, -1, -1, 153, -1, -1, 137, 130, 122, -1, -1, 160, -1, 168, 146,
    -1, 161, -1, -1, 169, -1, -1, 138, -1, 176, 154, 162, -1, 184, 123, 147, 177, -1, -1, -1, 192, 185, 139,
    -1, 200, -1, 193, 178, -1, 124, 201, -1, 208, 163, -1, 170, -1, 209, -1, 179, 186, -1, -1, -1, 216, 194,
    202, -1, 224, 217, 140, -1, -1, 187, 225, -1, 232, 203, 233, 188, 148, 210, 218, 226, 234, 131, 155, 171,
    195, 211, 219, 227, 235, 132, 156, 164, 172, 180, 196, 204, 212, 220, 228, 236, 125, 133, 141, 149, 157,
    165, 173, 181, 189, 197, 205, 213, 221, 229, 237,
)
GATHER_WAYS = (
    0, 0, 0, 0, 0, 0, 2, 0, 2, 0, 0, 0, 0, 0, 2,
)
SCATTER_WAYS = (
    0, 2, 0, 1, 2, 0, 2, 1, 0, 1, 0, 0, 1, 0, 0,
)


def copy_kernel(count, *refs):
    sems = refs[-1]
    refs = refs[:-1]
    down = [pltpu.make_async_copy(refs[i], refs[2 * count + i], sems.at[i]) for i in range(count)]
    up = [pltpu.make_async_copy(refs[2 * count + i], refs[count + i], sems.at[i]) for i in range(count)]
    for copy in down:
        copy.start()
    for i in range(count):
        down[i].wait()
        up[i].start()
    for copy in up:
        copy.wait()


def by_kernels(mesh, sz):
    vmem = pl.BlockSpec(memory_space=pltpu.VMEM)
    smem = pl.BlockSpec(memory_space=pltpu.SMEM)
    anyw = pl.BlockSpec(memory_space=pl.ANY)
    shape = jax.ShapeDtypeStruct
    t, w = sz.tokens, sz.width
    acts0 = sz.acts(0)
    clip_shape = shape((sz.slots, sz.patches, w), BF)
    dma = pltpu.SemaphoreType.DMA

    def landing(k, piece):
        full = sz.full(piece[0])
        full = full[:-1] + (full[-1] // SPLIT[piece[0]],)
        kind = F32 if piece[0] == "gain" else BF
        return [pltpu.VMEM(s, kind) for s in Scatter.landing(full, SCATTER_WAYS[k])]

    def run(video, frames, cotangent, qkv_weight, out_weight, in_weight, down_weight, attn_gain, mlp_gain):
        gain_shape = shape(attn_gain.shape, F32)
        shapes = [clip_shape, clip_shape]
        shapes += [shape((2,) + sz.shards[name], F32) for name in NAMES]
        shapes += [gain_shape, gain_shape]
        n_gather = [sum(Gather.semaphores(way)[i] for way in GATHER_WAYS) for i in range(2)]
        n_scatter = [sum(Scatter.semaphores(way)[i] for way in SCATTER_WAYS) for i in range(2)]
        res = pl.pallas_call(
            functools.partial(layer_kernel, sz),
            out_shape=shapes + [shape(*acts0[name]) for name in KEPT],
            in_specs=[vmem, vmem, smem] + [vmem] * 6,
            out_specs=[vmem] * len(shapes) + [anyw] * len(KEPT),
            scratch_shapes=[pltpu.VMEM(*acts0[name]) for name in ACTS]
            + [pltpu.VMEM(*sz.acts(1)["probs"]), pltpu.VMEM((t, w), F32)]
            + [pltpu.VMEM(sz.full(name), BF) for name, _ in [GAIN] + keys_of_weights()]
            + [pltpu.VMEM(sz.full(name), BF) for name in NAMES]
            + [pltpu.VMEM(sz.full("gain"), F32)]
            + [buffer for k, piece in enumerate(SCATTER_ORDER) for buffer in landing(k, piece)]
            + [
                pltpu.VMEM((4, w), F32),
                pltpu.VMEM((sz.group, LANES), F32),
                pltpu.VMEM(TILE_GAIN, F32),
                pltpu.VMEM((t, w), F32),
                pltpu.VMEM((t, w), F32),
                pltpu.VMEM((t, w), F32),
                pltpu.VMEM((t, w), BF),
                pltpu.VMEM((t, w), BF),
                pltpu.VMEM((SUB, w), F32),
                dma((n_gather[0],)),
                dma((n_gather[1],)),
                dma((n_scatter[0],)),
                dma((n_scatter[1],)),
                dma((len(KEPT),)),
            ],
            compiler_params=pltpu.CompilerParams(
                collective_id=0, has_side_effects=True, vmem_limit_bytes=VMEM_LIMIT
            ),
        )(
            video.reshape(t, w),
            cotangent.reshape(clip_shape.shape),
            frames,
            attn_gain,
            mlp_gain,
            qkv_weight,
            out_weight,
            in_weight,
            down_weight,
        )
        res = list(res)[: len(shapes)]
        res = pl.pallas_call(
            functools.partial(copy_kernel, len(res)),
            out_shape=shapes,
            in_specs=[anyw] * len(res),
            out_specs=[anyw] * len(res),
            scratch_shapes=[pltpu.VMEM(x.shape, x.dtype) for x in shapes] + [dma((len(res),))],
        )(*res)
        return (res[0].reshape(video.shape), res[1].reshape(video.shape), *res[2:])

    return run


def norm_rows(inputs, scaling):
    centre = jnp.mean(inputs, axis=-1, keepdims=True)
    centred = inputs - centre
    spread = jnp.mean(centred * centred, axis=-1, keepdims=True)
    return centred * lax.rsqrt(spread + EPS) * scaling


def project(rows_in, matrix):
    return jnp.einsum("cspd,de->cspe", rows_in, matrix, preferred_element_type=jnp.float32)


def project_back(rows_in, matrix):
    return jnp.einsum("cspe,de->cspd", rows_in, matrix, preferred_element_type=jnp.float32)


def weight_grad(left, right):
    return jnp.einsum("cspd,cspe->de", left, right, preferred_element_type=jnp.float32)


def pair_scores(first, second, which_block):
    if which_block == 0:
        return jnp.einsum("csphe,csqhe->cshpq", first, second, preferred_element_type=jnp.float32)
    return jnp.einsum("csphe,ctphe->cphst", first, second, preferred_element_type=jnp.float32)


def pair_mix(weighting, second, which_block):
    if which_block == 0:
        return jnp.einsum(
            "cshpq,csqhe->csphe", weighting, second, preferred_element_type=jnp.float32
        )
    return jnp.einsum("cphst,ctphe->csphe", weighting, second, preferred_element_type=jnp.float32)


def pair_back(weighting, first, which_block):
    if which_block == 0:
        return jnp.einsum(
            "cshpq,csphe->csqhe", weighting, first, preferred_element_type=jnp.float32
        )
    return jnp.einsum("cphst,csphe->ctphe", weighting, first, preferred_element_type=jnp.float32)


def masked_scores(queries, key_rows, which_block, allowed):
    head_size = queries.shape[-1]
    scores = pair_scores(queries, key_rows, which_block) * head_size ** (-0.5)
    if which_block == 1:
        scores = jnp.where(allowed[:, None, None], scores, -1000000000.0)
    return scores


def block_forward(inputs, weights, which_block, allowed):
    qkv_matrix, out_matrix, in_matrix, down_matrix, attn_scaling, mlp_scaling = weights
    full_shape = inputs.shape
    head_size = full_shape[-1] // HEADS
    normed, norm_pull = jax.vjp(norm_rows, inputs, attn_scaling.astype(jnp.float32))
    normed_low = normed.astype(jnp.bfloat16)
    qkv_rows = project(normed_low, qkv_matrix).astype(jnp.bfloat16)
    split = qkv_rows.reshape(full_shape[:3] + (3, HEADS, head_size))
    queries = split[:, :, :, 0]
    key_rows = split[:, :, :, 1]
    value_rows = split[:, :, :, 2]
    scores = masked_scores(queries, key_rows, which_block, allowed)
    row_max = jnp.max(scores, axis=-1, keepdims=True)
    shifted = jnp.exp(scores - row_max)
    row_sum = jnp.sum(shifted, axis=-1, keepdims=True)
    log_total = row_max + jnp.log(row_sum)
    probs_low = (shifted / row_sum).astype(jnp.bfloat16)
    attended = pair_mix(probs_low, value_rows, which_block).reshape(full_shape).astype(jnp.bfloat16)
    middle = inputs + project(attended, out_matrix)
    normed_mlp, mlp_pull = jax.vjp(norm_rows, middle, mlp_scaling.astype(jnp.float32))
    normed_mlp_low = normed_mlp.astype(jnp.bfloat16)
    hidden = project(normed_mlp_low, in_matrix)
    active, gelu_pull = jax.vjp(jax.nn.gelu, hidden)
    active_low = active.astype(jnp.bfloat16)
    result = middle + project(active_low, down_matrix)
    stored = (
        norm_pull,
        normed_low,
        queries,
        key_rows,
        value_rows,
        log_total,
        attended,
        mlp_pull,
        normed_mlp_low,
        gelu_pull,
        active_low,
    )
    return (result, stored)


def block_backward(gradient, stored, weights, which_block, allowed):
    qkv_matrix, out_matrix, in_matrix, down_matrix, attn_scaling, mlp_scaling = weights
    (
        norm_pull,
        normed_low,
        queries,
        key_rows,
        value_rows,
        log_total,
        attended,
        mlp_pull,
        normed_mlp_low,
        gelu_pull,
        active_low,
    ) = stored
    full_shape = gradient.shape
    head_size = queries.shape[-1]
    result_low = gradient.astype(jnp.bfloat16)
    grad_down_w = weight_grad(active_low, result_low)
    grad_active = project_back(result_low, down_matrix)
    grad_hidden = gelu_pull(grad_active)[0].astype(jnp.bfloat16)
    grad_in_w = weight_grad(normed_mlp_low, grad_hidden)
    grad_normed_mlp = project_back(grad_hidden, in_matrix)
    middle_part, grad_mlp_scaling = mlp_pull(grad_normed_mlp)
    grad_middle = gradient + middle_part
    middle_low = grad_middle.astype(jnp.bfloat16)
    grad_out_w = weight_grad(attended, middle_low)
    grad_attended = project_back(middle_low, out_matrix).astype(jnp.bfloat16)
    grad_attended = grad_attended.reshape(queries.shape)
    scores = masked_scores(queries, key_rows, which_block, allowed)
    soft_probs = jnp.exp(scores - log_total)
    grad_probs = pair_scores(grad_attended, value_rows, which_block)
    row_delta = jnp.sum(grad_probs * soft_probs, axis=-1, keepdims=True)
    grad_scores = (soft_probs * (grad_probs - row_delta)).astype(jnp.bfloat16)
    score_scale = head_size ** (-0.5)
    grad_queries = pair_mix(grad_scores, key_rows, which_block) * score_scale
    grad_keys = pair_back(grad_scores, queries, which_block) * score_scale
    grad_values = pair_back(soft_probs.astype(jnp.bfloat16), grad_attended, which_block)
    grad_qkv_rows = jnp.stack([grad_queries, grad_keys, grad_values], axis=3).astype(jnp.bfloat16)
    grad_qkv_rows = grad_qkv_rows.reshape(full_shape[:3] + (3 * full_shape[-1],))
    grad_qkv_w = weight_grad(normed_low, grad_qkv_rows)
    grad_normed = project_back(grad_qkv_rows, qkv_matrix)
    input_part, grad_attn_scaling = norm_pull(grad_normed)
    grad_input = grad_middle + input_part
    return (
        grad_input,
        (grad_qkv_w, grad_out_w, grad_in_w, grad_down_w, grad_attn_scaling, grad_mlp_scaling),
    )


def block_shards(qkv_weight, out_weight, in_weight, down_weight, attn_gain, mlp_gain, block_index):
    return (
        qkv_weight[block_index].astype(jnp.bfloat16),
        out_weight[block_index].astype(jnp.bfloat16),
        in_weight[block_index].astype(jnp.bfloat16),
        down_weight[block_index].astype(jnp.bfloat16),
        attn_gain[block_index].astype(jnp.bfloat16),
        mlp_gain[block_index].astype(jnp.bfloat16),
    )


def by_einsums(
    video, frames, cotangent, qkv_weight, out_weight, in_weight, down_weight, attn_gain, mlp_gain
):
    axes = ("wide", "narrow")
    slot_counts = (frames + 1) // 2
    positions = jnp.arange(video.shape[1], dtype=jnp.int32)
    allowed = (positions[None, None, :] <= positions[None, :, None]) & (
        positions[None, None, :] < slot_counts[:, None, None]
    )
    valid_slot = (positions[None, :] < slot_counts[:, None]).astype(jnp.float32)[:, :, None, None]
    weights = (qkv_weight, out_weight, in_weight, down_weight, attn_gain, mlp_gain)
    full = [
        tuple(lax.all_gather(part, axes, axis=0, tiled=True) for part in block_shards(*weights, b))
        for b in range(2)
    ]
    spatial_out, spatial_stored = block_forward(video.astype(jnp.float32), full[0], 0, allowed)
    temporal_out, temporal_stored = block_forward(spatial_out, full[1], 1, allowed)
    output = (temporal_out * valid_slot).astype(jnp.bfloat16)
    gradient = cotangent.astype(jnp.float32) * valid_slot
    grad_between, temporal_grads = block_backward(gradient, temporal_stored, full[1], 1, allowed)
    grad_start, spatial_grads = block_backward(grad_between, spatial_stored, full[0], 0, allowed)
    summed = [
        lax.psum_scatter(jnp.stack(pair), axes, scatter_dimension=1, tiled=True)
        for pair in zip(spatial_grads, temporal_grads)
    ]
    return (output, grad_start.astype(jnp.bfloat16), *summed)


def solution(mesh):
    both = ("wide", "narrow")
    clips = P(both, None, None, None)
    rows = P(None, both, None)
    in_specs = (clips, P(both), clips, rows, rows, rows, rows, P(None, both), P(None, both))
    out_specs = (clips, clips, rows, rows, rows, rows, P(None, both), P(None, both))

    def shards(*args):
        sz = Sizes(mesh, args[0], args[5])
        whole_tiles = all(rows % 16 == 0 for rows, _ in sz.shards.values())
        if whole_tiles and sz.depth == 4 and sz.narrow == 4 and args[0].shape[0] == 1:
            return by_kernels(mesh, sz)(*args)
        return by_einsums(*args)

    return jax.shard_map(shards, mesh=mesh, in_specs=in_specs, out_specs=out_specs, check_vma=False)
```

```python
import functools

import jax
import jax.numpy as jnp
from jax import lax
from jax.experimental import pallas as pl
from jax.experimental.pallas import tpu as pltpu
from jax.sharding import PartitionSpec as P

HEADS = 8
EPS = 1e-05
BF = jnp.bfloat16
F32 = jnp.float32
MESH = pl.DeviceIdType.MESH
VMEM_LIMIT = 62 * 2**20


def dot(a, b, ca, cb):
    return lax.dot_general(a, b, (((ca,), (cb,)), ((), ())), preferred_element_type=F32)


def ds(start, size):
    if isinstance(start, int):
        return pl.ds(start, size)
    return pl.ds(pl.multiple_of(start, size), size)


def loop(count, body, first=0):
    if count - first == 1:
        body(first)
        return

    def step(i, carry):
        body(i)
        return carry

    lax.fori_loop(first, count, step, 0)


class Place:
    def __init__(self):
        self.w = lax.axis_index("wide")
        self.n = lax.axis_index("narrow")
        self.z = self.w // 2
        self.c = self.w % 2
        first = 1 + self.c
        self.na = self.flip(self.n, first)
        self.nb = self.flip(self.n, 3 - first)
        self.nab = 3 - self.n
        self.z1 = self.flip(self.z, 1)
        self.z2 = self.flip(self.z, 2)
        self.z3 = 3 - self.z
        self.others = (self.z1, self.z2, self.z3)
        self.end = (self.z == 0) | (self.z == 3)
        self.middle = (self.z == 1) | (self.z == 2)

    @staticmethod
    def flip(n, step):
        bit = (n // step) % 2
        return n + step - 2 * step * bit

    def sib(self):
        return (self.z * 2 + 1 - self.c, self.n)

    def a(self):
        return (self.w, self.na)

    def b(self):
        return (self.w, self.nb)

    def chip(self, z):
        return (z * 2 + self.c, self.n)

    def greet(self):
        targets = [self.sib(), self.a(), self.b()] + [self.chip(z) for z in self.others]
        for t in targets:
            pl.semaphore_signal(pltpu.get_barrier_semaphore(), inc=1, device_id=t, device_id_type=MESH)
        return len(targets)

    def met(self, count):
        pl.semaphore_wait(pltpu.get_barrier_semaphore(), count)


def remote(src, dst, send, recv, target):
    return pltpu.make_async_remote_copy(src, dst, send, recv, device_id=target, device_id_type=MESH)


class Gather:
    def __init__(self, place, full, send, recv, way):
        self.p, self.full, self.send, self.recv, self.way = place, full, send, recv, way
        self.sent = set()

    A, B, SIB, Z, ZA = range(5)
    @staticmethod
    def semaphores(way):
        return (5, 7) if way == 1 else (4, 5)

    @staticmethod
    def near_far(which):
        return (3, 4) if which == 0 else (5, 6)

    def go(self, out, into, index, target):
        view = self.full.at[index]
        remote(view, view, self.send.at[out], self.recv.at[into], target).start()
        self.sent.add(out)

    def take(self, slot, view):
        remote(view, view, self.send.at[0], self.recv.at[slot], self.p.sib()).wait_recv()

    def shards(self, count):
        p = self.p
        return self.full.at[p.z, p.c, p.n] if count == 1 else self.full.at[0:count, p.c, p.n]

    def pass_on(self, slot, index):
        p = self.p
        self.go(slot, slot, index, {self.A: p.a, self.B: p.b, self.SIB: p.sib}[slot]())

    def others(self, n, slots):
        p = self.p
        for z in p.others:
            for slot in slots:
                self.pass_on(slot, (z, p.c, n))

    def column(self, n, slots):
        for slot in slots:
            self.pass_on(slot, (slice(None), self.p.c, n))

    def along(self, which, n):
        p = self.p
        near, far = self.near_far(which)
        own = (p.z, p.c, n)
        self.go(self.Z + which, far, own, p.chip(p.z2))
        self.go(self.Z + which, near, own, p.chip(p.z1))

        @pl.when(p.middle)
        def _():
            self.go(self.Z + which, near, own, p.chip(p.z3))

    def relay(self, which, n):
        p = self.p
        near, far = self.near_far(which)
        self.take(far, self.shards(1))

        @pl.when(p.middle)
        def _():
            self.go(self.Z + which, near, (p.z2, p.c, n), p.chip(p.z1))

    def take_near(self, which):
        self.take(self.near_far(which)[0], self.shards(2))

    def steps(self):
        p = self.p
        A, B, SIB = self.A, self.B, self.SIB

        def start():
            own = (p.z, p.c, p.n)
            self.pass_on(A, own)
            self.pass_on(B, own)
            self.along(0, p.n)
            self.pass_on(SIB, own)

        def own_relay():
            self.relay(0, p.n)

        def own_column():
            self.take_near(0)
            self.others(p.n, (A, B, SIB))

        def column_of_a():
            self.take(A, self.shards(self.full.shape[0]))
            self.column(p.na, (B, SIB))

        def shard_of_a():
            self.take(A, self.shards(1))
            self.along(1, p.na)
            self.pass_on(B, (p.z, p.c, p.na))
            self.pass_on(SIB, (p.z, p.c, p.na))

        def own_column_late():
            self.take_near(0)
            self.others(p.n, (B, SIB))
            self.relay(1, p.na)

        def column_of_a_late():
            self.take_near(1)
            self.others(p.na, (B, SIB))

        def from_b():
            self.take(B, self.full.at[:, p.c, 0:2])
            self.column(p.nb, (SIB,))
            self.column(p.nab, (SIB,))

        def from_sib():
            self.take(SIB, self.full.at[:, p.c])

        def start_row():
            self.pass_on(A, (p.z, p.c, p.n))
            self.pass_on(B, (p.z, p.c, p.n))

        def shard_of_a_on():
            self.take(A, self.shards(1))
            self.pass_on(B, (p.z, p.c, p.na))

        near, far = self.near_far(0)
        row = (p.z, p.c)

        def row_along():
            self.take(B, self.shards(2))
            self.go(self.Z, far, row, p.chip(p.z2))
            self.go(self.Z, near, row, p.chip(p.z1))

            @pl.when(p.middle)
            def _():
                self.go(self.Z, near, row, p.chip(p.z3))

        def row_relay():
            self.take(far, self.full.at[p.z, p.c])

            @pl.when(p.middle)
            def _():
                self.go(self.Z, near, (p.z2, p.c), p.chip(p.z1))

        def rows_over():
            self.take(near, self.full.at[0:2, p.c])
            self.pass_on(SIB, (slice(None), p.c))

        if self.way == 2:
            return [start_row, shard_of_a_on, row_along, row_relay, rows_over, from_sib]
        if self.way == 1:
            return [start, shard_of_a, own_relay, own_column_late, column_of_a_late, from_b, from_sib]
        return [start, own_relay, own_column, column_of_a, from_b, from_sib]

    def finish(self):
        p, full = self.p, self.full
        if not self.sent:
            return

        def sent(slot, view):
            remote(view, view, self.send.at[slot], self.recv.at[0], p.sib()).wait_send()

        sent(self.A, self.shards(full.shape[0] if self.way == 0 else 1))
        sent(self.B, self.shards(2) if self.way == 2 else full.at[:, p.c, 0:2])
        sent(self.SIB, full.at[:, p.c])
        for which in range(2 if self.way == 1 else 1):

            @pl.when(p.middle)
            def _(which=which):
                sent(self.Z + which, full.at[:, p.c] if self.way == 2 else self.shards(4))

            @pl.when(p.end)
            def _(which=which):
                sent(self.Z + which, full.at[0:2, p.c] if self.way == 2 else self.shards(2))

        self.sent = set()

    def step(self, i):
        self.steps()[i]()


class Scatter:
    def __init__(self, place, full, from_sib, from_b, from_a, from_z, out, send, recv, way):
        self.p, self.full, self.out, self.send, self.recv = place, full, out, send, recv
        self.from_sib, self.from_b, self.from_a, self.from_z = from_sib, from_b, from_a, from_z
        self.way = way
        self.sent = set()

    @staticmethod
    def semaphores(way):
        return (5, 8) if way == 1 else (4, 6)

    @staticmethod
    def landing(full, way):
        z, _, n, r, c = full
        if way == 2:
            return [(z, n, r, c), (2, 1, r, c), (1, r, c), (4, n, r, c)]
        if way == 1:
            return [(z, n, r, c), (2, z, r, c), (1, r, c), (8, r, c)]
        return [(z, n, r, c), (2, z, r, c), (z, r, c), (4, r, c)]

    SIB, A, B, Z, ZA = range(5)
    B1 = 3

    @staticmethod
    def sum_relay(which):
        return (4, 5) if which == 0 else (6, 7)

    def go(self, out, into, src, dst, target):
        remote(src, dst, self.send.at[out], self.recv.at[into], target).start()
        self.sent.add(out)

    def take(self, slot, view):
        remote(view, view, self.send.at[0], self.recv.at[slot], self.p.sib()).wait_recv()

    def add(self, n, part):
        c = self.p.c
        for z in range(self.full.shape[0]):
            self.full[z, c, n] = self.full[z, c, n] + part(z)


    def along(self, which, n):
        p = self.p
        total, relay = self.sum_relay(which)

        def send(z, target, land, into):
            self.go(self.Z + which, into, self.full.at[z, p.c, n], self.from_z.at[4 * which + land], p.chip(target))

        @pl.when(p.end)
        def _():
            send(p.z3, p.z1, 3, relay)
            send(p.z2, p.z2, 1, total)

        @pl.when(p.middle)
        def _():
            send(p.z3, p.z3, 2, total)

        send(p.z1, p.z1, 0, total)

    def relay(self, which, n):
        p = self.p
        total, relay = self.sum_relay(which)

        @pl.when(p.middle)
        def _():
            land = self.from_z.at[4 * which + 3]
            self.take(relay, land)
            self.full[p.z2, p.c, n] = self.full[p.z2, p.c, n] + self.from_z[4 * which + 3]
            view = self.full.at[p.z2, p.c, n]
            self.go(self.Z + which, total, view, self.from_z.at[4 * which + 1], p.chip(p.z2))

    def sum_along(self, which, n, put):
        p = self.p
        total, _ = self.sum_relay(which)
        first = 4 * which

        def add_up(count):
            self.take(total, self.from_z.at[first : first + count])
            x = self.full[p.z, p.c, n].astype(F32)
            for i in range(count):
                x = x + self.from_z[first + i].astype(F32)
            put(x)

        @pl.when(p.end)
        def _():
            add_up(2)

        @pl.when(p.middle)
        def _():
            add_up(3)

    def steps(self):
        p = self.p

        def start():
            self.go(self.SIB, self.SIB, self.full.at[:, 1 - p.c], self.from_sib, p.sib())

        def other_core():
            self.take(self.SIB, self.from_sib)
            for slot, half, n in ((self.B, 0, p.nab), (self.B1, 1, p.nb)):
                self.add(n, lambda z, n=n: self.from_sib[z, n])
                self.go(self.B, slot, self.full.at[:, p.c, n], self.from_b.at[half], p.b())
            for n in (p.na, p.n):
                self.add(n, lambda z, n=n: self.from_sib[z, n])

        def partner_b():
            self.take(self.B, self.from_b.at[0])
            self.add(p.na, lambda z: self.from_b[0, z])
            if self.way == 1:
                self.along(1, p.na)
            else:
                self.go(self.A, self.A, self.full.at[:, p.c, p.na], self.from_a, p.a())
            self.take(self.B1, self.from_b.at[1])
            self.add(p.n, lambda z: self.from_b[1, z])
            if self.way == 1:
                self.along(0, p.n)

        def partner_a():
            self.take(self.A, self.from_a)
            self.add(p.n, lambda z: self.from_a[z])
            self.along(0, p.n)

        def relay():
            self.relay(0, p.n)

        def store(x):
            self.out[...] = x

        def end():
            self.sum_along(0, p.n, store)

        def relay_both():
            self.relay(1, p.na)
            self.relay(0, p.n)

        def to_a():
            def put(x):
                self.full[p.z, p.c, p.na] = x.astype(self.full.dtype)

            self.sum_along(1, p.na, put)
            self.go(self.A, self.A, self.full.at[p.z, p.c, p.na], self.from_a.at[0], p.a())
            self.sum_along(0, p.n, store)

        def end_a():
            self.take(self.A, self.from_a.at[0])
            self.out[...] = self.out[...] + self.from_a[0].astype(F32)

        total, relayed = self.sum_relay(0)

        def row(z, target, land, into):
            self.go(self.Z, into, self.full.at[z, p.c], self.from_z.at[land], p.chip(target))

        def rows_along():
            self.take(self.SIB, self.from_sib)
            for n in range(self.full.shape[2]):
                self.add(n, lambda z, n=n: self.from_sib[z, n])

            @pl.when(p.end)
            def _():
                row(p.z3, p.z1, 3, relayed)
                row(p.z2, p.z2, 1, total)

            @pl.when(p.middle)
            def _():
                row(p.z3, p.z3, 2, total)

            row(p.z1, p.z1, 0, total)

        def row_relay():
            @pl.when(p.middle)
            def _():
                self.take(relayed, self.from_z.at[3])
                for n in range(self.full.shape[2]):
                    self.full[p.z2, p.c, n] = self.full[p.z2, p.c, n] + self.from_z[3, n]
                row(p.z2, p.z2, 1, total)

        def row_to_b():
            def add_up(count):
                self.take(total, self.from_z.at[0:count])
                for n in range(self.full.shape[2]):
                    x = self.full[p.z, p.c, n].astype(F32)
                    for i in range(count):
                        x = x + self.from_z[i, n].astype(F32)
                    self.full[p.z, p.c, n] = x.astype(self.full.dtype)

            @pl.when(p.end)
            def _():
                add_up(2)

            @pl.when(p.middle)
            def _():
                add_up(3)

            for slot, half, n in ((self.B, 0, p.nab), (self.B1, 1, p.nb)):
                self.go(self.B, slot, self.full.at[p.z, p.c, n], self.from_b.at[half, 0], p.b())

        def shard_to_a():
            self.take(self.B, self.from_b.at[0, 0])
            self.full[p.z, p.c, p.na] = self.full[p.z, p.c, p.na] + self.from_b[0, 0]
            self.go(self.A, self.A, self.full.at[p.z, p.c, p.na], self.from_a.at[0], p.a())
            self.take(self.B1, self.from_b.at[1, 0])
            self.out[...] = self.full[p.z, p.c, p.n].astype(F32) + self.from_b[1, 0].astype(F32)

        if self.way == 2:
            return [start, rows_along, row_relay, row_to_b, shard_to_a, end_a]
        if self.way == 1:
            return [start, other_core, partner_b, relay_both, to_a, end_a]
        return [start, other_core, partner_b, partner_a, relay, end]

    def finish(self):
        p, full = self.p, self.full
        if not self.sent:
            return
        one, all_z, some = full.at[p.z, p.c, p.n], full.at[:, p.c, p.n], full.at[0:3, p.c, p.n]
        views = {
            self.SIB: full.at[:, p.c],
            self.A: all_z if self.way == 0 else one,
            self.B: full.at[0:2, p.c, p.n] if self.way == 2 else full.at[:, p.c, 0:2],
            self.Z: full.at[0:3, p.c] if self.way == 2 else some,
            self.ZA: some,
        }
        for slot in sorted(self.sent):
            view = views[slot]
            remote(view, view, self.send.at[slot], self.recv.at[0], p.sib()).wait_send()
        self.sent = set()

    def step(self, i):
        self.steps()[i]()


def stats(x):
    centre = jnp.mean(x, axis=-1, keepdims=True)
    centred = x - centre
    spread = jnp.mean(centred * centred, axis=-1, keepdims=True)
    r = lax.rsqrt(spread + EPS)
    return centred * r, r


def norm_into(src, gain, dst, rows):
    total = src.shape[0]

    def body(i):
        at = ds(i * rows, rows)
        xn, _ = stats(src[at, :].astype(F32))
        dst[at, :] = (xn * gain).astype(BF)

    loop(total // rows, body)


def halves(shape):
    return lax.broadcasted_iota(jnp.int32, shape, 1) < shape[1] // 2


def split_heads(x):
    low = halves(x.shape)
    zero = jnp.zeros_like(x)
    return jnp.concatenate([jnp.where(low, x, zero), jnp.where(low, zero, x)], 0)


def head_ones(keys):
    shape = (2 * keys, LANES)
    row = lax.broadcasted_iota(jnp.int32, shape, 0) < keys
    low = lax.broadcasted_iota(jnp.int32, shape, 1) < LANES // 2
    return jnp.where(row == low, 1.0, 0.0).astype(BF)


def unroll(first, last, body):
    for i in range(first, last):
        body(i)


def spatial_forward(qkv, probs, att, patches, width, first, last):
    head = width // HEADS
    scale = head ** -0.5
    pairs = range(HEADS // 2)
    ones = head_ones(patches)

    def body(s):
        at = ds(s * patches, patches)
        parts = []
        for pair in pairs:
            lane = pair * 2 * head
            q = qkv[at, lane : lane + 2 * head]
            parts.append(dot(q, split_heads(qkv[at, width + lane : width + lane + 2 * head]), 1, 1))
        scores = jnp.concatenate(parts, 0) * scale
        low = halves(scores.shape)
        top0 = jnp.max(jnp.where(low, scores, -jnp.inf), axis=-1, keepdims=True)
        top1 = jnp.max(jnp.where(low, -jnp.inf, scores), axis=-1, keepdims=True)
        e = jnp.exp(scores - jnp.where(low, top0, top1))
        e_low = e.astype(BF)
        parts = []
        for pair in pairs:
            lane = pair * 2 * head
            v2 = split_heads(qkv[at, 2 * width + lane : 2 * width + lane + 2 * head])
            rows = slice(pair * patches, (pair + 1) * patches)
            parts.append(dot(e_low[rows], jnp.concatenate([v2, ones], 1), 1, 0))
        both = jnp.concatenate(parts, 0)
        r = 1.0 / both[:, 2 * head :]
        probs[s] = (e * r).astype(BF).reshape(HEADS // 2, patches, 2 * patches)
        new = (both[:, : 2 * head] * r).astype(BF)
        for pair in pairs:
            att[at, pair * 2 * head : (pair + 1) * 2 * head] = new[pair * patches : (pair + 1) * patches]

    unroll(first, last, body)


def pad_heads(x, lanes):
    low = halves(x.shape)
    zero = jnp.zeros_like(x)
    fill = jnp.zeros((lanes - x.shape[0], x.shape[1]), x.dtype)
    return jnp.concatenate([jnp.where(low, x, zero), fill, jnp.where(low, zero, x), fill], 0).astype(BF)


LANES = 128
SUB = 8


def temporal_forward(qkv, probs, att, bias, slots, width, first, last):
    head = width // HEADS
    scale = head ** -0.5
    group = slots * SUB
    pairs = range(HEADS // 2)
    parts_of = [slice(half * group, (half + 1) * group) for half in range(2)]

    def body(i):
        at = ds(i * 2 * group, 2 * group)
        parts = []
        for pair in pairs:
            lane = pair * 2 * head
            q = qkv[at, lane : lane + 2 * head].astype(F32)
            k = qkv[at, width + lane : width + lane + 2 * head].astype(F32)
            for rows in parts_of:
                x = dot(q[rows].astype(BF), pad_heads(k[rows], LANES), 1, 1)
                parts += [x[:, :LANES], x[:, LANES:]]
        scores = jnp.stack(parts, 0) * scale + bias[...][None]
        e = jnp.exp(scores - jnp.max(scores, axis=-1, keepdims=True))
        p = (e / jnp.sum(e, axis=-1, keepdims=True)).astype(BF)
        for pair in pairs:
            lane = pair * 2 * head
            v = qkv[at, 2 * width + lane : 2 * width + lane + 2 * head].astype(F32)
            out = []
            for half, rows in enumerate(parts_of):
                j = (pair * 2 + half) * 2
                both = jnp.concatenate([p[j], p[j + 1]], 1)
                probs[i * 2 + half, pair] = both
                out.append(dot(both, pad_heads(v[rows], LANES), 1, 0))
            att[at, lane : lane + 2 * head] = jnp.concatenate(out, 0).astype(BF)

    unroll(first, last, body)


def make_bias(bias, count, slots):
    group = slots * SUB
    q = lax.broadcasted_iota(jnp.int32, (group, LANES), 0)
    k = lax.broadcasted_iota(jnp.int32, (group, LANES), 1)
    sq, sk = q // SUB, k // SUB
    ok = (q - sq * SUB == k - sk * SUB) & (sk <= sq) & (sk < count)
    bias[...] = jnp.where(ok, 0.0, -1e9)


def gelu_pair(z):
    k0 = 0.7978845608028654
    k1 = k0 * 0.044715
    z2 = z * z
    half = 0.5 + 0.5 * jnp.tanh(z * (k0 + k1 * z2))
    active = z * half
    slope = half + half * (z - active) * (2.0 * k0 + 6.0 * k1 * z2)
    return active, slope


def wide_rows(ref, width, columns=None):
    x = ref[...] if columns is None else ref[:, :, :, :, columns]
    return x.reshape(width, x.shape[-1])


def unsplit_heads(x, second, rows):
    low = halves((rows, x.shape[1]))
    return jnp.where(low, x[:rows], x[second : second + rows])


def spatial_backward(qkv, probs, grad, patches, width, first, last):
    head = width // HEADS
    scale = head ** -0.5
    pairs = range(HEADS // 2)
    rows_of = [slice(pair * patches, (pair + 1) * patches) for pair in pairs]

    def body(s):
        at = ds(s * patches, patches)
        cols = [[slice(t * width + p * 2 * head, t * width + (p + 1) * 2 * head) for t in range(3)] for p in pairs]
        p_low = probs[s].reshape(HEADS // 2 * patches, 2 * patches)
        soft = p_low.astype(F32)
        q = [qkv[at, cols[p][0]] for p in pairs]
        k2 = [split_heads(qkv[at, cols[p][1]]) for p in pairs]
        g = [grad[at, p * 2 * head : (p + 1) * 2 * head] for p in pairs]
        gp = [dot(g[p], split_heads(qkv[at, cols[p][2]]), 1, 1) for p in pairs]
        gv = [dot(p_low[rows_of[p]], g[p], 0, 0) for p in pairs]
        gp = jnp.concatenate(gp, 0)
        low = halves(gp.shape)
        both = gp * soft
        sum0 = jnp.sum(jnp.where(low, both, 0.0), axis=-1, keepdims=True)
        sum1 = jnp.sum(jnp.where(low, 0.0, both), axis=-1, keepdims=True)
        gs = (soft * (gp - jnp.where(low, sum0, sum1))).astype(BF)
        gq = [dot(gs[rows_of[p]], k2[p], 1, 0) for p in pairs]
        gk = [dot(gs[rows_of[p]], q[p], 0, 0) for p in pairs]
        for p in pairs:
            qkv[at, cols[p][0]] = (gq[p] * scale).astype(BF)
            qkv[at, cols[p][1]] = (unsplit_heads(gk[p], patches, patches) * scale).astype(BF)
            qkv[at, cols[p][2]] = unsplit_heads(gv[p], patches, patches).astype(BF)

    unroll(first, last, body)


def temporal_backward(qkv, probs, grad, slots, width, first, last):
    head = width // HEADS
    scale = head ** -0.5
    group = slots * SUB
    pairs = range(HEADS // 2)
    parts_of = [slice(half * group, (half + 1) * group) for half in range(2)]

    def body(i):
        at = ds(i * 2 * group, 2 * group)
        cols = [[slice(t * width + p * 2 * head, t * width + (p + 1) * 2 * head) for t in range(3)] for p in pairs]
        qs, ks, gs_in, ps, gp, soft = [], [], [], [], [], []
        for pair in pairs:
            q, k, v = (qkv[at, c].astype(F32) for c in cols[pair])
            g = grad[at, pair * 2 * head : (pair + 1) * 2 * head].astype(F32)
            for half, rows in enumerate(parts_of):
                qs.append(q[rows].astype(BF))
                ks.append(pad_heads(k[rows], LANES))
                gs_in.append(g[rows].astype(BF))
                p = probs[i * 2 + half, pair]
                ps.append(p)
                x = dot(gs_in[-1], pad_heads(v[rows], LANES), 1, 1)
                wide = p.astype(F32)
                gp += [x[:, :LANES], x[:, LANES:]]
                soft += [wide[:, :LANES], wide[:, LANES:]]
        many = range(len(ps))
        gv = [unsplit_heads(dot(ps[j], gs_in[j], 0, 0), LANES, group) for j in many]
        gp = jnp.stack(gp, 0)
        soft = jnp.stack(soft, 0)
        delta = jnp.sum(gp * soft, axis=-1, keepdims=True)
        gs = (soft * (gp - delta)).astype(BF)
        gs = [jnp.concatenate([gs[2 * j], gs[2 * j + 1]], 1) for j in many]
        gq = [dot(gs[j], ks[j], 1, 0) * scale for j in many]
        gk = [unsplit_heads(dot(gs[j], qs[j], 0, 0), LANES, group) * scale for j in many]
        for pair in pairs:
            for c, outs in zip(cols[pair], (gq, gk, gv)):
                qkv[at, c] = jnp.concatenate(outs[2 * pair : 2 * pair + 2], 0).astype(BF)

    unroll(first, last, body)


def norm_back(src, grad, gain, base, dst, low, sums, rows):
    total, width = grad.shape
    sums[...] = jnp.zeros_like(sums)

    def body(i):
        at = ds(i * rows, rows)
        xn, r = stats(src[at, :].astype(F32))
        g = grad[at, :]
        e = g * gain
        inner = e - jnp.mean(e, axis=-1, keepdims=True) - xn * jnp.mean(e * xn, axis=-1, keepdims=True)
        res = base[at, :] + r * inner
        if dst is not None:
            dst[at, :] = res
        low[at, :] = res.astype(BF)
        sums[...] += jnp.sum((g * xn).reshape(rows // SUB, SUB, width), axis=0)

    loop(total // rows, body)


def gain_row(gains, which):
    return gains[which : which + 1, :]


class Sizes:
    def __init__(self, mesh, video, in_weight):
        self.depth = mesh.shape["wide"] // 2
        self.narrow = mesh.shape["narrow"]
        self.slots, self.patches, self.width = video.shape[1:]
        self.hidden = in_weight.shape[2]
        self.tokens = self.slots * self.patches
        self.group = self.slots * SUB
        devices = 2 * self.depth * self.narrow
        w = self.width // devices
        self.shards = {
            "qkv": (w, 3 * self.width),
            "out": (w, self.width),
            "in": (w, self.hidden),
            "down": (self.hidden // devices, self.width),
        }
        self.mesh_dims = (self.depth, 2, self.narrow)

    def full(self, name):
        return self.mesh_dims + (TILE_GAIN if name == "gain" else self.shards[name])

    def acts(self, b):
        t, w, f = self.tokens, self.width, self.hidden
        pairs = HEADS // 2
        if b == 0:
            probs = (self.slots, pairs, self.patches, 2 * self.patches)
        else:
            probs = (self.patches // SUB, pairs, self.group, 2 * LANES)
        return {
            "normed": ((t, w), BF),
            "qkv": ((t, 3 * w), BF),
            "probs": (probs, BF),
            "att": ((t, w), BF),
            "middle": ((t, w), F32),
            "mlp": ((t, w), BF),
            "active": ((t, f), BF),
            "slope": ((t, f), BF),
        }


TILE_GAIN = (16, LANES)
NAMES = ("qkv", "out", "in", "down")
ACTS = ("normed", "qkv", "probs", "att", "middle", "mlp", "active", "slope")
SPLIT = {"gain": 1, "qkv": 2, "out": 1, "in": 2, "down": 2}


def pieces_of(name, b):
    return [(name, b, i) for i in range(SPLIT[name])]


GAIN = ("gain", 0)
GATHER_ORDER = [(*GAIN, 0)] + [piece for b in range(2) for name in NAMES for piece in pieces_of(name, b)]
SCATTER_ORDER = [
    piece for b in (1, 0) for name in ("down", "in", "out", "qkv") for piece in pieces_of(name, b)
] + [(*GAIN, 0)]


def columns_of(piece, columns):
    name, _, i = piece
    part = columns // SPLIT[name]
    return slice(i * part, (i + 1) * part)


def row_tile(tokens):
    return tokens // 2 if tokens % 32 == 0 else tokens


def keys_of_weights():
    return [(name, b) for b in range(2) for name in NAMES]


KEPT = ("normed", "qkv", "att", "middle", "mlp", "active", "slope")


def layer_kernel(sz, *refs):
    refs = list(refs)

    def grab(n):
        taken, refs[:n] = refs[:n], []
        return taken

    video, cotangent, frames, attn_gain, mlp_gain = grab(5)
    shard = dict(zip(NAMES, grab(4)))
    out, grad_video = grab(2)
    outs = dict(zip(NAMES, grab(4)))
    gain_outs = grab(2)
    acts_hbm = dict(zip(KEPT, grab(len(KEPT))))
    acts = dict(zip(ACTS, grab(8)))
    probs1, h1 = grab(2)
    full = dict(zip([GAIN] + keys_of_weights(), grab(9)))
    grads = dict(zip([(name, 1) for name in NAMES] + [GAIN], grab(5)))
    landing = {piece: grab(4) for piece in SCATTER_ORDER}
    gains, bias, gain_out, grad, grad_mid, grad_norm, low, grad_att, sums = grab(9)
    gather_send, gather_recv, scatter_send, scatter_recv, local = grab(5)
    assert not refs
    for name in NAMES:
        grads[(name, 0)] = full[(name, 1)]

    place = Place()
    met = place.greet()

    def part_of(ref, piece, columns):
        if SPLIT[piece[0]] == 1:
            return ref
        return ref.at[(slice(None),) * (len(ref.shape) - 1) + (columns_of(piece, columns),)]

    gathers = {}
    at_send = at_recv = 0
    for k, piece in enumerate(GATHER_ORDER):
        n_send, n_recv = Gather.semaphores(GATHER_WAYS[k])
        ref = full[piece[:2]]
        sems = [gather_send.at[at_send : at_send + n_send], gather_recv.at[at_recv : at_recv + n_recv]]
        gathers[piece] = Gather(place, part_of(ref, piece, ref.shape[-1]), *sems, GATHER_WAYS[k])
        at_send += n_send
        at_recv += n_recv
    scatters = {}
    at_send = at_recv = 0
    for k, piece in enumerate(SCATTER_ORDER):
        n_send, n_recv = Scatter.semaphores(SCATTER_WAYS[k])
        ref = grads[piece[:2]]
        columns = ref.shape[-1]
        target = gain_out if piece[:2] == GAIN else outs[piece[0]].at[piece[1]]
        sems = [scatter_send.at[at_send : at_send + n_send], scatter_recv.at[at_recv : at_recv + n_recv]]
        scatters[piece] = Scatter(
            place,
            part_of(ref, piece, columns),
            *landing[piece],
            part_of(target, piece, columns),
            *sems,
            SCATTER_WAYS[k],
        )
        at_send += n_send
        at_recv += n_recv
    own = (place.z, place.c, place.n)
    full[GAIN][own] = place_gains(attn_gain, mlp_gain, place.w * sz.narrow + place.n)
    for key in keys_of_weights():
        full[key][own] = shard[key[0]][key[1]].astype(BF)
    place.met(met)

    moving = {}

    def move(name, src, dst):
        copy = pltpu.make_async_copy(src, dst, local.at[KEPT.index(name)])
        copy.start()
        moving[name] = copy

    def settle(*names):
        for name in names:
            if name in moving:
                moving.pop(name).wait()

    def act(name, b):
        return probs1 if (name, b) == ("probs", 1) else acts[name]

    def keep(b, *names):
        for name in names:
            if b == 0 and name in KEPT:
                move(name, acts[name], acts_hbm[name])

    def fetch(b, *names):
        for name in names:
            if b == 1 and name in KEPT:
                settle(name)
                move(name, acts_hbm[name], acts[name])

    count = (frames[0] + 1) // 2
    t, w = sz.tokens, sz.width

    def stage_gain():
        make_bias(bias, count, sz.slots)
        tile = jnp.sum(full[GAIN][...].astype(F32).reshape(-1, 16, LANES), axis=0)
        for g in range(4):
            rows = [tile[g * 4 + r : g * 4 + r + 1, :] for r in range(w // LANES)]
            gains[g : g + 1, :] = jnp.concatenate(rows, 1)

    def forward_stages(b):
        a = {name: act(name, b) for name in ACTS}
        h = video if b == 0 else h1

        def norm1():
            settle("normed")
            norm_into(h, gain_row(gains, 2 * b), a["normed"], row_tile(t))
            keep(b, "normed")

        def qkv(first, last):
            settle("qkv")
            at = slice(first, last)
            a["qkv"][:, at] = dot(a["normed"][...], wide_rows(full[("qkv", b)], w, at), 1, 0).astype(BF)
            if last == 3 * w:
                keep(b, "qkv")

        def attend(first, last):
            settle("att")
            if b == 0:
                spatial_forward(a["qkv"], a["probs"], a["att"], sz.patches, w, first, last)
                end = sz.slots
            else:
                temporal_forward(a["qkv"], a["probs"], a["att"], bias, sz.slots, w, first, last)
                end = sz.patches // (2 * SUB)
            if last == end:
                keep(b, "probs", "att")

        def project():
            settle("middle")
            new = dot(a["att"][...], wide_rows(full[("out", b)], w), 1, 0)
            a["middle"][...] = h[...].astype(F32) + new
            keep(b, "middle")

        def norm2():
            settle("mlp")
            norm_into(a["middle"], gain_row(gains, 2 * b + 1), a["mlp"], row_tile(t))
            keep(b, "mlp")

        def expand(first, last):
            at = slice(first, last)
            settle("active", "slope")
            weight = wide_rows(full[("in", b)], w, at)
            rows = row_tile(t)
            for r in range(0, t, rows):
                active, slope = gelu_pair(dot(a["mlp"][r : r + rows, :], weight, 1, 0))
                a["active"][r : r + rows, at] = active.astype(BF)
                a["slope"][r : r + rows, at] = slope.astype(BF)
            if last == sz.hidden:
                keep(b, "active", "slope")

        def contract(first, last):
            at = slice(first, last)
            new = a["middle"][:, at] + dot(a["active"][...], wide_rows(full[("down", b)], sz.hidden, at), 1, 0)
            if b == 0:
                new = new.reshape(sz.slots, sz.patches // SUB, SUB, last - first)
                for s in range(sz.slots):
                    h1_view[:, s * SUB : (s + 1) * SUB, at] = new[s]
            else:
                valid = lax.broadcasted_iota(jnp.int32, (sz.slots, 1, 1), 0) < count
                new = new.reshape(sz.patches // (2 * SUB), 2, sz.slots, SUB, last - first)
                for i in range(sz.patches // (2 * SUB)):
                    rows = jnp.concatenate([new[i, 0], new[i, 1]], axis=1)
                    out[:, i * 2 * SUB : (i + 1) * 2 * SUB, at] = jnp.where(valid, rows, 0.0).astype(BF)
                if last == w:
                    fetch(b, "active", "middle")

        n_a = sz.slots if b == 0 else sz.patches // (2 * SUB)
        cuts = [-(-n_a * i // 4) for i in range(5)]
        todo = [norm1]
        todo += [functools.partial(qkv, 3 * w * i // 2, 3 * w * (i + 1) // 2) for i in range(2)]
        todo += [functools.partial(attend, cuts[i], cuts[i + 1]) for i in range(4)]
        todo += [project, norm2]
        todo += [functools.partial(expand, sz.hidden * i // 4, sz.hidden * (i + 1) // 4) for i in range(4)]
        last = [functools.partial(contract, w * i // 2, w * (i + 1) // 2) for i in range(2)]
        return todo, last

    h1_view = h1.reshape(sz.patches // SUB, sz.group, w)

    def start():
        valid = lax.broadcasted_iota(jnp.int32, (sz.slots, 1, 1), 0) < count

        def body(i):
            rows = cotangent[:, ds(i * 2 * SUB, 2 * SUB), :].astype(F32)
            rows = jnp.where(valid, rows, 0.0)
            both = [rows[:, half * SUB : (half + 1) * SUB, :].reshape(sz.group, w) for half in range(2)]
            rows = jnp.concatenate(both, 0)
            at = ds(i * 2 * sz.group, 2 * sz.group)
            grad[at, :] = rows
            low[at, :] = rows.astype(BF)

        loop(sz.patches // (2 * SUB), body)

    def put_gain(which):
        row = jnp.sum(sums[...], axis=0, keepdims=True)
        per = w // LANES
        tile = jnp.concatenate([row[:, r * LANES : (r + 1) * LANES] for r in range(per)], 0)
        gain_rows[which * per : (which + 1) * per, :] = tile

    gain_rows = gain_out

    def backward_stages(b):
        a = {name: act(name, b) for name in ACTS}

        half = sz.hidden // 2
        z_half = sz.depth // 2

        def down_grad(i):
            settle("active")
            if b == 0 and i == 0:
                for gather in gathers.values():
                    gather.finish()
            at = slice(i * w // 2, (i + 1) * w // 2)
            g = dot(a["active"][...], low[:, at], 0, 0).astype(BF)
            grads[("down", b)][:, :, :, :, at] = g.reshape(sz.full("down")[:-1] + (w // 2,))

        def hidden_back(i):
            settle("slope")
            at = slice(i * half, (i + 1) * half)
            weight = full[("down", b)][i * z_half : (i + 1) * z_half].reshape(half, w)
            a["slope"][:, at] = (dot(low[...], weight, 1, 1) * a["slope"][:, at].astype(F32)).astype(BF)

        def in_grad(i):
            settle("mlp")
            at = slice(i * half, (i + 1) * half)
            g = dot(a["mlp"][...], a["slope"][:, at], 0, 0).astype(BF)
            grads[("in", b)][:, :, :, :, at] = g.reshape(sz.full("in")[:-1] + (half,))
            if i == 1:
                fetch(b, "mlp")

        def back_rows(src, weight, put):
            put(dot(src[...], wide_rows(weight, w), 1, 1))

        def mlp_back():

            def put(x):
                grad_norm[...] = x

            back_rows(a["slope"], full[("in", b)], put)
            fetch(b, "slope")

        def norm2_back():
            settle("middle")
            norm_back(a["middle"], grad_norm, gain_row(gains, 2 * b + 1), grad, grad_mid, low, sums, row_tile(t))
            put_gain(2 * b + 1)

        def out_grad():
            settle("att")

            g = dot(a["att"][...], low[...], 0, 0).astype(BF)
            grads[("out", b)][...] = g.reshape(sz.full("out"))
            fetch(b, "att")

        def att_back():

            def put(x):
                grad_att[...] = x.astype(BF)

            back_rows(low, full[("out", b)], put)

        def attend(first, last):
            settle("qkv", "probs")
            if b == 0:
                spatial_backward(a["qkv"], a["probs"], grad_att, sz.patches, w, first, last)
            else:
                temporal_backward(a["qkv"], a["probs"], grad_att, sz.slots, w, first, last)

        def qkv_grad(first, last):
            settle("normed")
            at = slice(first, last)
            g = dot(a["normed"][...], a["qkv"][:, at], 0, 0).astype(BF)
            grads[("qkv", b)][:, :, :, :, at] = g.reshape(sz.full("qkv")[:-1] + (last - first,))
            if last == 3 * w:
                fetch(b, "normed")

        def qkv_back():

            def put(x):
                grad_norm[...] = x

            back_rows(a["qkv"], full[("qkv", b)], put)
            fetch(b, "qkv")

        def norm1_back():
            src = h1 if b == 1 else video
            if b == 1:
                norm_back(src, grad_norm, gain_row(gains, 2), grad_mid, grad, low, sums, row_tile(t))
            else:
                norm_back(src, grad_norm, gain_row(gains, 0), grad_mid, None, low, sums, row_tile(t))
                grad_video[...] = low[...].reshape(grad_video.shape)
            put_gain(2 * b)

        def reorder():
            view = grad.reshape(sz.patches // SUB, sz.group, w)

            def body(s):
                rows = view[:, ds(s * SUB, SUB), :].reshape(sz.patches, w)
                at = ds(s * sz.patches, sz.patches)
                grad_norm[at, :] = rows
                low[at, :] = rows.astype(BF)

            loop(sz.slots, body)
            grad[...] = grad_norm[...]

        n_a = sz.slots if b == 0 else sz.patches // (2 * SUB)
        cuts = [-(-n_a * i // 4) for i in range(5)]
        todo = []
        for piece in (down_grad, hidden_back, in_grad):
            todo += [functools.partial(piece, i) for i in range(2)]
        todo += [mlp_back, norm2_back, out_grad, att_back]
        todo += [functools.partial(attend, cuts[i], cuts[i + 1]) for i in range(4)]
        todo += [functools.partial(qkv_grad, 3 * w * i // 2, 3 * w * (i + 1) // 2) for i in range(2)]
        if b == 1:
            todo += output
        todo += [qkv_back, norm1_back]
        if b == 1:
            todo += [reorder]
        return todo

    def spread_gain():
        tile = gain_out[...]
        grads[GAIN][...] = jnp.broadcast_to(tile, sz.full("gain"))

    first, last = forward_stages(0)
    second, output = forward_stages(1)
    work = [start, stage_gain] + first + last + second
    work = iter(work + backward_stages(1) + backward_stages(0) + [spread_gain])
    steps = [gathers[piece] for piece in GATHER_ORDER] + [scatters[piece] for piece in SCATTER_ORDER]
    for op in PLAN:
        if op < 0:
            next(work)()
        else:
            steps[op // 8].step(op % 8)
    assert next(work, None) is None
    pick_gains(gain_out[...], gain_outs, place.w * sz.narrow + place.n)
    settle(*KEPT)
    for scatter in scatters.values():
        scatter.finish()


def place_gains(attn_gain, mlp_gain, index):
    own = attn_gain.shape[1]
    per = LANES // own
    row = lax.broadcasted_iota(jnp.int32, (TILE_GAIN[0] // 4, LANES), 0)
    lane = lax.broadcasted_iota(jnp.int32, (TILE_GAIN[0] // 4, LANES), 1) // own
    here = row * per + lane == index
    tiles = []
    for b in range(2):
        for ref in (attn_gain, mlp_gain):
            values = jnp.concatenate([ref[b : b + 1, :]] * per, 1)
            tiles.append(jnp.where(here, values, 0.0))
    return jnp.concatenate(tiles, 0).astype(BF)


def pick_gains(tile, outs, index):
    attn, mlp = outs
    own = mlp.shape[-1]
    per = LANES // own
    rows = TILE_GAIN[0] // 4
    row = lax.broadcasted_iota(jnp.int32, (rows, own), 0)
    for b in range(2):
        for kind in range(2):
            first = (2 * b + kind) * rows
            total = jnp.zeros((rows, own), F32)
            for j in range(per):
                piece = tile[first : first + rows, j * own : (j + 1) * own]
                total = total + jnp.where(row * per + j == index, piece, 0.0)
            if kind == 1:
                mlp[b : b + 1, :] = jnp.sum(total, axis=0, keepdims=True)
            else:
                for part in range(2):
                    half = total[part * rows // 2 : (part + 1) * rows // 2]
                    attn[part, b : b + 1, :] = jnp.sum(half, axis=0, keepdims=True)


PLAN = (
    112, 8, 48, 0, 24, 16, 1, 9, 64, 40, 104, 17, 88, 113, 49, 2, 10, 41, 25, 32, 72, 80, 18, 65, 3, 33, 96,
    26, 56, 11, 19, -1, 27, 57, 73, 81, 4, 42, 50, 34, 12, 5, -1, -1, 13, -1, 20, 21, -1, 58, 28, -1, 35, 89,
    97, 74, 51, -1, 66, -1, 43, 59, -1, 29, -1, -1, 75, 82, 90, 36, 37, -1, -1, 67, 44, 52, 98, 45, -1, 105,
    -1, 60, 83, 114, 91, 53, -1, 61, -1, 68, 99, 106, 76, -1, 69, -1, 77, -1, -1, -1, 84, -1, -1, 92, 115,
    107, 85, -1, -1, 100, 93, -1, -1, 101, -1, -1, 108, 116, -1, 120, -1, 128, 109, 117, -1, -1, 129, 121,
    -1, 136, -1, 144, -1, -1, -1, 152, 145, -1, -1, 153, -1, -1, 137, 130, 122, -1, -1, 160, -1, 168, 146,
    -1, 161, -1, -1, 169, -1, -1, 138, -1, 176, 154, 162, -1, 184, 123, 147, 177, -1, -1, -1, 192, 185, 139,
    -1, 200, -1, 193, 178, -1, 124, 201, -1, 208, 163, -1, 170, -1, 209, -1, 179, 186, -1, -1, -1, 216, 194,
    202, -1, 224, 217, 140, -1, -1, 187, 225, -1, 232, 203, 233, 188, 148, 210, 218, 226, 234, 131, 155, 171,
    195, 211, 219, 227, 235, 132, 156, 164, 172, 180, 196, 204, 212, 220, 228, 236, 125, 133, 141, 149, 157,
    165, 173, 181, 189, 197, 205, 213, 221, 229, 237,
)
GATHER_WAYS = (
    0, 0, 0, 0, 0, 0, 2, 0, 2, 0, 0, 0, 0, 0, 2,
)
SCATTER_WAYS = (
    0, 2, 0, 1, 2, 0, 2, 1, 0, 1, 0, 0, 1, 0, 0,
)


def copy_kernel(count, *refs):
    sems = refs[-1]
    refs = refs[:-1]
    down = [pltpu.make_async_copy(refs[i], refs[2 * count + i], sems.at[i]) for i in range(count)]
    up = [pltpu.make_async_copy(refs[2 * count + i], refs[count + i], sems.at[i]) for i in range(count)]
    for copy in down:
        copy.start()
    for i in range(count):
        down[i].wait()
        up[i].start()
    for copy in up:
        copy.wait()


def by_kernels(mesh, sz):
    vmem = pl.BlockSpec(memory_space=pltpu.VMEM)
    smem = pl.BlockSpec(memory_space=pltpu.SMEM)
    anyw = pl.BlockSpec(memory_space=pl.ANY)
    shape = jax.ShapeDtypeStruct
    t, w = sz.tokens, sz.width
    acts0 = sz.acts(0)
    clip_shape = shape((sz.slots, sz.patches, w), BF)
    dma = pltpu.SemaphoreType.DMA

    def landing(k, piece):
        full = sz.full(piece[0])
        full = full[:-1] + (full[-1] // SPLIT[piece[0]],)
        kind = F32 if piece[0] == "gain" else BF
        return [pltpu.VMEM(s, kind) for s in Scatter.landing(full, SCATTER_WAYS[k])]

    def run(video, frames, cotangent, qkv_weight, out_weight, in_weight, down_weight, attn_gain, mlp_gain):
        gain_shape = shape(attn_gain.shape, F32)
        shapes = [clip_shape, clip_shape]
        shapes += [shape((2,) + sz.shards[name], F32) for name in NAMES]
        shapes += [shape((2,) + attn_gain.shape, F32), gain_shape]
        n_gather = [sum(Gather.semaphores(way)[i] for way in GATHER_WAYS) for i in range(2)]
        n_scatter = [sum(Scatter.semaphores(way)[i] for way in SCATTER_WAYS) for i in range(2)]
        res = pl.pallas_call(
            functools.partial(layer_kernel, sz),
            out_shape=shapes + [shape(*acts0[name]) for name in KEPT],
            in_specs=[vmem, vmem, smem] + [vmem] * 6,
            out_specs=[vmem] * len(shapes) + [anyw] * len(KEPT),
            scratch_shapes=[pltpu.VMEM(*acts0[name]) for name in ACTS]
            + [pltpu.VMEM(*sz.acts(1)["probs"]), pltpu.VMEM((t, w), F32)]
            + [pltpu.VMEM(sz.full(name), BF) for name, _ in [GAIN] + keys_of_weights()]
            + [pltpu.VMEM(sz.full(name), BF) for name in NAMES]
            + [pltpu.VMEM(sz.full("gain"), F32)]
            + [buffer for k, piece in enumerate(SCATTER_ORDER) for buffer in landing(k, piece)]
            + [
                pltpu.VMEM((4, w), F32),
                pltpu.VMEM((sz.group, LANES), F32),
                pltpu.VMEM(TILE_GAIN, F32),
                pltpu.VMEM((t, w), F32),
                pltpu.VMEM((t, w), F32),
                pltpu.VMEM((t, w), F32),
                pltpu.VMEM((t, w), BF),
                pltpu.VMEM((t, w), BF),
                pltpu.VMEM((SUB, w), F32),
                dma((n_gather[0],)),
                dma((n_gather[1],)),
                dma((n_scatter[0],)),
                dma((n_scatter[1],)),
                dma((len(KEPT),)),
            ],
            compiler_params=pltpu.CompilerParams(
                collective_id=0, has_side_effects=True, vmem_limit_bytes=VMEM_LIMIT
            ),
        )(
            video.reshape(t, w),
            cotangent.reshape(clip_shape.shape),
            frames,
            attn_gain,
            mlp_gain,
            qkv_weight,
            out_weight,
            in_weight,
            down_weight,
        )
        res = list(res)[: len(shapes)]
        res = pl.pallas_call(
            functools.partial(copy_kernel, len(res)),
            out_shape=shapes,
            in_specs=[anyw] * len(res),
            out_specs=[anyw] * len(res),
            scratch_shapes=[pltpu.VMEM(x.shape, x.dtype) for x in shapes] + [dma((len(res),))],
        )(*res)
        grad_attn = res[-2][0] + res[-2][1]
        return (res[0].reshape(video.shape), res[1].reshape(video.shape), *res[2:-2], grad_attn, res[-1])

    return run


def norm_rows(inputs, scaling):
    centre = jnp.mean(inputs, axis=-1, keepdims=True)
    centred = inputs - centre
    spread = jnp.mean(centred * centred, axis=-1, keepdims=True)
    return centred * lax.rsqrt(spread + EPS) * scaling


def project(rows_in, matrix):
    return jnp.einsum("cspd,de->cspe", rows_in, matrix, preferred_element_type=jnp.float32)


def project_back(rows_in, matrix):
    return jnp.einsum("cspe,de->cspd", rows_in, matrix, preferred_element_type=jnp.float32)


def weight_grad(left, right):
    return jnp.einsum("cspd,cspe->de", left, right, preferred_element_type=jnp.float32)


def pair_scores(first, second, which_block):
    if which_block == 0:
        return jnp.einsum("csphe,csqhe->cshpq", first, second, preferred_element_type=jnp.float32)
    return jnp.einsum("csphe,ctphe->cphst", first, second, preferred_element_type=jnp.float32)


def pair_mix(weighting, second, which_block):
    if which_block == 0:
        return jnp.einsum(
            "cshpq,csqhe->csphe", weighting, second, preferred_element_type=jnp.float32
        )
    return jnp.einsum("cphst,ctphe->csphe", weighting, second, preferred_element_type=jnp.float32)


def pair_back(weighting, first, which_block):
    if which_block == 0:
        return jnp.einsum(
            "cshpq,csphe->csqhe", weighting, first, preferred_element_type=jnp.float32
        )
    return jnp.einsum("cphst,csphe->ctphe", weighting, first, preferred_element_type=jnp.float32)


def masked_scores(queries, key_rows, which_block, allowed):
    head_size = queries.shape[-1]
    scores = pair_scores(queries, key_rows, which_block) * head_size ** (-0.5)
    if which_block == 1:
        scores = jnp.where(allowed[:, None, None], scores, -1000000000.0)
    return scores


def block_forward(inputs, weights, which_block, allowed):
    qkv_matrix, out_matrix, in_matrix, down_matrix, attn_scaling, mlp_scaling = weights
    full_shape = inputs.shape
    head_size = full_shape[-1] // HEADS
    normed, norm_pull = jax.vjp(norm_rows, inputs, attn_scaling.astype(jnp.float32))
    normed_low = normed.astype(jnp.bfloat16)
    qkv_rows = project(normed_low, qkv_matrix).astype(jnp.bfloat16)
    split = qkv_rows.reshape(full_shape[:3] + (3, HEADS, head_size))
    queries = split[:, :, :, 0]
    key_rows = split[:, :, :, 1]
    value_rows = split[:, :, :, 2]
    scores = masked_scores(queries, key_rows, which_block, allowed)
    row_max = jnp.max(scores, axis=-1, keepdims=True)
    shifted = jnp.exp(scores - row_max)
    row_sum = jnp.sum(shifted, axis=-1, keepdims=True)
    log_total = row_max + jnp.log(row_sum)
    probs_low = (shifted / row_sum).astype(jnp.bfloat16)
    attended = pair_mix(probs_low, value_rows, which_block).reshape(full_shape).astype(jnp.bfloat16)
    middle = inputs + project(attended, out_matrix)
    normed_mlp, mlp_pull = jax.vjp(norm_rows, middle, mlp_scaling.astype(jnp.float32))
    normed_mlp_low = normed_mlp.astype(jnp.bfloat16)
    hidden = project(normed_mlp_low, in_matrix)
    active, gelu_pull = jax.vjp(jax.nn.gelu, hidden)
    active_low = active.astype(jnp.bfloat16)
    result = middle + project(active_low, down_matrix)
    stored = (
        norm_pull,
        normed_low,
        queries,
        key_rows,
        value_rows,
        log_total,
        attended,
        mlp_pull,
        normed_mlp_low,
        gelu_pull,
        active_low,
    )
    return (result, stored)


def block_backward(gradient, stored, weights, which_block, allowed):
    qkv_matrix, out_matrix, in_matrix, down_matrix, attn_scaling, mlp_scaling = weights
    (
        norm_pull,
        normed_low,
        queries,
        key_rows,
        value_rows,
        log_total,
        attended,
        mlp_pull,
        normed_mlp_low,
        gelu_pull,
        active_low,
    ) = stored
    full_shape = gradient.shape
    head_size = queries.shape[-1]
    result_low = gradient.astype(jnp.bfloat16)
    grad_down_w = weight_grad(active_low, result_low)
    grad_active = project_back(result_low, down_matrix)
    grad_hidden = gelu_pull(grad_active)[0].astype(jnp.bfloat16)
    grad_in_w = weight_grad(normed_mlp_low, grad_hidden)
    grad_normed_mlp = project_back(grad_hidden, in_matrix)
    middle_part, grad_mlp_scaling = mlp_pull(grad_normed_mlp)
    grad_middle = gradient + middle_part
    middle_low = grad_middle.astype(jnp.bfloat16)
    grad_out_w = weight_grad(attended, middle_low)
    grad_attended = project_back(middle_low, out_matrix).astype(jnp.bfloat16)
    grad_attended = grad_attended.reshape(queries.shape)
    scores = masked_scores(queries, key_rows, which_block, allowed)
    soft_probs = jnp.exp(scores - log_total)
    grad_probs = pair_scores(grad_attended, value_rows, which_block)
    row_delta = jnp.sum(grad_probs * soft_probs, axis=-1, keepdims=True)
    grad_scores = (soft_probs * (grad_probs - row_delta)).astype(jnp.bfloat16)
    score_scale = head_size ** (-0.5)
    grad_queries = pair_mix(grad_scores, key_rows, which_block) * score_scale
    grad_keys = pair_back(grad_scores, queries, which_block) * score_scale
    grad_values = pair_back(soft_probs.astype(jnp.bfloat16), grad_attended, which_block)
    grad_qkv_rows = jnp.stack([grad_queries, grad_keys, grad_values], axis=3).astype(jnp.bfloat16)
    grad_qkv_rows = grad_qkv_rows.reshape(full_shape[:3] + (3 * full_shape[-1],))
    grad_qkv_w = weight_grad(normed_low, grad_qkv_rows)
    grad_normed = project_back(grad_qkv_rows, qkv_matrix)
    input_part, grad_attn_scaling = norm_pull(grad_normed)
    grad_input = grad_middle + input_part
    return (
        grad_input,
        (grad_qkv_w, grad_out_w, grad_in_w, grad_down_w, grad_attn_scaling, grad_mlp_scaling),
    )


def block_shards(qkv_weight, out_weight, in_weight, down_weight, attn_gain, mlp_gain, block_index):
    return (
        qkv_weight[block_index].astype(jnp.bfloat16),
        out_weight[block_index].astype(jnp.bfloat16),
        in_weight[block_index].astype(jnp.bfloat16),
        down_weight[block_index].astype(jnp.bfloat16),
        attn_gain[block_index].astype(jnp.bfloat16),
        mlp_gain[block_index].astype(jnp.bfloat16),
    )


def by_einsums(
    video, frames, cotangent, qkv_weight, out_weight, in_weight, down_weight, attn_gain, mlp_gain
):
    axes = ("wide", "narrow")
    slot_counts = (frames + 1) // 2
    positions = jnp.arange(video.shape[1], dtype=jnp.int32)
    allowed = (positions[None, None, :] <= positions[None, :, None]) & (
        positions[None, None, :] < slot_counts[:, None, None]
    )
    valid_slot = (positions[None, :] < slot_counts[:, None]).astype(jnp.float32)[:, :, None, None]
    weights = (qkv_weight, out_weight, in_weight, down_weight, attn_gain, mlp_gain)
    full = [
        tuple(lax.all_gather(part, axes, axis=0, tiled=True) for part in block_shards(*weights, b))
        for b in range(2)
    ]
    spatial_out, spatial_stored = block_forward(video.astype(jnp.float32), full[0], 0, allowed)
    temporal_out, temporal_stored = block_forward(spatial_out, full[1], 1, allowed)
    output = (temporal_out * valid_slot).astype(jnp.bfloat16)
    gradient = cotangent.astype(jnp.float32) * valid_slot
    grad_between, temporal_grads = block_backward(gradient, temporal_stored, full[1], 1, allowed)
    grad_start, spatial_grads = block_backward(grad_between, spatial_stored, full[0], 0, allowed)
    summed = [
        lax.psum_scatter(jnp.stack(pair), axes, scatter_dimension=1, tiled=True)
        for pair in zip(spatial_grads, temporal_grads)
    ]
    return (output, grad_start.astype(jnp.bfloat16), *summed)


def solution(mesh):
    both = ("wide", "narrow")
    clips = P(both, None, None, None)
    rows = P(None, both, None)
    in_specs = (clips, P(both), clips, rows, rows, rows, rows, P(None, both), P(None, both))
    out_specs = (clips, clips, rows, rows, rows, rows, P(None, both), P(None, both))

    def shards(*args):
        sz = Sizes(mesh, args[0], args[5])
        whole_tiles = all(rows % 16 == 0 for rows, _ in sz.shards.values())
        if whole_tiles and sz.depth == 4 and sz.narrow == 4 and args[0].shape[0] == 1:
            return by_kernels(mesh, sz)(*args)
        return by_einsums(*args)

    return jax.shard_map(shards, mesh=mesh, in_specs=in_specs, out_specs=out_specs, check_vma=False)
```

```python
import functools

import jax
import jax.numpy as jnp
from jax import lax
from jax.experimental import pallas as pl
from jax.experimental.pallas import tpu as pltpu
from jax.sharding import PartitionSpec as P

HEADS = 8
EPS = 1e-05
BF = jnp.bfloat16
F32 = jnp.float32
MESH = pl.DeviceIdType.MESH
VMEM_LIMIT = 62 * 2**20


def dot(a, b, ca, cb):
    return lax.dot_general(a, b, (((ca,), (cb,)), ((), ())), preferred_element_type=F32)


def ds(start, size):
    if isinstance(start, int):
        return pl.ds(start, size)
    return pl.ds(pl.multiple_of(start, size), size)


def loop(count, body, first=0):
    if count - first == 1:
        body(first)
        return

    def step(i, carry):
        body(i)
        return carry

    lax.fori_loop(first, count, step, 0)


class Place:
    def __init__(self):
        self.w = lax.axis_index("wide")
        self.n = lax.axis_index("narrow")
        self.z = self.w // 2
        self.c = self.w % 2
        first = 1 + self.c
        self.na = self.flip(self.n, first)
        self.nb = self.flip(self.n, 3 - first)
        self.nab = 3 - self.n
        self.z1 = self.flip(self.z, 1)
        self.z2 = self.flip(self.z, 2)
        self.z3 = 3 - self.z
        self.others = (self.z1, self.z2, self.z3)
        self.end = (self.z == 0) | (self.z == 3)
        self.middle = (self.z == 1) | (self.z == 2)

    @staticmethod
    def flip(n, step):
        bit = (n // step) % 2
        return n + step - 2 * step * bit

    def sib(self):
        return (self.z * 2 + 1 - self.c, self.n)

    def a(self):
        return (self.w, self.na)

    def b(self):
        return (self.w, self.nb)

    def chip(self, z):
        return (z * 2 + self.c, self.n)

    def greet(self):
        targets = [self.sib(), self.a(), self.b()] + [self.chip(z) for z in self.others]
        for t in targets:
            pl.semaphore_signal(pltpu.get_barrier_semaphore(), inc=1, device_id=t, device_id_type=MESH)
        return len(targets)

    def met(self, count):
        pl.semaphore_wait(pltpu.get_barrier_semaphore(), count)


def remote(src, dst, send, recv, target):
    return pltpu.make_async_remote_copy(src, dst, send, recv, device_id=target, device_id_type=MESH)


class Gather:
    def __init__(self, place, full, send, recv, way):
        self.p, self.full, self.send, self.recv, self.way = place, full, send, recv, way
        self.sent = set()

    A, B, SIB, Z, ZA = range(5)
    @staticmethod
    def semaphores(way):
        return (5, 7) if way == 1 else (4, 5)

    @staticmethod
    def near_far(which):
        return (3, 4) if which == 0 else (5, 6)

    def go(self, out, into, index, target):
        view = self.full.at[index]
        remote(view, view, self.send.at[out], self.recv.at[into], target).start()
        self.sent.add(out)

    def take(self, slot, view):
        remote(view, view, self.send.at[0], self.recv.at[slot], self.p.sib()).wait_recv()

    def shards(self, count):
        p = self.p
        return self.full.at[p.z, p.c, p.n] if count == 1 else self.full.at[0:count, p.c, p.n]

    def pass_on(self, slot, index):
        p = self.p
        self.go(slot, slot, index, {self.A: p.a, self.B: p.b, self.SIB: p.sib}[slot]())

    def others(self, n, slots):
        p = self.p
        for z in p.others:
            for slot in slots:
                self.pass_on(slot, (z, p.c, n))

    def column(self, n, slots):
        for slot in slots:
            self.pass_on(slot, (slice(None), self.p.c, n))

    def along(self, which, n):
        p = self.p
        near, far = self.near_far(which)
        own = (p.z, p.c, n)
        self.go(self.Z + which, far, own, p.chip(p.z2))
        self.go(self.Z + which, near, own, p.chip(p.z1))

        @pl.when(p.middle)
        def _():
            self.go(self.Z + which, near, own, p.chip(p.z3))

    def relay(self, which, n):
        p = self.p
        near, far = self.near_far(which)
        self.take(far, self.shards(1))

        @pl.when(p.middle)
        def _():
            self.go(self.Z + which, near, (p.z2, p.c, n), p.chip(p.z1))

    def take_near(self, which):
        self.take(self.near_far(which)[0], self.shards(2))

    def steps(self):
        p = self.p
        A, B, SIB = self.A, self.B, self.SIB

        def start():
            own = (p.z, p.c, p.n)
            self.pass_on(A, own)
            self.pass_on(B, own)
            self.along(0, p.n)
            self.pass_on(SIB, own)

        def own_relay():
            self.relay(0, p.n)

        def own_column():
            self.take_near(0)
            self.others(p.n, (A, B, SIB))

        def column_of_a():
            self.take(A, self.shards(self.full.shape[0]))
            self.column(p.na, (B, SIB))

        def shard_of_a():
            self.take(A, self.shards(1))
            self.along(1, p.na)
            self.pass_on(B, (p.z, p.c, p.na))
            self.pass_on(SIB, (p.z, p.c, p.na))

        def own_column_late():
            self.take_near(0)
            self.others(p.n, (B, SIB))
            self.relay(1, p.na)

        def column_of_a_late():
            self.take_near(1)
            self.others(p.na, (B, SIB))

        def from_b():
            self.take(B, self.full.at[:, p.c, 0:2])
            self.column(p.nb, (SIB,))
            self.column(p.nab, (SIB,))

        def from_sib():
            self.take(SIB, self.full.at[:, p.c])

        def start_row():
            self.pass_on(A, (p.z, p.c, p.n))
            self.pass_on(B, (p.z, p.c, p.n))

        def shard_of_a_on():
            self.take(A, self.shards(1))
            self.pass_on(B, (p.z, p.c, p.na))

        near, far = self.near_far(0)
        row = (p.z, p.c)

        def row_along():
            self.take(B, self.shards(2))
            self.go(self.Z, far, row, p.chip(p.z2))
            self.go(self.Z, near, row, p.chip(p.z1))

            @pl.when(p.middle)
            def _():
                self.go(self.Z, near, row, p.chip(p.z3))

        def row_relay():
            self.take(far, self.full.at[p.z, p.c])

            @pl.when(p.middle)
            def _():
                self.go(self.Z, near, (p.z2, p.c), p.chip(p.z1))

        def rows_over():
            self.take(near, self.full.at[0:2, p.c])
            self.pass_on(SIB, (slice(None), p.c))

        if self.way == 2:
            return [start_row, shard_of_a_on, row_along, row_relay, rows_over, from_sib]
        if self.way == 1:
            return [start, shard_of_a, own_relay, own_column_late, column_of_a_late, from_b, from_sib]
        return [start, own_relay, own_column, column_of_a, from_b, from_sib]

    def finish(self):
        p, full = self.p, self.full
        if not self.sent:
            return

        def sent(slot, view):
            remote(view, view, self.send.at[slot], self.recv.at[0], p.sib()).wait_send()

        sent(self.A, self.shards(full.shape[0] if self.way == 0 else 1))
        sent(self.B, self.shards(2) if self.way == 2 else full.at[:, p.c, 0:2])
        sent(self.SIB, full.at[:, p.c])
        for which in range(2 if self.way == 1 else 1):

            @pl.when(p.middle)
            def _(which=which):
                sent(self.Z + which, full.at[:, p.c] if self.way == 2 else self.shards(4))

            @pl.when(p.end)
            def _(which=which):
                sent(self.Z + which, full.at[0:2, p.c] if self.way == 2 else self.shards(2))

        self.sent = set()

    def step(self, i):
        self.steps()[i]()


class Scatter:
    def __init__(self, place, full, from_sib, from_b, from_a, from_z, out, send, recv, way):
        self.p, self.full, self.out, self.send, self.recv = place, full, out, send, recv
        self.from_sib, self.from_b, self.from_a, self.from_z = from_sib, from_b, from_a, from_z
        self.way = way
        self.sent = set()

    @staticmethod
    def semaphores(way):
        return (5, 8) if way == 1 else (4, 6)

    @staticmethod
    def landing(full, way):
        z, _, n, r, c = full
        if way == 2:
            return [(z, n, r, c), (2, 1, r, c), (1, r, c), (4, n, r, c)]
        if way == 1:
            return [(z, n, r, c), (2, z, r, c), (1, r, c), (8, r, c)]
        return [(z, n, r, c), (2, z, r, c), (z, r, c), (4, r, c)]

    SIB, A, B, Z, ZA = range(5)
    B1 = 3

    @staticmethod
    def sum_relay(which):
        return (4, 5) if which == 0 else (6, 7)

    def go(self, out, into, src, dst, target):
        remote(src, dst, self.send.at[out], self.recv.at[into], target).start()
        self.sent.add(out)

    def take(self, slot, view):
        remote(view, view, self.send.at[0], self.recv.at[slot], self.p.sib()).wait_recv()

    def add(self, n, part):
        c = self.p.c
        for z in range(self.full.shape[0]):
            self.full[z, c, n] = self.full[z, c, n] + part(z)


    def along(self, which, n):
        p = self.p
        total, relay = self.sum_relay(which)

        def send(z, target, land, into):
            self.go(self.Z + which, into, self.full.at[z, p.c, n], self.from_z.at[4 * which + land], p.chip(target))

        @pl.when(p.end)
        def _():
            send(p.z3, p.z1, 3, relay)
            send(p.z2, p.z2, 1, total)

        @pl.when(p.middle)
        def _():
            send(p.z3, p.z3, 2, total)

        send(p.z1, p.z1, 0, total)

    def relay(self, which, n):
        p = self.p
        total, relay = self.sum_relay(which)

        @pl.when(p.middle)
        def _():
            land = self.from_z.at[4 * which + 3]
            self.take(relay, land)
            self.full[p.z2, p.c, n] = self.full[p.z2, p.c, n] + self.from_z[4 * which + 3]
            view = self.full.at[p.z2, p.c, n]
            self.go(self.Z + which, total, view, self.from_z.at[4 * which + 1], p.chip(p.z2))

    def sum_along(self, which, n, put):
        p = self.p
        total, _ = self.sum_relay(which)
        first = 4 * which

        def add_up(count):
            self.take(total, self.from_z.at[first : first + count])
            x = self.full[p.z, p.c, n].astype(F32)
            for i in range(count):
                x = x + self.from_z[first + i].astype(F32)
            put(x)

        @pl.when(p.end)
        def _():
            add_up(2)

        @pl.when(p.middle)
        def _():
            add_up(3)

    def steps(self):
        p = self.p

        def start():
            self.go(self.SIB, self.SIB, self.full.at[:, 1 - p.c], self.from_sib, p.sib())

        def other_core():
            self.take(self.SIB, self.from_sib)
            for slot, half, n in ((self.B, 0, p.nab), (self.B1, 1, p.nb)):
                self.add(n, lambda z, n=n: self.from_sib[z, n])
                self.go(self.B, slot, self.full.at[:, p.c, n], self.from_b.at[half], p.b())
            for n in (p.na, p.n):
                self.add(n, lambda z, n=n: self.from_sib[z, n])

        def partner_b():
            self.take(self.B, self.from_b.at[0])
            self.add(p.na, lambda z: self.from_b[0, z])
            if self.way == 1:
                self.along(1, p.na)
            else:
                self.go(self.A, self.A, self.full.at[:, p.c, p.na], self.from_a, p.a())
            self.take(self.B1, self.from_b.at[1])
            self.add(p.n, lambda z: self.from_b[1, z])
            if self.way == 1:
                self.along(0, p.n)

        def partner_a():
            self.take(self.A, self.from_a)
            self.add(p.n, lambda z: self.from_a[z])
            self.along(0, p.n)

        def relay():
            self.relay(0, p.n)

        def store(x):
            self.out[...] = x

        def end():
            self.sum_along(0, p.n, store)

        def relay_both():
            self.relay(1, p.na)
            self.relay(0, p.n)

        def to_a():
            def put(x):
                self.full[p.z, p.c, p.na] = x.astype(self.full.dtype)

            self.sum_along(1, p.na, put)
            self.go(self.A, self.A, self.full.at[p.z, p.c, p.na], self.from_a.at[0], p.a())
            self.sum_along(0, p.n, store)

        def end_a():
            self.take(self.A, self.from_a.at[0])
            self.out[...] = self.out[...] + self.from_a[0].astype(F32)

        total, relayed = self.sum_relay(0)

        def row(z, target, land, into):
            self.go(self.Z, into, self.full.at[z, p.c], self.from_z.at[land], p.chip(target))

        def rows_along():
            self.take(self.SIB, self.from_sib)
            for n in range(self.full.shape[2]):
                self.add(n, lambda z, n=n: self.from_sib[z, n])

            @pl.when(p.end)
            def _():
                row(p.z3, p.z1, 3, relayed)
                row(p.z2, p.z2, 1, total)

            @pl.when(p.middle)
            def _():
                row(p.z3, p.z3, 2, total)

            row(p.z1, p.z1, 0, total)

        def row_relay():
            @pl.when(p.middle)
            def _():
                self.take(relayed, self.from_z.at[3])
                for n in range(self.full.shape[2]):
                    self.full[p.z2, p.c, n] = self.full[p.z2, p.c, n] + self.from_z[3, n]
                row(p.z2, p.z2, 1, total)

        def row_to_b():
            def add_up(count):
                self.take(total, self.from_z.at[0:count])
                for n in range(self.full.shape[2]):
                    x = self.full[p.z, p.c, n].astype(F32)
                    for i in range(count):
                        x = x + self.from_z[i, n].astype(F32)
                    self.full[p.z, p.c, n] = x.astype(self.full.dtype)

            @pl.when(p.end)
            def _():
                add_up(2)

            @pl.when(p.middle)
            def _():
                add_up(3)

            for slot, half, n in ((self.B, 0, p.nab), (self.B1, 1, p.nb)):
                self.go(self.B, slot, self.full.at[p.z, p.c, n], self.from_b.at[half, 0], p.b())

        def shard_to_a():
            self.take(self.B, self.from_b.at[0, 0])
            self.full[p.z, p.c, p.na] = self.full[p.z, p.c, p.na] + self.from_b[0, 0]
            self.go(self.A, self.A, self.full.at[p.z, p.c, p.na], self.from_a.at[0], p.a())
            self.take(self.B1, self.from_b.at[1, 0])
            self.out[...] = self.full[p.z, p.c, p.n].astype(F32) + self.from_b[1, 0].astype(F32)

        if self.way == 2:
            return [start, rows_along, row_relay, row_to_b, shard_to_a, end_a]
        if self.way == 1:
            return [start, other_core, partner_b, relay_both, to_a, end_a]
        return [start, other_core, partner_b, partner_a, relay, end]

    def finish(self):
        p, full = self.p, self.full
        if not self.sent:
            return
        one, all_z, some = full.at[p.z, p.c, p.n], full.at[:, p.c, p.n], full.at[0:3, p.c, p.n]
        views = {
            self.SIB: full.at[:, p.c],
            self.A: all_z if self.way == 0 else one,
            self.B: full.at[0:2, p.c, p.n] if self.way == 2 else full.at[:, p.c, 0:2],
            self.Z: full.at[0:3, p.c] if self.way == 2 else some,
            self.ZA: some,
        }
        for slot in sorted(self.sent):
            view = views[slot]
            remote(view, view, self.send.at[slot], self.recv.at[0], p.sib()).wait_send()
        self.sent = set()

    def step(self, i):
        self.steps()[i]()


def stats(x):
    centre = jnp.mean(x, axis=-1, keepdims=True)
    centred = x - centre
    spread = jnp.mean(centred * centred, axis=-1, keepdims=True)
    r = lax.rsqrt(spread + EPS)
    return centred * r, r


def norm_into(src, gain, dst, rows):
    total = src.shape[0]

    def body(i):
        at = ds(i * rows, rows)
        xn, _ = stats(src[at, :].astype(F32))
        dst[at, :] = (xn * gain).astype(BF)

    loop(total // rows, body)


def halves(shape):
    return lax.broadcasted_iota(jnp.int32, shape, 1) < shape[1] // 2


def split_heads(x):
    low = halves(x.shape)
    zero = jnp.zeros_like(x)
    return jnp.concatenate([jnp.where(low, x, zero), jnp.where(low, zero, x)], 0)


def head_ones(keys):
    shape = (2 * keys, LANES)
    row = lax.broadcasted_iota(jnp.int32, shape, 0) < keys
    low = lax.broadcasted_iota(jnp.int32, shape, 1) < LANES // 2
    return jnp.where(row == low, 1.0, 0.0).astype(BF)


def unroll(first, last, body):
    for i in range(first, last):
        body(i)


def spatial_forward(qkv, probs, att, patches, width, first, last):
    head = width // HEADS
    scale = head ** -0.5
    pairs = range(HEADS // 2)
    ones = head_ones(patches)

    def body(s):
        at = ds(s * patches, patches)
        parts = []
        for pair in pairs:
            lane = pair * 2 * head
            q = qkv[at, lane : lane + 2 * head]
            parts.append(dot(q, split_heads(qkv[at, width + lane : width + lane + 2 * head]), 1, 1))
        scores = jnp.concatenate(parts, 0) * scale
        low = halves(scores.shape)
        top0 = jnp.max(jnp.where(low, scores, -jnp.inf), axis=-1, keepdims=True)
        top1 = jnp.max(jnp.where(low, -jnp.inf, scores), axis=-1, keepdims=True)
        e = jnp.exp(scores - jnp.where(low, top0, top1))
        e_low = e.astype(BF)
        parts = []
        for pair in pairs:
            lane = pair * 2 * head
            v2 = split_heads(qkv[at, 2 * width + lane : 2 * width + lane + 2 * head])
            rows = slice(pair * patches, (pair + 1) * patches)
            parts.append(dot(e_low[rows], jnp.concatenate([v2, ones], 1), 1, 0))
        both = jnp.concatenate(parts, 0)
        r = 1.0 / both[:, 2 * head :]
        probs[s] = (e * r).astype(BF).reshape(HEADS // 2, patches, 2 * patches)
        new = (both[:, : 2 * head] * r).astype(BF)
        for pair in pairs:
            att[at, pair * 2 * head : (pair + 1) * 2 * head] = new[pair * patches : (pair + 1) * patches]

    unroll(first, last, body)


def pad_heads(x, lanes):
    low = halves(x.shape)
    zero = jnp.zeros_like(x)
    fill = jnp.zeros((lanes - x.shape[0], x.shape[1]), x.dtype)
    return jnp.concatenate([jnp.where(low, x, zero), fill, jnp.where(low, zero, x), fill], 0).astype(BF)


LANES = 128
SUB = 8


def temporal_forward(qkv, probs, att, bias, slots, width, first, last):
    head = width // HEADS
    scale = head ** -0.5
    group = slots * SUB
    pairs = range(HEADS // 2)
    parts_of = [slice(half * group, (half + 1) * group) for half in range(2)]

    def body(i):
        at = ds(i * 2 * group, 2 * group)
        parts = []
        for pair in pairs:
            lane = pair * 2 * head
            q = qkv[at, lane : lane + 2 * head].astype(F32)
            k = qkv[at, width + lane : width + lane + 2 * head].astype(F32)
            for rows in parts_of:
                x = dot(q[rows].astype(BF), pad_heads(k[rows], LANES), 1, 1)
                parts += [x[:, :LANES], x[:, LANES:]]
        scores = jnp.stack(parts, 0) * scale + bias[...][None]
        e = jnp.exp(scores - jnp.max(scores, axis=-1, keepdims=True))
        p = (e / jnp.sum(e, axis=-1, keepdims=True)).astype(BF)
        for pair in pairs:
            lane = pair * 2 * head
            v = qkv[at, 2 * width + lane : 2 * width + lane + 2 * head].astype(F32)
            out = []
            for half, rows in enumerate(parts_of):
                j = (pair * 2 + half) * 2
                both = jnp.concatenate([p[j], p[j + 1]], 1)
                probs[i * 2 + half, pair] = both
                out.append(dot(both, pad_heads(v[rows], LANES), 1, 0))
            att[at, lane : lane + 2 * head] = jnp.concatenate(out, 0).astype(BF)

    unroll(first, last, body)


def make_bias(bias, count, slots):
    group = slots * SUB
    q = lax.broadcasted_iota(jnp.int32, (group, LANES), 0)
    k = lax.broadcasted_iota(jnp.int32, (group, LANES), 1)
    sq, sk = q // SUB, k // SUB
    ok = (q - sq * SUB == k - sk * SUB) & (sk <= sq) & (sk < count)
    bias[...] = jnp.where(ok, 0.0, -1e9)


def gelu_pair(z):
    k0 = 0.7978845608028654
    k1 = k0 * 0.044715
    z2 = z * z
    half = 0.5 + 0.5 * jnp.tanh(z * (k0 + k1 * z2))
    active = z * half
    slope = half + half * (z - active) * (2.0 * k0 + 6.0 * k1 * z2)
    return active, slope


def wide_rows(ref, width, columns=None):
    x = ref[...] if columns is None else ref[:, :, :, :, columns]
    return x.reshape(width, x.shape[-1])


def unsplit_heads(x, second, rows):
    low = halves((rows, x.shape[1]))
    return jnp.where(low, x[:rows], x[second : second + rows])


def spatial_backward(qkv, probs, grad, patches, width, first, last):
    head = width // HEADS
    scale = head ** -0.5
    pairs = range(HEADS // 2)
    rows_of = [slice(pair * patches, (pair + 1) * patches) for pair in pairs]

    def body(s):
        at = ds(s * patches, patches)
        cols = [[slice(t * width + p * 2 * head, t * width + (p + 1) * 2 * head) for t in range(3)] for p in pairs]
        p_low = probs[s].reshape(HEADS // 2 * patches, 2 * patches)
        soft = p_low.astype(F32)
        q = [qkv[at, cols[p][0]] for p in pairs]
        k2 = [split_heads(qkv[at, cols[p][1]]) for p in pairs]
        g = [grad[at, p * 2 * head : (p + 1) * 2 * head] for p in pairs]
        gp = [dot(g[p], split_heads(qkv[at, cols[p][2]]), 1, 1) for p in pairs]
        gv = [dot(p_low[rows_of[p]], g[p], 0, 0) for p in pairs]
        gp = jnp.concatenate(gp, 0)
        low = halves(gp.shape)
        both = gp * soft
        sum0 = jnp.sum(jnp.where(low, both, 0.0), axis=-1, keepdims=True)
        sum1 = jnp.sum(jnp.where(low, 0.0, both), axis=-1, keepdims=True)
        gs = (soft * (gp - jnp.where(low, sum0, sum1))).astype(BF)
        gq = [dot(gs[rows_of[p]], k2[p], 1, 0) for p in pairs]
        gk = [dot(gs[rows_of[p]], q[p], 0, 0) for p in pairs]
        for p in pairs:
            qkv[at, cols[p][0]] = (gq[p] * scale).astype(BF)
            qkv[at, cols[p][1]] = (unsplit_heads(gk[p], patches, patches) * scale).astype(BF)
            qkv[at, cols[p][2]] = unsplit_heads(gv[p], patches, patches).astype(BF)

    unroll(first, last, body)


def temporal_backward(qkv, probs, grad, slots, width, first, last):
    head = width // HEADS
    scale = head ** -0.5
    group = slots * SUB
    pairs = range(HEADS // 2)
    parts_of = [slice(half * group, (half + 1) * group) for half in range(2)]

    def body(i):
        at = ds(i * 2 * group, 2 * group)
        cols = [[slice(t * width + p * 2 * head, t * width + (p + 1) * 2 * head) for t in range(3)] for p in pairs]
        qs, ks, gs_in, ps, gp, soft = [], [], [], [], [], []
        for pair in pairs:
            q, k, v = (qkv[at, c].astype(F32) for c in cols[pair])
            g = grad[at, pair * 2 * head : (pair + 1) * 2 * head].astype(F32)
            for half, rows in enumerate(parts_of):
                qs.append(q[rows].astype(BF))
                ks.append(pad_heads(k[rows], LANES))
                gs_in.append(g[rows].astype(BF))
                p = probs[i * 2 + half, pair]
                ps.append(p)
                x = dot(gs_in[-1], pad_heads(v[rows], LANES), 1, 1)
                wide = p.astype(F32)
                gp += [x[:, :LANES], x[:, LANES:]]
                soft += [wide[:, :LANES], wide[:, LANES:]]
        many = range(len(ps))
        gv = [unsplit_heads(dot(ps[j], gs_in[j], 0, 0), LANES, group) for j in many]
        gp = jnp.stack(gp, 0)
        soft = jnp.stack(soft, 0)
        delta = jnp.sum(gp * soft, axis=-1, keepdims=True)
        gs = (soft * (gp - delta)).astype(BF)
        gs = [jnp.concatenate([gs[2 * j], gs[2 * j + 1]], 1) for j in many]
        gq = [dot(gs[j], ks[j], 1, 0) * scale for j in many]
        gk = [unsplit_heads(dot(gs[j], qs[j], 0, 0), LANES, group) * scale for j in many]
        for pair in pairs:
            for c, outs in zip(cols[pair], (gq, gk, gv)):
                qkv[at, c] = jnp.concatenate(outs[2 * pair : 2 * pair + 2], 0).astype(BF)

    unroll(first, last, body)


def norm_back(src, grad, gain, base, dst, low, sums, rows):
    total, width = grad.shape
    sums[...] = jnp.zeros_like(sums)

    def body(i):
        at = ds(i * rows, rows)
        xn, r = stats(src[at, :].astype(F32))
        g = grad[at, :]
        e = g * gain
        inner = e - jnp.mean(e, axis=-1, keepdims=True) - xn * jnp.mean(e * xn, axis=-1, keepdims=True)
        res = base[at, :] + r * inner
        if dst is not None:
            dst[at, :] = res
        low[at, :] = res.astype(BF)
        sums[...] += jnp.sum((g * xn).reshape(rows // SUB, SUB, width), axis=0)

    loop(total // rows, body)


def gain_row(gains, which):
    return gains[which : which + 1, :]


class Sizes:
    def __init__(self, mesh, video, in_weight):
        self.depth = mesh.shape["wide"] // 2
        self.narrow = mesh.shape["narrow"]
        self.slots, self.patches, self.width = video.shape[1:]
        self.hidden = in_weight.shape[2]
        self.tokens = self.slots * self.patches
        self.group = self.slots * SUB
        devices = 2 * self.depth * self.narrow
        w = self.width // devices
        self.shards = {
            "qkv": (w, 3 * self.width),
            "out": (w, self.width),
            "in": (w, self.hidden),
            "down": (self.hidden // devices, self.width),
        }
        self.mesh_dims = (self.depth, 2, self.narrow)

    def full(self, name):
        return self.mesh_dims + (TILE_GAIN if name == "gain" else self.shards[name])

    def acts(self, b):
        t, w, f = self.tokens, self.width, self.hidden
        pairs = HEADS // 2
        if b == 0:
            probs = (self.slots, pairs, self.patches, 2 * self.patches)
        else:
            probs = (self.patches // SUB, pairs, self.group, 2 * LANES)
        return {
            "normed": ((t, w), BF),
            "qkv": ((t, 3 * w), BF),
            "probs": (probs, BF),
            "att": ((t, w), BF),
            "middle": ((t, w), F32),
            "mlp": ((t, w), BF),
            "active": ((t, f), BF),
            "slope": ((t, f), BF),
        }


TILE_GAIN = (16, LANES)
NAMES = ("qkv", "out", "in", "down")
ACTS = ("normed", "qkv", "probs", "att", "middle", "mlp", "active", "slope")
SPLIT = {"gain": 1, "qkv": 2, "out": 1, "in": 2, "down": 2}


def pieces_of(name, b):
    return [(name, b, i) for i in range(SPLIT[name])]


GAIN = ("gain", 0)
GATHER_ORDER = [(*GAIN, 0)] + [piece for b in range(2) for name in NAMES for piece in pieces_of(name, b)]
SCATTER_ORDER = [
    piece for b in (1, 0) for name in ("down", "in", "out", "qkv") for piece in pieces_of(name, b)
] + [(*GAIN, 0)]


def columns_of(piece, columns):
    name, _, i = piece
    part = columns // SPLIT[name]
    return slice(i * part, (i + 1) * part)


def row_tile(tokens):
    return tokens // 2 if tokens % 32 == 0 else tokens


def keys_of_weights():
    return [(name, b) for b in range(2) for name in NAMES]


KEPT = ("normed", "qkv", "att", "middle", "mlp", "active", "slope")


def layer_kernel(sz, *refs):
    refs = list(refs)

    def grab(n):
        taken, refs[:n] = refs[:n], []
        return taken

    video, cotangent, slot_count, attn_gain, mlp_gain = grab(5)
    shard = dict(zip(NAMES, grab(4)))
    out, grad_video = grab(2)
    outs = dict(zip(NAMES, grab(4)))
    gain_outs = grab(2)
    acts_hbm = dict(zip(KEPT, grab(len(KEPT))))
    acts = dict(zip(ACTS, grab(8)))
    probs1, h1 = grab(2)
    full = dict(zip([GAIN] + keys_of_weights(), grab(9)))
    grads = dict(zip([(name, 1) for name in NAMES] + [GAIN], grab(5)))
    landing = {piece: grab(4) for piece in SCATTER_ORDER}
    gains, bias, gain_out, grad, grad_mid, grad_norm, low, grad_att, sums = grab(9)
    gather_send, gather_recv, scatter_send, scatter_recv, local = grab(5)
    assert not refs
    for name in NAMES:
        grads[(name, 0)] = full[(name, 1)]

    place = Place()
    met = place.greet()

    def part_of(ref, piece, columns):
        if SPLIT[piece[0]] == 1:
            return ref
        return ref.at[(slice(None),) * (len(ref.shape) - 1) + (columns_of(piece, columns),)]

    gathers = {}
    at_send = at_recv = 0
    for k, piece in enumerate(GATHER_ORDER):
        n_send, n_recv = Gather.semaphores(GATHER_WAYS[k])
        ref = full[piece[:2]]
        sems = [gather_send.at[at_send : at_send + n_send], gather_recv.at[at_recv : at_recv + n_recv]]
        gathers[piece] = Gather(place, part_of(ref, piece, ref.shape[-1]), *sems, GATHER_WAYS[k])
        at_send += n_send
        at_recv += n_recv
    scatters = {}
    at_send = at_recv = 0
    for k, piece in enumerate(SCATTER_ORDER):
        n_send, n_recv = Scatter.semaphores(SCATTER_WAYS[k])
        ref = grads[piece[:2]]
        columns = ref.shape[-1]
        target = gain_out if piece[:2] == GAIN else outs[piece[0]].at[piece[1]]
        sems = [scatter_send.at[at_send : at_send + n_send], scatter_recv.at[at_recv : at_recv + n_recv]]
        scatters[piece] = Scatter(
            place,
            part_of(ref, piece, columns),
            *landing[piece],
            part_of(target, piece, columns),
            *sems,
            SCATTER_WAYS[k],
        )
        at_send += n_send
        at_recv += n_recv
    own = (place.z, place.c, place.n)
    full[GAIN][own] = place_gains(attn_gain, mlp_gain, place.w * sz.narrow + place.n)
    for key in keys_of_weights():
        full[key][own] = shard[key[0]][key[1]].astype(BF)
    place.met(met)

    moving = {}

    def move(name, src, dst):
        copy = pltpu.make_async_copy(src, dst, local.at[KEPT.index(name)])
        copy.start()
        moving[name] = copy

    def settle(*names):
        for name in names:
            if name in moving:
                moving.pop(name).wait()

    def act(name, b):
        return probs1 if (name, b) == ("probs", 1) else acts[name]

    def keep(b, *names):
        for name in names:
            if b == 0 and name in KEPT:
                move(name, acts[name], acts_hbm[name])

    def fetch(b, *names):
        for name in names:
            if b == 1 and name in KEPT:
                settle(name)
                move(name, acts_hbm[name], acts[name])

    count = slot_count[0]
    t, w = sz.tokens, sz.width

    def stage_gain():
        make_bias(bias, count, sz.slots)
        tile = jnp.sum(full[GAIN][...].astype(F32).reshape(-1, 16, LANES), axis=0)
        for g in range(4):
            rows = [tile[g * 4 + r : g * 4 + r + 1, :] for r in range(w // LANES)]
            gains[g : g + 1, :] = jnp.concatenate(rows, 1)

    def forward_stages(b):
        a = {name: act(name, b) for name in ACTS}
        h = video if b == 0 else h1

        def norm1():
            settle("normed")
            norm_into(h, gain_row(gains, 2 * b), a["normed"], row_tile(t))
            keep(b, "normed")

        def qkv(first, last):
            settle("qkv")
            at = slice(first, last)
            a["qkv"][:, at] = dot(a["normed"][...], wide_rows(full[("qkv", b)], w, at), 1, 0).astype(BF)
            if last == 3 * w:
                keep(b, "qkv")

        def attend(first, last):
            settle("att")
            if b == 0:
                spatial_forward(a["qkv"], a["probs"], a["att"], sz.patches, w, first, last)
                end = sz.slots
            else:
                temporal_forward(a["qkv"], a["probs"], a["att"], bias, sz.slots, w, first, last)
                end = sz.patches // (2 * SUB)
            if last == end:
                keep(b, "probs", "att")

        def project():
            settle("middle")
            new = dot(a["att"][...], wide_rows(full[("out", b)], w), 1, 0)
            a["middle"][...] = h[...].astype(F32) + new
            keep(b, "middle")

        def norm2():
            settle("mlp")
            norm_into(a["middle"], gain_row(gains, 2 * b + 1), a["mlp"], row_tile(t))
            keep(b, "mlp")

        def expand(first, last):
            at = slice(first, last)
            settle("active", "slope")
            weight = wide_rows(full[("in", b)], w, at)
            rows = row_tile(t)
            for r in range(0, t, rows):
                active, slope = gelu_pair(dot(a["mlp"][r : r + rows, :], weight, 1, 0))
                a["active"][r : r + rows, at] = active.astype(BF)
                a["slope"][r : r + rows, at] = slope.astype(BF)
            if last == sz.hidden:
                keep(b, "active", "slope")

        def contract(first, last):
            at = slice(first, last)
            new = a["middle"][:, at] + dot(a["active"][...], wide_rows(full[("down", b)], sz.hidden, at), 1, 0)
            if b == 0:
                new = new.reshape(sz.slots, sz.patches // SUB, SUB, last - first)
                for s in range(sz.slots):
                    h1_view[:, s * SUB : (s + 1) * SUB, at] = new[s]
            else:
                valid = lax.broadcasted_iota(jnp.int32, (sz.slots, 1, 1), 0) < count
                new = new.reshape(sz.patches // (2 * SUB), 2, sz.slots, SUB, last - first)
                for i in range(sz.patches // (2 * SUB)):
                    rows = jnp.concatenate([new[i, 0], new[i, 1]], axis=1)
                    out[:, i * 2 * SUB : (i + 1) * 2 * SUB, at] = jnp.where(valid, rows, 0.0).astype(BF)
                if last == w:
                    fetch(b, "active", "middle")

        n_a = sz.slots if b == 0 else sz.patches // (2 * SUB)
        cuts = [-(-n_a * i // 4) for i in range(5)]
        todo = [norm1]
        todo += [functools.partial(qkv, 3 * w * i // 2, 3 * w * (i + 1) // 2) for i in range(2)]
        todo += [functools.partial(attend, cuts[i], cuts[i + 1]) for i in range(4)]
        todo += [project, norm2]
        todo += [functools.partial(expand, sz.hidden * i // 4, sz.hidden * (i + 1) // 4) for i in range(4)]
        last = [functools.partial(contract, w * i // 2, w * (i + 1) // 2) for i in range(2)]
        return todo, last

    h1_view = h1.reshape(sz.patches // SUB, sz.group, w)

    def start():
        valid = lax.broadcasted_iota(jnp.int32, (sz.slots, 1, 1), 0) < count

        def body(i):
            rows = cotangent[:, ds(i * 2 * SUB, 2 * SUB), :].astype(F32)
            rows = jnp.where(valid, rows, 0.0)
            both = [rows[:, half * SUB : (half + 1) * SUB, :].reshape(sz.group, w) for half in range(2)]
            rows = jnp.concatenate(both, 0)
            at = ds(i * 2 * sz.group, 2 * sz.group)
            grad[at, :] = rows
            low[at, :] = rows.astype(BF)

        loop(sz.patches // (2 * SUB), body)

    def put_gain(which):
        row = jnp.sum(sums[...], axis=0, keepdims=True)
        per = w // LANES
        tile = jnp.concatenate([row[:, r * LANES : (r + 1) * LANES] for r in range(per)], 0)
        gain_rows[which * per : (which + 1) * per, :] = tile

    gain_rows = gain_out

    def backward_stages(b):
        a = {name: act(name, b) for name in ACTS}

        half = sz.hidden // 2
        z_half = sz.depth // 2

        def down_grad(i):
            settle("active")
            if b == 0 and i == 0:
                for gather in gathers.values():
                    gather.finish()
            at = slice(i * w // 2, (i + 1) * w // 2)
            g = dot(a["active"][...], low[:, at], 0, 0).astype(BF)
            grads[("down", b)][:, :, :, :, at] = g.reshape(sz.full("down")[:-1] + (w // 2,))

        def hidden_back(i):
            settle("slope")
            at = slice(i * half, (i + 1) * half)
            weight = full[("down", b)][i * z_half : (i + 1) * z_half].reshape(half, w)
            a["slope"][:, at] = (dot(low[...], weight, 1, 1) * a["slope"][:, at].astype(F32)).astype(BF)

        def in_grad(i):
            settle("mlp")
            at = slice(i * half, (i + 1) * half)
            g = dot(a["mlp"][...], a["slope"][:, at], 0, 0).astype(BF)
            grads[("in", b)][:, :, :, :, at] = g.reshape(sz.full("in")[:-1] + (half,))
            if i == 1:
                fetch(b, "mlp")

        def back_rows(src, weight, put):
            put(dot(src[...], wide_rows(weight, w), 1, 1))

        def mlp_back():

            def put(x):
                grad_norm[...] = x

            back_rows(a["slope"], full[("in", b)], put)
            fetch(b, "slope")

        def norm2_back():
            settle("middle")
            norm_back(a["middle"], grad_norm, gain_row(gains, 2 * b + 1), grad, grad_mid, low, sums, row_tile(t))
            put_gain(2 * b + 1)

        def out_grad():
            settle("att")

            g = dot(a["att"][...], low[...], 0, 0).astype(BF)
            grads[("out", b)][...] = g.reshape(sz.full("out"))
            fetch(b, "att")

        def att_back():

            def put(x):
                grad_att[...] = x.astype(BF)

            back_rows(low, full[("out", b)], put)

        def attend(first, last):
            settle("qkv", "probs")
            if b == 0:
                spatial_backward(a["qkv"], a["probs"], grad_att, sz.patches, w, first, last)
            else:
                temporal_backward(a["qkv"], a["probs"], grad_att, sz.slots, w, first, last)

        def qkv_grad(first, last):
            settle("normed")
            at = slice(first, last)
            g = dot(a["normed"][...], a["qkv"][:, at], 0, 0).astype(BF)
            grads[("qkv", b)][:, :, :, :, at] = g.reshape(sz.full("qkv")[:-1] + (last - first,))
            if last == 3 * w:
                fetch(b, "normed")

        def qkv_back():

            def put(x):
                grad_norm[...] = x

            back_rows(a["qkv"], full[("qkv", b)], put)
            fetch(b, "qkv")

        def norm1_back():
            src = h1 if b == 1 else video
            if b == 1:
                norm_back(src, grad_norm, gain_row(gains, 2), grad_mid, grad, low, sums, row_tile(t))
            else:
                norm_back(src, grad_norm, gain_row(gains, 0), grad_mid, None, low, sums, row_tile(t))
                grad_video[...] = low[...].reshape(grad_video.shape)
            put_gain(2 * b)

        def reorder():
            view = grad.reshape(sz.patches // SUB, sz.group, w)

            def body(s):
                rows = view[:, ds(s * SUB, SUB), :].reshape(sz.patches, w)
                at = ds(s * sz.patches, sz.patches)
                grad_norm[at, :] = rows
                low[at, :] = rows.astype(BF)

            loop(sz.slots, body)
            grad[...] = grad_norm[...]

        n_a = sz.slots if b == 0 else sz.patches // (2 * SUB)
        cuts = [-(-n_a * i // 4) for i in range(5)]
        todo = []
        for piece in (down_grad, hidden_back, in_grad):
            todo += [functools.partial(piece, i) for i in range(2)]
        todo += [mlp_back, norm2_back, out_grad, att_back]
        todo += [functools.partial(attend, cuts[i], cuts[i + 1]) for i in range(4)]
        todo += [functools.partial(qkv_grad, 3 * w * i // 2, 3 * w * (i + 1) // 2) for i in range(2)]
        if b == 1:
            todo += output
        todo += [qkv_back, norm1_back]
        if b == 1:
            todo += [reorder]
        return todo

    def spread_gain():
        tile = gain_out[...]
        grads[GAIN][...] = jnp.broadcast_to(tile, sz.full("gain"))

    first, last = forward_stages(0)
    second, output = forward_stages(1)
    work = [start, stage_gain] + first + last + second
    work = iter(work + backward_stages(1) + backward_stages(0) + [spread_gain])
    steps = [gathers[piece] for piece in GATHER_ORDER] + [scatters[piece] for piece in SCATTER_ORDER]
    for op in PLAN:
        if op < 0:
            next(work)()
        else:
            steps[op // 8].step(op % 8)
    assert next(work, None) is None
    pick_gains(gain_out[...], gain_outs, place.w * sz.narrow + place.n)
    settle(*KEPT)
    for scatter in scatters.values():
        scatter.finish()


def place_gains(attn_gain, mlp_gain, index):
    own = attn_gain.shape[1]
    per = LANES // own
    row = lax.broadcasted_iota(jnp.int32, (TILE_GAIN[0] // 4, LANES), 0)
    lane = lax.broadcasted_iota(jnp.int32, (TILE_GAIN[0] // 4, LANES), 1) // own
    here = row * per + lane == index
    tiles = []
    for b in range(2):
        for ref in (attn_gain, mlp_gain):
            values = jnp.concatenate([ref[b : b + 1, :]] * per, 1)
            tiles.append(jnp.where(here, values, 0.0))
    return jnp.concatenate(tiles, 0).astype(BF)


def pick_gains(tile, outs, index):
    own = outs[0].shape[1]
    per = LANES // own
    rows = TILE_GAIN[0] // 4
    row = lax.broadcasted_iota(jnp.int32, (rows, own), 0)
    for b in range(2):
        for kind, out in enumerate(outs):
            first = (2 * b + kind) * rows
            total = jnp.zeros((rows, own), F32)
            for j in range(per):
                piece = tile[first : first + rows, j * own : (j + 1) * own]
                total = total + jnp.where(row * per + j == index, piece, 0.0)
            out[b : b + 1, :] = jnp.sum(total, axis=0, keepdims=True)


PLAN = (
    112, 8, 48, 0, 24, 16, 1, 9, 64, 40, 104, 17, 88, 113, 49, 2, 10, 41, 25, 32, 72, 80, 18, 65, 3, 33, 96,
    26, 56, 11, 19, -1, 27, 57, 73, 81, 4, 42, 50, 34, 12, 5, -1, -1, 13, -1, 20, 21, -1, 58, 28, -1, 35, 89,
    97, 74, 51, -1, 66, -1, 43, 59, -1, 29, -1, -1, 75, 82, 90, 36, 37, -1, -1, 67, 44, 52, 98, 45, -1, 105,
    -1, 60, 83, 114, 91, 53, -1, 61, -1, 68, 99, 106, 76, -1, 69, -1, 77, -1, -1, -1, 84, -1, -1, 92, 115,
    107, 85, -1, -1, 100, 93, -1, -1, 101, -1, -1, 108, 116, -1, 120, -1, 128, 109, 117, -1, -1, 129, 121,
    -1, 136, -1, 144, -1, -1, -1, 152, 145, -1, -1, 153, -1, -1, 137, 130, 122, -1, -1, 160, -1, 168, 146,
    -1, 161, -1, -1, 169, -1, -1, 138, -1, 176, 154, 162, -1, 184, 123, 147, 177, -1, -1, -1, 192, 185, 139,
    -1, 200, -1, 193, 178, -1, 124, 201, -1, 208, 163, -1, 170, -1, 209, -1, 179, 186, -1, -1, -1, 216, 194,
    202, -1, 224, 217, 140, -1, -1, 187, 225, -1, 232, 203, 233, 188, 148, 210, 218, 226, 234, 131, 155, 171,
    195, 211, 219, 227, 235, 132, 156, 164, 172, 180, 196, 204, 212, 220, 228, 236, 125, 133, 141, 149, 157,
    165, 173, 181, 189, 197, 205, 213, 221, 229, 237,
)
GATHER_WAYS = (
    0, 0, 0, 0, 0, 0, 2, 0, 2, 0, 0, 0, 0, 0, 2,
)
SCATTER_WAYS = (
    0, 2, 0, 1, 2, 0, 2, 1, 0, 1, 0, 0, 1, 0, 0,
)


def copy_kernel(count, *refs):
    sems = refs[-1]
    refs = refs[:-1]
    down = [pltpu.make_async_copy(refs[i], refs[2 * count + i], sems.at[i]) for i in range(count)]
    up = [pltpu.make_async_copy(refs[2 * count + i], refs[count + i], sems.at[i]) for i in range(count)]
    for copy in down:
        copy.start()
    for i in range(count):
        down[i].wait()
        up[i].start()
    for copy in up:
        copy.wait()


def by_kernels(mesh, sz):
    vmem = pl.BlockSpec(memory_space=pltpu.VMEM)
    smem = pl.BlockSpec(memory_space=pltpu.SMEM)
    anyw = pl.BlockSpec(memory_space=pl.ANY)
    shape = jax.ShapeDtypeStruct
    t, w = sz.tokens, sz.width
    acts0 = sz.acts(0)
    clip_shape = shape((sz.slots, sz.patches, w), BF)
    dma = pltpu.SemaphoreType.DMA

    def landing(k, piece):
        full = sz.full(piece[0])
        full = full[:-1] + (full[-1] // SPLIT[piece[0]],)
        kind = F32 if piece[0] == "gain" else BF
        return [pltpu.VMEM(s, kind) for s in Scatter.landing(full, SCATTER_WAYS[k])]

    def run(video, frames, cotangent, qkv_weight, out_weight, in_weight, down_weight, attn_gain, mlp_gain):
        gain_shape = shape(attn_gain.shape, F32)
        shapes = [clip_shape, clip_shape]
        shapes += [shape((2,) + sz.shards[name], F32) for name in NAMES]
        shapes += [gain_shape, gain_shape]
        n_gather = [sum(Gather.semaphores(way)[i] for way in GATHER_WAYS) for i in range(2)]
        n_scatter = [sum(Scatter.semaphores(way)[i] for way in SCATTER_WAYS) for i in range(2)]
        res = pl.pallas_call(
            functools.partial(layer_kernel, sz),
            out_shape=shapes + [shape(*acts0[name]) for name in KEPT],
            in_specs=[vmem, vmem, smem] + [vmem] * 6,
            out_specs=[vmem] * len(shapes) + [anyw] * len(KEPT),
            scratch_shapes=[pltpu.VMEM(*acts0[name]) for name in ACTS]
            + [pltpu.VMEM(*sz.acts(1)["probs"]), pltpu.VMEM((t, w), F32)]
            + [pltpu.VMEM(sz.full(name), BF) for name, _ in [GAIN] + keys_of_weights()]
            + [pltpu.VMEM(sz.full(name), BF) for name in NAMES]
            + [pltpu.VMEM(sz.full("gain"), F32)]
            + [buffer for k, piece in enumerate(SCATTER_ORDER) for buffer in landing(k, piece)]
            + [
                pltpu.VMEM((4, w), F32),
                pltpu.VMEM((sz.group, LANES), F32),
                pltpu.VMEM(TILE_GAIN, F32),
                pltpu.VMEM((t, w), F32),
                pltpu.VMEM((t, w), F32),
                pltpu.VMEM((t, w), F32),
                pltpu.VMEM((t, w), BF),
                pltpu.VMEM((t, w), BF),
                pltpu.VMEM((SUB, w), F32),
                dma((n_gather[0],)),
                dma((n_gather[1],)),
                dma((n_scatter[0],)),
                dma((n_scatter[1],)),
                dma((len(KEPT),)),
            ],
            compiler_params=pltpu.CompilerParams(
                collective_id=0, has_side_effects=True, vmem_limit_bytes=VMEM_LIMIT
            ),
        )(
            video.reshape(t, w),
            cotangent.reshape(clip_shape.shape),
            (frames + 1) // 2,
            attn_gain,
            mlp_gain,
            qkv_weight,
            out_weight,
            in_weight,
            down_weight,
        )
        res = list(res)[: len(shapes)]
        res = pl.pallas_call(
            functools.partial(copy_kernel, len(res)),
            out_shape=shapes,
            in_specs=[anyw] * len(res),
            out_specs=[anyw] * len(res),
            scratch_shapes=[pltpu.VMEM(x.shape, x.dtype) for x in shapes] + [dma((len(res),))],
        )(*res)
        return (res[0].reshape(video.shape), res[1].reshape(video.shape), *res[2:])

    return run


def norm_rows(inputs, scaling):
    centre = jnp.mean(inputs, axis=-1, keepdims=True)
    centred = inputs - centre
    spread = jnp.mean(centred * centred, axis=-1, keepdims=True)
    return centred * lax.rsqrt(spread + EPS) * scaling


def project(rows_in, matrix):
    return jnp.einsum("cspd,de->cspe", rows_in, matrix, preferred_element_type=jnp.float32)


def project_back(rows_in, matrix):
    return jnp.einsum("cspe,de->cspd", rows_in, matrix, preferred_element_type=jnp.float32)


def weight_grad(left, right):
    return jnp.einsum("cspd,cspe->de", left, right, preferred_element_type=jnp.float32)


def pair_scores(first, second, which_block):
    if which_block == 0:
        return jnp.einsum("csphe,csqhe->cshpq", first, second, preferred_element_type=jnp.float32)
    return jnp.einsum("csphe,ctphe->cphst", first, second, preferred_element_type=jnp.float32)


def pair_mix(weighting, second, which_block):
    if which_block == 0:
        return jnp.einsum(
            "cshpq,csqhe->csphe", weighting, second, preferred_element_type=jnp.float32
        )
    return jnp.einsum("cphst,ctphe->csphe", weighting, second, preferred_element_type=jnp.float32)


def pair_back(weighting, first, which_block):
    if which_block == 0:
        return jnp.einsum(
            "cshpq,csphe->csqhe", weighting, first, preferred_element_type=jnp.float32
        )
    return jnp.einsum("cphst,csphe->ctphe", weighting, first, preferred_element_type=jnp.float32)


def masked_scores(queries, key_rows, which_block, allowed):
    head_size = queries.shape[-1]
    scores = pair_scores(queries, key_rows, which_block) * head_size ** (-0.5)
    if which_block == 1:
        scores = jnp.where(allowed[:, None, None], scores, -1000000000.0)
    return scores


def block_forward(inputs, weights, which_block, allowed):
    qkv_matrix, out_matrix, in_matrix, down_matrix, attn_scaling, mlp_scaling = weights
    full_shape = inputs.shape
    head_size = full_shape[-1] // HEADS
    normed, norm_pull = jax.vjp(norm_rows, inputs, attn_scaling.astype(jnp.float32))
    normed_low = normed.astype(jnp.bfloat16)
    qkv_rows = project(normed_low, qkv_matrix).astype(jnp.bfloat16)
    split = qkv_rows.reshape(full_shape[:3] + (3, HEADS, head_size))
    queries = split[:, :, :, 0]
    key_rows = split[:, :, :, 1]
    value_rows = split[:, :, :, 2]
    scores = masked_scores(queries, key_rows, which_block, allowed)
    row_max = jnp.max(scores, axis=-1, keepdims=True)
    shifted = jnp.exp(scores - row_max)
    row_sum = jnp.sum(shifted, axis=-1, keepdims=True)
    log_total = row_max + jnp.log(row_sum)
    probs_low = (shifted / row_sum).astype(jnp.bfloat16)
    attended = pair_mix(probs_low, value_rows, which_block).reshape(full_shape).astype(jnp.bfloat16)
    middle = inputs + project(attended, out_matrix)
    normed_mlp, mlp_pull = jax.vjp(norm_rows, middle, mlp_scaling.astype(jnp.float32))
    normed_mlp_low = normed_mlp.astype(jnp.bfloat16)
    hidden = project(normed_mlp_low, in_matrix)
    active, gelu_pull = jax.vjp(jax.nn.gelu, hidden)
    active_low = active.astype(jnp.bfloat16)
    result = middle + project(active_low, down_matrix)
    stored = (
        norm_pull,
        normed_low,
        queries,
        key_rows,
        value_rows,
        log_total,
        attended,
        mlp_pull,
        normed_mlp_low,
        gelu_pull,
        active_low,
    )
    return (result, stored)


def block_backward(gradient, stored, weights, which_block, allowed):
    qkv_matrix, out_matrix, in_matrix, down_matrix, attn_scaling, mlp_scaling = weights
    (
        norm_pull,
        normed_low,
        queries,
        key_rows,
        value_rows,
        log_total,
        attended,
        mlp_pull,
        normed_mlp_low,
        gelu_pull,
        active_low,
    ) = stored
    full_shape = gradient.shape
    head_size = queries.shape[-1]
    result_low = gradient.astype(jnp.bfloat16)
    grad_down_w = weight_grad(active_low, result_low)
    grad_active = project_back(result_low, down_matrix)
    grad_hidden = gelu_pull(grad_active)[0].astype(jnp.bfloat16)
    grad_in_w = weight_grad(normed_mlp_low, grad_hidden)
    grad_normed_mlp = project_back(grad_hidden, in_matrix)
    middle_part, grad_mlp_scaling = mlp_pull(grad_normed_mlp)
    grad_middle = gradient + middle_part
    middle_low = grad_middle.astype(jnp.bfloat16)
    grad_out_w = weight_grad(attended, middle_low)
    grad_attended = project_back(middle_low, out_matrix).astype(jnp.bfloat16)
    grad_attended = grad_attended.reshape(queries.shape)
    scores = masked_scores(queries, key_rows, which_block, allowed)
    soft_probs = jnp.exp(scores - log_total)
    grad_probs = pair_scores(grad_attended, value_rows, which_block)
    row_delta = jnp.sum(grad_probs * soft_probs, axis=-1, keepdims=True)
    grad_scores = (soft_probs * (grad_probs - row_delta)).astype(jnp.bfloat16)
    score_scale = head_size ** (-0.5)
    grad_queries = pair_mix(grad_scores, key_rows, which_block) * score_scale
    grad_keys = pair_back(grad_scores, queries, which_block) * score_scale
    grad_values = pair_back(soft_probs.astype(jnp.bfloat16), grad_attended, which_block)
    grad_qkv_rows = jnp.stack([grad_queries, grad_keys, grad_values], axis=3).astype(jnp.bfloat16)
    grad_qkv_rows = grad_qkv_rows.reshape(full_shape[:3] + (3 * full_shape[-1],))
    grad_qkv_w = weight_grad(normed_low, grad_qkv_rows)
    grad_normed = project_back(grad_qkv_rows, qkv_matrix)
    input_part, grad_attn_scaling = norm_pull(grad_normed)
    grad_input = grad_middle + input_part
    return (
        grad_input,
        (grad_qkv_w, grad_out_w, grad_in_w, grad_down_w, grad_attn_scaling, grad_mlp_scaling),
    )


def block_shards(qkv_weight, out_weight, in_weight, down_weight, attn_gain, mlp_gain, block_index):
    return (
        qkv_weight[block_index].astype(jnp.bfloat16),
        out_weight[block_index].astype(jnp.bfloat16),
        in_weight[block_index].astype(jnp.bfloat16),
        down_weight[block_index].astype(jnp.bfloat16),
        attn_gain[block_index].astype(jnp.bfloat16),
        mlp_gain[block_index].astype(jnp.bfloat16),
    )


def by_einsums(
    video, frames, cotangent, qkv_weight, out_weight, in_weight, down_weight, attn_gain, mlp_gain
):
    axes = ("wide", "narrow")
    slot_counts = (frames + 1) // 2
    positions = jnp.arange(video.shape[1], dtype=jnp.int32)
    allowed = (positions[None, None, :] <= positions[None, :, None]) & (
        positions[None, None, :] < slot_counts[:, None, None]
    )
    valid_slot = (positions[None, :] < slot_counts[:, None]).astype(jnp.float32)[:, :, None, None]
    weights = (qkv_weight, out_weight, in_weight, down_weight, attn_gain, mlp_gain)
    full = [
        tuple(lax.all_gather(part, axes, axis=0, tiled=True) for part in block_shards(*weights, b))
        for b in range(2)
    ]
    spatial_out, spatial_stored = block_forward(video.astype(jnp.float32), full[0], 0, allowed)
    temporal_out, temporal_stored = block_forward(spatial_out, full[1], 1, allowed)
    output = (temporal_out * valid_slot).astype(jnp.bfloat16)
    gradient = cotangent.astype(jnp.float32) * valid_slot
    grad_between, temporal_grads = block_backward(gradient, temporal_stored, full[1], 1, allowed)
    grad_start, spatial_grads = block_backward(grad_between, spatial_stored, full[0], 0, allowed)
    summed = [
        lax.psum_scatter(jnp.stack(pair), axes, scatter_dimension=1, tiled=True)
        for pair in zip(spatial_grads, temporal_grads)
    ]
    return (output, grad_start.astype(jnp.bfloat16), *summed)


def solution(mesh):
    both = ("wide", "narrow")
    clips = P(both, None, None, None)
    rows = P(None, both, None)
    in_specs = (clips, P(both), clips, rows, rows, rows, rows, P(None, both), P(None, both))
    out_specs = (clips, clips, rows, rows, rows, rows, P(None, both), P(None, both))

    def shards(*args):
        sz = Sizes(mesh, args[0], args[5])
        whole_tiles = all(rows % 16 == 0 for rows, _ in sz.shards.values())
        if whole_tiles and sz.depth == 4 and sz.narrow == 4 and args[0].shape[0] == 1:
            return by_kernels(mesh, sz)(*args)
        return by_einsums(*args)

    return jax.shard_map(shards, mesh=mesh, in_specs=in_specs, out_specs=out_specs, check_vma=False)
```

```python
import functools

import jax
import jax.numpy as jnp
from jax import lax
from jax.experimental import pallas as pl
from jax.experimental.pallas import tpu as pltpu
from jax.sharding import PartitionSpec as P

HEADS = 8
EPS = 1e-05
BF = jnp.bfloat16
F32 = jnp.float32
MESH = pl.DeviceIdType.MESH
VMEM_LIMIT = 62 * 2**20


def dot(a, b, ca, cb):
    return lax.dot_general(a, b, (((ca,), (cb,)), ((), ())), preferred_element_type=F32)


def ds(start, size):
    if isinstance(start, int):
        return pl.ds(start, size)
    return pl.ds(pl.multiple_of(start, size), size)


def loop(count, body, first=0):
    if count - first == 1:
        body(first)
        return

    def step(i, carry):
        body(i)
        return carry

    lax.fori_loop(first, count, step, 0)


class Place:
    def __init__(self):
        self.w = lax.axis_index("wide")
        self.n = lax.axis_index("narrow")
        self.z = self.w // 2
        self.c = self.w % 2
        first = 1 + self.c
        self.na = self.flip(self.n, first)
        self.nb = self.flip(self.n, 3 - first)
        self.nab = 3 - self.n
        self.z1 = self.flip(self.z, 1)
        self.z2 = self.flip(self.z, 2)
        self.z3 = 3 - self.z
        self.others = (self.z1, self.z2, self.z3)
        self.end = (self.z == 0) | (self.z == 3)
        self.middle = (self.z == 1) | (self.z == 2)

    @staticmethod
    def flip(n, step):
        bit = (n // step) % 2
        return n + step - 2 * step * bit

    def sib(self):
        return (self.z * 2 + 1 - self.c, self.n)

    def a(self):
        return (self.w, self.na)

    def b(self):
        return (self.w, self.nb)

    def chip(self, z):
        return (z * 2 + self.c, self.n)

    def greet(self):
        targets = [self.sib(), self.a(), self.b()] + [self.chip(z) for z in self.others]
        for t in targets:
            pl.semaphore_signal(pltpu.get_barrier_semaphore(), inc=1, device_id=t, device_id_type=MESH)
        return len(targets)

    def met(self, count):
        pl.semaphore_wait(pltpu.get_barrier_semaphore(), count)


def remote(src, dst, send, recv, target):
    return pltpu.make_async_remote_copy(src, dst, send, recv, device_id=target, device_id_type=MESH)


class Gather:
    def __init__(self, place, full, send, recv, way):
        self.p, self.full, self.send, self.recv, self.way = place, full, send, recv, way
        self.sent = set()

    A, B, SIB, Z, ZA = range(5)
    @staticmethod
    def semaphores(way):
        return (5, 7) if way == 1 else (4, 5)

    @staticmethod
    def near_far(which):
        return (3, 4) if which == 0 else (5, 6)

    def go(self, out, into, index, target):
        view = self.full.at[index]
        remote(view, view, self.send.at[out], self.recv.at[into], target).start()
        self.sent.add(out)

    def take(self, slot, view):
        remote(view, view, self.send.at[0], self.recv.at[slot], self.p.sib()).wait_recv()

    def shards(self, count):
        p = self.p
        return self.full.at[p.z, p.c, p.n] if count == 1 else self.full.at[0:count, p.c, p.n]

    def pass_on(self, slot, index):
        p = self.p
        self.go(slot, slot, index, {self.A: p.a, self.B: p.b, self.SIB: p.sib}[slot]())

    def others(self, n, slots):
        p = self.p
        for z in p.others:
            for slot in slots:
                self.pass_on(slot, (z, p.c, n))

    def column(self, n, slots):
        for slot in slots:
            self.pass_on(slot, (slice(None), self.p.c, n))

    def along(self, which, n):
        p = self.p
        near, far = self.near_far(which)
        own = (p.z, p.c, n)
        self.go(self.Z + which, far, own, p.chip(p.z2))
        self.go(self.Z + which, near, own, p.chip(p.z1))

        @pl.when(p.middle)
        def _():
            self.go(self.Z + which, near, own, p.chip(p.z3))

    def relay(self, which, n):
        p = self.p
        near, far = self.near_far(which)
        self.take(far, self.shards(1))

        @pl.when(p.middle)
        def _():
            self.go(self.Z + which, near, (p.z2, p.c, n), p.chip(p.z1))

    def take_near(self, which):
        self.take(self.near_far(which)[0], self.shards(2))

    def steps(self):
        p = self.p
        A, B, SIB = self.A, self.B, self.SIB

        def start():
            own = (p.z, p.c, p.n)
            self.pass_on(A, own)
            self.pass_on(B, own)
            self.along(0, p.n)
            self.pass_on(SIB, own)

        def own_relay():
            self.relay(0, p.n)

        def own_column():
            self.take_near(0)
            self.others(p.n, (A, B, SIB))

        def column_of_a():
            self.take(A, self.shards(self.full.shape[0]))
            self.column(p.na, (B, SIB))

        def shard_of_a():
            self.take(A, self.shards(1))
            self.along(1, p.na)
            self.pass_on(B, (p.z, p.c, p.na))
            self.pass_on(SIB, (p.z, p.c, p.na))

        def own_column_late():
            self.take_near(0)
            self.others(p.n, (B, SIB))
            self.relay(1, p.na)

        def column_of_a_late():
            self.take_near(1)
            self.others(p.na, (B, SIB))

        def from_b():
            self.take(B, self.full.at[:, p.c, 0:2])
            self.column(p.nb, (SIB,))
            self.column(p.nab, (SIB,))

        def from_sib():
            self.take(SIB, self.full.at[:, p.c])

        def start_row():
            self.pass_on(A, (p.z, p.c, p.n))
            self.pass_on(B, (p.z, p.c, p.n))

        def shard_of_a_on():
            self.take(A, self.shards(1))
            self.pass_on(B, (p.z, p.c, p.na))

        near, far = self.near_far(0)
        row = (p.z, p.c)

        def row_along():
            self.take(B, self.shards(2))
            self.go(self.Z, far, row, p.chip(p.z2))
            self.go(self.Z, near, row, p.chip(p.z1))

            @pl.when(p.middle)
            def _():
                self.go(self.Z, near, row, p.chip(p.z3))

        def row_relay():
            self.take(far, self.full.at[p.z, p.c])

            @pl.when(p.middle)
            def _():
                self.go(self.Z, near, (p.z2, p.c), p.chip(p.z1))

        def rows_over():
            self.take(near, self.full.at[0:2, p.c])
            self.pass_on(SIB, (slice(None), p.c))

        if self.way == 2:
            return [start_row, shard_of_a_on, row_along, row_relay, rows_over, from_sib]
        if self.way == 1:
            return [start, shard_of_a, own_relay, own_column_late, column_of_a_late, from_b, from_sib]
        return [start, own_relay, own_column, column_of_a, from_b, from_sib]

    def finish(self):
        p, full = self.p, self.full
        if not self.sent:
            return

        def sent(slot, view):
            remote(view, view, self.send.at[slot], self.recv.at[0], p.sib()).wait_send()

        sent(self.A, self.shards(full.shape[0] if self.way == 0 else 1))
        sent(self.B, self.shards(2) if self.way == 2 else full.at[:, p.c, 0:2])
        sent(self.SIB, full.at[:, p.c])
        for which in range(2 if self.way == 1 else 1):

            @pl.when(p.middle)
            def _(which=which):
                sent(self.Z + which, full.at[:, p.c] if self.way == 2 else self.shards(4))

            @pl.when(p.end)
            def _(which=which):
                sent(self.Z + which, full.at[0:2, p.c] if self.way == 2 else self.shards(2))

        self.sent = set()

    def step(self, i):
        self.steps()[i]()


class Scatter:
    def __init__(self, place, full, from_sib, from_b, from_a, from_z, out, send, recv, way):
        self.p, self.full, self.out, self.send, self.recv = place, full, out, send, recv
        self.from_sib, self.from_b, self.from_a, self.from_z = from_sib, from_b, from_a, from_z
        self.way = way
        self.sent = set()

    @staticmethod
    def semaphores(way):
        return (5, 8) if way == 1 else (4, 6)

    @staticmethod
    def landing(full, way):
        z, _, n, r, c = full
        if way == 2:
            return [(z, n, r, c), (2, 1, r, c), (1, r, c), (4, n, r, c)]
        if way == 1:
            return [(z, n, r, c), (2, z, r, c), (1, r, c), (8, r, c)]
        return [(z, n, r, c), (2, z, r, c), (z, r, c), (4, r, c)]

    SIB, A, B, Z, ZA = range(5)
    B1 = 3

    @staticmethod
    def sum_relay(which):
        return (4, 5) if which == 0 else (6, 7)

    def go(self, out, into, src, dst, target):
        remote(src, dst, self.send.at[out], self.recv.at[into], target).start()
        self.sent.add(out)

    def take(self, slot, view):
        remote(view, view, self.send.at[0], self.recv.at[slot], self.p.sib()).wait_recv()

    def add(self, n, part):
        c = self.p.c
        for z in range(self.full.shape[0]):
            self.full[z, c, n] = self.full[z, c, n] + part(z)


    def along(self, which, n):
        p = self.p
        total, relay = self.sum_relay(which)

        def send(z, target, land, into):
            self.go(self.Z + which, into, self.full.at[z, p.c, n], self.from_z.at[4 * which + land], p.chip(target))

        @pl.when(p.end)
        def _():
            send(p.z3, p.z1, 3, relay)
            send(p.z2, p.z2, 1, total)

        @pl.when(p.middle)
        def _():
            send(p.z3, p.z3, 2, total)

        send(p.z1, p.z1, 0, total)

    def relay(self, which, n):
        p = self.p
        total, relay = self.sum_relay(which)

        @pl.when(p.middle)
        def _():
            land = self.from_z.at[4 * which + 3]
            self.take(relay, land)
            self.full[p.z2, p.c, n] = self.full[p.z2, p.c, n] + self.from_z[4 * which + 3]
            view = self.full.at[p.z2, p.c, n]
            self.go(self.Z + which, total, view, self.from_z.at[4 * which + 1], p.chip(p.z2))

    def sum_along(self, which, n, put):
        p = self.p
        total, _ = self.sum_relay(which)
        first = 4 * which

        def add_up(count):
            self.take(total, self.from_z.at[first : first + count])
            x = self.full[p.z, p.c, n].astype(F32)
            for i in range(count):
                x = x + self.from_z[first + i].astype(F32)
            put(x)

        @pl.when(p.end)
        def _():
            add_up(2)

        @pl.when(p.middle)
        def _():
            add_up(3)

    def steps(self):
        p = self.p

        def start():
            self.go(self.SIB, self.SIB, self.full.at[:, 1 - p.c], self.from_sib, p.sib())

        def other_core():
            self.take(self.SIB, self.from_sib)
            for slot, half, n in ((self.B, 0, p.nab), (self.B1, 1, p.nb)):
                self.add(n, lambda z, n=n: self.from_sib[z, n])
                self.go(self.B, slot, self.full.at[:, p.c, n], self.from_b.at[half], p.b())
            for n in (p.na, p.n):
                self.add(n, lambda z, n=n: self.from_sib[z, n])

        def partner_b():
            self.take(self.B, self.from_b.at[0])
            self.add(p.na, lambda z: self.from_b[0, z])
            if self.way == 1:
                self.along(1, p.na)
            else:
                self.go(self.A, self.A, self.full.at[:, p.c, p.na], self.from_a, p.a())
            self.take(self.B1, self.from_b.at[1])
            self.add(p.n, lambda z: self.from_b[1, z])
            if self.way == 1:
                self.along(0, p.n)

        def partner_a():
            self.take(self.A, self.from_a)
            self.add(p.n, lambda z: self.from_a[z])
            self.along(0, p.n)

        def relay():
            self.relay(0, p.n)

        def store(x):
            self.out[...] = x

        def end():
            self.sum_along(0, p.n, store)

        def relay_both():
            self.relay(1, p.na)
            self.relay(0, p.n)

        def to_a():
            def put(x):
                self.full[p.z, p.c, p.na] = x.astype(self.full.dtype)

            self.sum_along(1, p.na, put)
            self.go(self.A, self.A, self.full.at[p.z, p.c, p.na], self.from_a.at[0], p.a())
            self.sum_along(0, p.n, store)

        def end_a():
            self.take(self.A, self.from_a.at[0])
            self.out[...] = self.out[...] + self.from_a[0].astype(F32)

        total, relayed = self.sum_relay(0)

        def row(z, target, land, into):
            self.go(self.Z, into, self.full.at[z, p.c], self.from_z.at[land], p.chip(target))

        def rows_along():
            self.take(self.SIB, self.from_sib)
            for n in range(self.full.shape[2]):
                self.add(n, lambda z, n=n: self.from_sib[z, n])

            @pl.when(p.end)
            def _():
                row(p.z3, p.z1, 3, relayed)
                row(p.z2, p.z2, 1, total)

            @pl.when(p.middle)
            def _():
                row(p.z3, p.z3, 2, total)

            row(p.z1, p.z1, 0, total)

        def row_relay():
            @pl.when(p.middle)
            def _():
                self.take(relayed, self.from_z.at[3])
                for n in range(self.full.shape[2]):
                    self.full[p.z2, p.c, n] = self.full[p.z2, p.c, n] + self.from_z[3, n]
                row(p.z2, p.z2, 1, total)

        def row_to_b():
            def add_up(count):
                self.take(total, self.from_z.at[0:count])
                for n in range(self.full.shape[2]):
                    x = self.full[p.z, p.c, n].astype(F32)
                    for i in range(count):
                        x = x + self.from_z[i, n].astype(F32)
                    self.full[p.z, p.c, n] = x.astype(self.full.dtype)

            @pl.when(p.end)
            def _():
                add_up(2)

            @pl.when(p.middle)
            def _():
                add_up(3)

            for slot, half, n in ((self.B, 0, p.nab), (self.B1, 1, p.nb)):
                self.go(self.B, slot, self.full.at[p.z, p.c, n], self.from_b.at[half, 0], p.b())

        def shard_to_a():
            self.take(self.B, self.from_b.at[0, 0])
            self.full[p.z, p.c, p.na] = self.full[p.z, p.c, p.na] + self.from_b[0, 0]
            self.go(self.A, self.A, self.full.at[p.z, p.c, p.na], self.from_a.at[0], p.a())
            self.take(self.B1, self.from_b.at[1, 0])
            self.out[...] = self.full[p.z, p.c, p.n].astype(F32) + self.from_b[1, 0].astype(F32)

        if self.way == 2:
            return [start, rows_along, row_relay, row_to_b, shard_to_a, end_a]
        if self.way == 1:
            return [start, other_core, partner_b, relay_both, to_a, end_a]
        return [start, other_core, partner_b, partner_a, relay, end]

    def finish(self):
        p, full = self.p, self.full
        if not self.sent:
            return
        one, all_z, some = full.at[p.z, p.c, p.n], full.at[:, p.c, p.n], full.at[0:3, p.c, p.n]
        views = {
            self.SIB: full.at[:, p.c],
            self.A: all_z if self.way == 0 else one,
            self.B: full.at[0:2, p.c, p.n] if self.way == 2 else full.at[:, p.c, 0:2],
            self.Z: full.at[0:3, p.c] if self.way == 2 else some,
            self.ZA: some,
        }
        for slot in sorted(self.sent):
            view = views[slot]
            remote(view, view, self.send.at[slot], self.recv.at[0], p.sib()).wait_send()
        self.sent = set()

    def step(self, i):
        self.steps()[i]()


def stats(x):
    centre = jnp.mean(x, axis=-1, keepdims=True)
    centred = x - centre
    spread = jnp.mean(centred * centred, axis=-1, keepdims=True)
    r = lax.rsqrt(spread + EPS)
    return centred * r, r


def norm_into(src, gain, dst, rows):
    total = src.shape[0]

    def body(i):
        at = ds(i * rows, rows)
        xn, _ = stats(src[at, :].astype(F32))
        dst[at, :] = (xn * gain).astype(BF)

    loop(total // rows, body)


def halves(shape):
    return lax.broadcasted_iota(jnp.int32, shape, 1) < shape[1] // 2


def split_heads(x):
    low = halves(x.shape)
    zero = jnp.zeros_like(x)
    return jnp.concatenate([jnp.where(low, x, zero), jnp.where(low, zero, x)], 0)


def head_ones(keys):
    shape = (2 * keys, LANES)
    row = lax.broadcasted_iota(jnp.int32, shape, 0) < keys
    low = lax.broadcasted_iota(jnp.int32, shape, 1) < LANES // 2
    return jnp.where(row == low, 1.0, 0.0).astype(BF)


def unroll(first, last, body):
    for i in range(first, last):
        body(i)


def spatial_forward(qkv, probs, att, patches, width, first, last):
    head = width // HEADS
    scale = head ** -0.5
    pairs = range(HEADS // 2)
    ones = head_ones(patches)

    def body(s):
        at = ds(s * patches, patches)
        parts = []
        for pair in pairs:
            lane = pair * 2 * head
            q = qkv[at, lane : lane + 2 * head]
            parts.append(dot(q, split_heads(qkv[at, width + lane : width + lane + 2 * head]), 1, 1))
        scores = jnp.concatenate(parts, 0) * scale
        low = halves(scores.shape)
        top0 = jnp.max(jnp.where(low, scores, -jnp.inf), axis=-1, keepdims=True)
        top1 = jnp.max(jnp.where(low, -jnp.inf, scores), axis=-1, keepdims=True)
        e = jnp.exp(scores - jnp.where(low, top0, top1))
        e_low = e.astype(BF)
        parts = []
        for pair in pairs:
            lane = pair * 2 * head
            v2 = split_heads(qkv[at, 2 * width + lane : 2 * width + lane + 2 * head])
            rows = slice(pair * patches, (pair + 1) * patches)
            parts.append(dot(e_low[rows], jnp.concatenate([v2, ones], 1), 1, 0))
        both = jnp.concatenate(parts, 0)
        r = 1.0 / both[:, 2 * head :]
        probs[s] = (e * r).astype(BF).reshape(HEADS // 2, patches, 2 * patches)
        new = (both[:, : 2 * head] * r).astype(BF)
        for pair in pairs:
            att[at, pair * 2 * head : (pair + 1) * 2 * head] = new[pair * patches : (pair + 1) * patches]

    unroll(first, last, body)


def pad_heads(x, lanes):
    low = halves(x.shape)
    zero = jnp.zeros_like(x)
    fill = jnp.zeros((lanes - x.shape[0], x.shape[1]), x.dtype)
    return jnp.concatenate([jnp.where(low, x, zero), fill, jnp.where(low, zero, x), fill], 0).astype(BF)


LANES = 128
SUB = 8


def temporal_forward(qkv, probs, att, bias, slots, width, first, last):
    head = width // HEADS
    scale = head ** -0.5
    group = slots * SUB
    pairs = range(HEADS // 2)
    parts_of = [slice(half * group, (half + 1) * group) for half in range(2)]

    def body(i):
        at = ds(i * 2 * group, 2 * group)
        parts = []
        for pair in pairs:
            lane = pair * 2 * head
            q = qkv[at, lane : lane + 2 * head].astype(F32)
            k = qkv[at, width + lane : width + lane + 2 * head].astype(F32)
            for rows in parts_of:
                x = dot(q[rows].astype(BF), pad_heads(k[rows], LANES), 1, 1)
                parts += [x[:, :LANES], x[:, LANES:]]
        scores = jnp.stack(parts, 0) * scale + bias[...][None]
        e = jnp.exp(scores - jnp.max(scores, axis=-1, keepdims=True))
        p = (e / jnp.sum(e, axis=-1, keepdims=True)).astype(BF)
        for pair in pairs:
            lane = pair * 2 * head
            v = qkv[at, 2 * width + lane : 2 * width + lane + 2 * head].astype(F32)
            out = []
            for half, rows in enumerate(parts_of):
                j = (pair * 2 + half) * 2
                both = jnp.concatenate([p[j], p[j + 1]], 1)
                probs[i * 2 + half, pair] = both
                out.append(dot(both, pad_heads(v[rows], LANES), 1, 0))
            att[at, lane : lane + 2 * head] = jnp.concatenate(out, 0).astype(BF)

    unroll(first, last, body)


def make_bias(bias, count, slots):
    group = slots * SUB
    q = lax.broadcasted_iota(jnp.int32, (group, LANES), 0)
    k = lax.broadcasted_iota(jnp.int32, (group, LANES), 1)
    sq, sk = q // SUB, k // SUB
    ok = (q - sq * SUB == k - sk * SUB) & (sk <= sq) & (sk < count)
    bias[...] = jnp.where(ok, 0.0, -1e9)


def gelu_pair(z):
    k0 = 0.7978845608028654
    k1 = k0 * 0.044715
    z2 = z * z
    half = 0.5 + 0.5 * jnp.tanh(z * (k0 + k1 * z2))
    active = z * half
    slope = half + half * (z - active) * (2.0 * k0 + 6.0 * k1 * z2)
    return active, slope


def wide_rows(ref, width, columns=None):
    x = ref[...] if columns is None else ref[:, :, :, :, columns]
    return x.reshape(width, x.shape[-1])


def unsplit_heads(x, second, rows):
    low = halves((rows, x.shape[1]))
    return jnp.where(low, x[:rows], x[second : second + rows])


def spatial_backward(qkv, probs, grad, patches, width, first, last):
    head = width // HEADS
    scale = head ** -0.5
    pairs = range(HEADS // 2)
    rows_of = [slice(pair * patches, (pair + 1) * patches) for pair in pairs]

    def body(s):
        at = ds(s * patches, patches)
        cols = [[slice(t * width + p * 2 * head, t * width + (p + 1) * 2 * head) for t in range(3)] for p in pairs]
        p_low = probs[s].reshape(HEADS // 2 * patches, 2 * patches)
        soft = p_low.astype(F32)
        q = [qkv[at, cols[p][0]] for p in pairs]
        k2 = [split_heads(qkv[at, cols[p][1]]) for p in pairs]
        g = [grad[at, p * 2 * head : (p + 1) * 2 * head] for p in pairs]
        gp = [dot(g[p], split_heads(qkv[at, cols[p][2]]), 1, 1) for p in pairs]
        gv = [dot(p_low[rows_of[p]], g[p], 0, 0) for p in pairs]
        gp = jnp.concatenate(gp, 0)
        low = halves(gp.shape)
        both = gp * soft
        sum0 = jnp.sum(jnp.where(low, both, 0.0), axis=-1, keepdims=True)
        sum1 = jnp.sum(jnp.where(low, 0.0, both), axis=-1, keepdims=True)
        gs = (soft * (gp - jnp.where(low, sum0, sum1))).astype(BF)
        gq = [dot(gs[rows_of[p]], k2[p], 1, 0) for p in pairs]
        gk = [dot(gs[rows_of[p]], q[p], 0, 0) for p in pairs]
        for p in pairs:
            qkv[at, cols[p][0]] = (gq[p] * scale).astype(BF)
            qkv[at, cols[p][1]] = (unsplit_heads(gk[p], patches, patches) * scale).astype(BF)
            qkv[at, cols[p][2]] = unsplit_heads(gv[p], patches, patches).astype(BF)

    unroll(first, last, body)


def temporal_backward(qkv, probs, grad, slots, width, first, last):
    head = width // HEADS
    scale = head ** -0.5
    group = slots * SUB
    pairs = range(HEADS // 2)
    parts_of = [slice(half * group, (half + 1) * group) for half in range(2)]

    def body(i):
        at = ds(i * 2 * group, 2 * group)
        cols = [[slice(t * width + p * 2 * head, t * width + (p + 1) * 2 * head) for t in range(3)] for p in pairs]
        qs, ks, gs_in, ps, gp, soft = [], [], [], [], [], []
        for pair in pairs:
            q, k, v = (qkv[at, c].astype(F32) for c in cols[pair])
            g = grad[at, pair * 2 * head : (pair + 1) * 2 * head].astype(F32)
            for half, rows in enumerate(parts_of):
                qs.append(q[rows].astype(BF))
                ks.append(pad_heads(k[rows], LANES))
                gs_in.append(g[rows].astype(BF))
                p = probs[i * 2 + half, pair]
                ps.append(p)
                x = dot(gs_in[-1], pad_heads(v[rows], LANES), 1, 1)
                wide = p.astype(F32)
                gp += [x[:, :LANES], x[:, LANES:]]
                soft += [wide[:, :LANES], wide[:, LANES:]]
        many = range(len(ps))
        gv = [unsplit_heads(dot(ps[j], gs_in[j], 0, 0), LANES, group) for j in many]
        gp = jnp.stack(gp, 0)
        soft = jnp.stack(soft, 0)
        delta = jnp.sum(gp * soft, axis=-1, keepdims=True)
        gs = (soft * (gp - delta)).astype(BF)
        gs = [jnp.concatenate([gs[2 * j], gs[2 * j + 1]], 1) for j in many]
        gq = [dot(gs[j], ks[j], 1, 0) * scale for j in many]
        gk = [unsplit_heads(dot(gs[j], qs[j], 0, 0), LANES, group) * scale for j in many]
        for pair in pairs:
            for c, outs in zip(cols[pair], (gq, gk, gv)):
                qkv[at, c] = jnp.concatenate(outs[2 * pair : 2 * pair + 2], 0).astype(BF)

    unroll(first, last, body)


def norm_back(src, grad, gain, base, dst, low, sums, rows):
    total, width = grad.shape
    sums[...] = jnp.zeros_like(sums)

    def body(i):
        at = ds(i * rows, rows)
        xn, r = stats(src[at, :].astype(F32))
        g = grad[at, :]
        e = g * gain
        inner = e - jnp.mean(e, axis=-1, keepdims=True) - xn * jnp.mean(e * xn, axis=-1, keepdims=True)
        res = base[at, :] + r * inner
        if dst is not None:
            dst[at, :] = res
        low[at, :] = res.astype(BF)
        sums[...] += jnp.sum((g * xn).reshape(rows // SUB, SUB, width), axis=0)

    loop(total // rows, body)


def gain_row(gains, which):
    return gains[which : which + 1, :]


class Sizes:
    def __init__(self, mesh, video, in_weight):
        self.depth = mesh.shape["wide"] // 2
        self.narrow = mesh.shape["narrow"]
        self.slots, self.patches, self.width = video.shape[1:]
        self.hidden = in_weight.shape[2]
        self.tokens = self.slots * self.patches
        self.group = self.slots * SUB
        devices = 2 * self.depth * self.narrow
        w = self.width // devices
        self.shards = {
            "qkv": (w, 3 * self.width),
            "out": (w, self.width),
            "in": (w, self.hidden),
            "down": (self.hidden // devices, self.width),
        }
        self.mesh_dims = (self.depth, 2, self.narrow)

    def full(self, name):
        return self.mesh_dims + (TILE_GAIN if name == "gain" else self.shards[name])

    def acts(self, b):
        t, w, f = self.tokens, self.width, self.hidden
        pairs = HEADS // 2
        if b == 0:
            probs = (self.slots, pairs, self.patches, 2 * self.patches)
        else:
            probs = (self.patches // SUB, pairs, self.group, 2 * LANES)
        return {
            "normed": ((t, w), BF),
            "qkv": ((t, 3 * w), BF),
            "probs": (probs, BF),
            "att": ((t, w), BF),
            "middle": ((t, w), F32),
            "mlp": ((t, w), BF),
            "active": ((t, f), BF),
            "slope": ((t, f), BF),
        }


TILE_GAIN = (16, LANES)
NAMES = ("qkv", "out", "in", "down")
ACTS = ("normed", "qkv", "probs", "att", "middle", "mlp", "active", "slope")
SPLIT = {"gain": 1, "qkv": 2, "out": 1, "in": 2, "down": 2}


def pieces_of(name, b):
    return [(name, b, i) for i in range(SPLIT[name])]


GAIN = ("gain", 0)
GATHER_ORDER = [(*GAIN, 0)] + [piece for b in range(2) for name in NAMES for piece in pieces_of(name, b)]
SCATTER_ORDER = [
    piece for b in (1, 0) for name in ("down", "in", "out", "qkv") for piece in pieces_of(name, b)
] + [(*GAIN, 0)]


def columns_of(piece, columns):
    name, _, i = piece
    part = columns // SPLIT[name]
    return slice(i * part, (i + 1) * part)


def row_tile(tokens):
    return tokens // 2 if tokens % 32 == 0 else tokens


def keys_of_weights():
    return [(name, b) for b in range(2) for name in NAMES]


KEPT = ("normed", "qkv", "att", "middle", "mlp", "active", "slope")


def layer_kernel(sz, *refs):
    refs = list(refs)

    def grab(n):
        taken, refs[:n] = refs[:n], []
        return taken

    video, cotangent, slot_count, attn_gain, mlp_gain = grab(5)
    shard = dict(zip(NAMES, grab(4)))
    out, grad_video = grab(2)
    outs = dict(zip(NAMES, grab(4)))
    gain_outs = grab(2)
    acts_hbm = dict(zip(KEPT, grab(len(KEPT))))
    acts = dict(zip(ACTS, grab(8)))
    probs1, h1 = grab(2)
    full = dict(zip([GAIN] + keys_of_weights(), grab(9)))
    grads = dict(zip([(name, 1) for name in NAMES] + [GAIN], grab(5)))
    landing = {piece: grab(4) for piece in SCATTER_ORDER}
    gains, bias, gain_out, grad, grad_mid, grad_norm, low, grad_att, sums = grab(9)
    gather_send, gather_recv, scatter_send, scatter_recv, local = grab(5)
    assert not refs
    for name in NAMES:
        grads[(name, 0)] = full[(name, 1)]

    place = Place()
    met = place.greet()

    def part_of(ref, piece, columns):
        if SPLIT[piece[0]] == 1:
            return ref
        return ref.at[(slice(None),) * (len(ref.shape) - 1) + (columns_of(piece, columns),)]

    gathers = {}
    at_send = at_recv = 0
    for k, piece in enumerate(GATHER_ORDER):
        n_send, n_recv = Gather.semaphores(GATHER_WAYS[k])
        ref = full[piece[:2]]
        sems = [gather_send.at[at_send : at_send + n_send], gather_recv.at[at_recv : at_recv + n_recv]]
        gathers[piece] = Gather(place, part_of(ref, piece, ref.shape[-1]), *sems, GATHER_WAYS[k])
        at_send += n_send
        at_recv += n_recv
    scatters = {}
    at_send = at_recv = 0
    for k, piece in enumerate(SCATTER_ORDER):
        n_send, n_recv = Scatter.semaphores(SCATTER_WAYS[k])
        ref = grads[piece[:2]]
        columns = ref.shape[-1]
        target = gain_out if piece[:2] == GAIN else outs[piece[0]].at[piece[1]]
        sems = [scatter_send.at[at_send : at_send + n_send], scatter_recv.at[at_recv : at_recv + n_recv]]
        scatters[piece] = Scatter(
            place,
            part_of(ref, piece, columns),
            *landing[piece],
            part_of(target, piece, columns),
            *sems,
            SCATTER_WAYS[k],
        )
        at_send += n_send
        at_recv += n_recv
    own = (place.z, place.c, place.n)
    full[GAIN][own] = place_gains(attn_gain, mlp_gain, place.w * sz.narrow + place.n)
    for key in keys_of_weights():
        full[key][own] = shard[key[0]][key[1]].astype(BF)
    place.met(met)

    moving = {}

    def move(name, src, dst):
        copy = pltpu.make_async_copy(src, dst, local.at[KEPT.index(name)])
        copy.start()
        moving[name] = copy

    def settle(*names):
        for name in names:
            if name in moving:
                moving.pop(name).wait()

    def act(name, b):
        return probs1 if (name, b) == ("probs", 1) else acts[name]

    def keep(b, *names):
        for name in names:
            if b == 0 and name in KEPT:
                move(name, acts[name], acts_hbm[name])

    def fetch(b, *names):
        for name in names:
            if b == 1 and name in KEPT:
                settle(name)
                move(name, acts_hbm[name], acts[name])

    count = slot_count[0]
    t, w = sz.tokens, sz.width

    def stage_gain():
        make_bias(bias, count, sz.slots)
        tile = jnp.sum(full[GAIN][...].astype(F32).reshape(-1, 16, LANES), axis=0)
        for g in range(4):
            rows = [tile[g * 4 + r : g * 4 + r + 1, :] for r in range(w // LANES)]
            gains[g : g + 1, :] = jnp.concatenate(rows, 1)

    def forward_stages(b):
        a = {name: act(name, b) for name in ACTS}
        h = video if b == 0 else h1

        def norm1():
            settle("normed")
            norm_into(h, gain_row(gains, 2 * b), a["normed"], row_tile(t))
            keep(b, "normed")

        def qkv(first, last):
            settle("qkv")
            at = slice(first, last)
            a["qkv"][:, at] = dot(a["normed"][...], wide_rows(full[("qkv", b)], w, at), 1, 0).astype(BF)
            if last == 3 * w:
                keep(b, "qkv")

        def attend(first, last):
            settle("att")
            if b == 0:
                spatial_forward(a["qkv"], a["probs"], a["att"], sz.patches, w, first, last)
                end = sz.slots
            else:
                temporal_forward(a["qkv"], a["probs"], a["att"], bias, sz.slots, w, first, last)
                end = sz.patches // (2 * SUB)
            if last == end:
                keep(b, "probs", "att")

        def project():
            settle("middle")
            new = dot(a["att"][...], wide_rows(full[("out", b)], w), 1, 0)
            a["middle"][...] = h[...].astype(F32) + new
            keep(b, "middle")

        def norm2():
            settle("mlp")
            norm_into(a["middle"], gain_row(gains, 2 * b + 1), a["mlp"], row_tile(t))
            keep(b, "mlp")

        def expand(first, last):
            at = slice(first, last)
            settle("active", "slope")
            weight = wide_rows(full[("in", b)], w, at)
            rows = row_tile(t)
            for r in range(0, t, rows):
                active, slope = gelu_pair(dot(a["mlp"][r : r + rows, :], weight, 1, 0))
                a["active"][r : r + rows, at] = active.astype(BF)
                a["slope"][r : r + rows, at] = slope.astype(BF)
            if last == sz.hidden:
                keep(b, "active", "slope")

        def contract(first, last):
            at = slice(first, last)
            new = a["middle"][:, at] + dot(a["active"][...], wide_rows(full[("down", b)], sz.hidden, at), 1, 0)
            if b == 0:
                new = new.reshape(sz.slots, sz.patches // SUB, SUB, last - first)
                for s in range(sz.slots):
                    h1_view[:, s * SUB : (s + 1) * SUB, at] = new[s]
            else:
                valid = lax.broadcasted_iota(jnp.int32, (sz.slots, 1, 1), 0) < count
                new = new.reshape(sz.patches // (2 * SUB), 2, sz.slots, SUB, last - first)
                for i in range(sz.patches // (2 * SUB)):
                    rows = jnp.concatenate([new[i, 0], new[i, 1]], axis=1)
                    out[:, i * 2 * SUB : (i + 1) * 2 * SUB, at] = jnp.where(valid, rows, 0.0).astype(BF)
                if last == w:
                    fetch(b, "active", "middle")

        n_a = sz.slots if b == 0 else sz.patches // (2 * SUB)
        cuts = [-(-n_a * i // 4) for i in range(5)]
        todo = [norm1]
        todo += [functools.partial(qkv, 3 * w * i // 2, 3 * w * (i + 1) // 2) for i in range(2)]
        todo += [functools.partial(attend, cuts[i], cuts[i + 1]) for i in range(4)]
        todo += [project, norm2]
        todo += [functools.partial(expand, sz.hidden * i // 4, sz.hidden * (i + 1) // 4) for i in range(4)]
        last = [functools.partial(contract, w * i // 2, w * (i + 1) // 2) for i in range(2)]
        return todo, last

    h1_view = h1.reshape(sz.patches // SUB, sz.group, w)

    def start():
        valid = lax.broadcasted_iota(jnp.int32, (sz.slots, 1, 1), 0) < count

        def body(i):
            rows = cotangent[:, ds(i * 2 * SUB, 2 * SUB), :].astype(F32)
            rows = jnp.where(valid, rows, 0.0)
            both = [rows[:, half * SUB : (half + 1) * SUB, :].reshape(sz.group, w) for half in range(2)]
            rows = jnp.concatenate(both, 0)
            at = ds(i * 2 * sz.group, 2 * sz.group)
            grad[at, :] = rows
            low[at, :] = rows.astype(BF)

        loop(sz.patches // (2 * SUB), body)

    def put_gain(which):
        row = jnp.sum(sums[...], axis=0, keepdims=True)
        per = w // LANES
        tile = jnp.concatenate([row[:, r * LANES : (r + 1) * LANES] for r in range(per)], 0)
        gain_rows[which * per : (which + 1) * per, :] = tile

    gain_rows = gain_out

    def backward_stages(b):
        a = {name: act(name, b) for name in ACTS}

        half = sz.hidden // 2
        z_half = sz.depth // 2

        def down_grad(i):
            settle("active")
            if b == 0 and i == 0:
                for gather in gathers.values():
                    gather.finish()
            at = slice(i * w // 2, (i + 1) * w // 2)
            g = dot(a["active"][...], low[:, at], 0, 0).astype(BF)
            grads[("down", b)][:, :, :, :, at] = g.reshape(sz.full("down")[:-1] + (w // 2,))

        def hidden_back(i):
            settle("slope")
            at = slice(i * half, (i + 1) * half)
            weight = full[("down", b)][i * z_half : (i + 1) * z_half].reshape(half, w)
            a["slope"][:, at] = (dot(low[...], weight, 1, 1) * a["slope"][:, at].astype(F32)).astype(BF)

        def in_grad(i):
            settle("mlp")
            at = slice(i * half, (i + 1) * half)
            g = dot(a["mlp"][...], a["slope"][:, at], 0, 0).astype(BF)
            grads[("in", b)][:, :, :, :, at] = g.reshape(sz.full("in")[:-1] + (half,))
            if i == 1:
                fetch(b, "mlp")

        def back_rows(src, weight, put):
            put(dot(src[...], wide_rows(weight, w), 1, 1))

        def mlp_back():

            def put(x):
                grad_norm[...] = x

            back_rows(a["slope"], full[("in", b)], put)
            fetch(b, "slope")

        def norm2_back():
            settle("middle")
            norm_back(a["middle"], grad_norm, gain_row(gains, 2 * b + 1), grad, grad_mid, low, sums, row_tile(t))
            put_gain(2 * b + 1)

        def out_grad():
            settle("att")

            g = dot(a["att"][...], low[...], 0, 0).astype(BF)
            grads[("out", b)][...] = g.reshape(sz.full("out"))
            fetch(b, "att")

        def att_back():

            def put(x):
                grad_att[...] = x.astype(BF)

            back_rows(low, full[("out", b)], put)

        def attend(first, last):
            settle("qkv", "probs")
            if b == 0:
                spatial_backward(a["qkv"], a["probs"], grad_att, sz.patches, w, first, last)
            else:
                temporal_backward(a["qkv"], a["probs"], grad_att, sz.slots, w, first, last)

        def qkv_grad(first, last):
            settle("normed")
            at = slice(first, last)
            g = dot(a["normed"][...], a["qkv"][:, at], 0, 0).astype(BF)
            grads[("qkv", b)][:, :, :, :, at] = g.reshape(sz.full("qkv")[:-1] + (last - first,))
            if last == 3 * w:
                fetch(b, "normed")

        def qkv_back():

            def put(x):
                grad_norm[...] = x

            back_rows(a["qkv"], full[("qkv", b)], put)
            fetch(b, "qkv")

        def norm1_back():
            src = h1 if b == 1 else video
            if b == 1:
                norm_back(src, grad_norm, gain_row(gains, 2), grad_mid, grad, low, sums, row_tile(t))
            else:
                norm_back(src, grad_norm, gain_row(gains, 0), grad_mid, None, low, sums, row_tile(t))
                grad_video[...] = low[...].reshape(grad_video.shape)
            put_gain(2 * b)

        def reorder():
            view = grad.reshape(sz.patches // SUB, sz.group, w)

            def body(s):
                rows = view[:, ds(s * SUB, SUB), :].reshape(sz.patches, w)
                at = ds(s * sz.patches, sz.patches)
                grad_norm[at, :] = rows
                low[at, :] = rows.astype(BF)

            loop(sz.slots, body)
            grad[...] = grad_norm[...]

        n_a = sz.slots if b == 0 else sz.patches // (2 * SUB)
        cuts = [-(-n_a * i // 4) for i in range(5)]
        todo = []
        for piece in (down_grad, hidden_back, in_grad):
            todo += [functools.partial(piece, i) for i in range(2)]
        todo += [mlp_back, norm2_back, out_grad, att_back]
        todo += [functools.partial(attend, cuts[i], cuts[i + 1]) for i in range(4)]
        todo += [functools.partial(qkv_grad, 3 * w * i // 2, 3 * w * (i + 1) // 2) for i in range(2)]
        if b == 1:
            todo += output
        todo += [qkv_back, norm1_back]
        if b == 1:
            todo += [reorder]
        return todo

    def spread_gain():
        tile = gain_out[...]
        grads[GAIN][...] = jnp.broadcast_to(tile, sz.full("gain"))

    first, last = forward_stages(0)
    second, output = forward_stages(1)
    work = [start, stage_gain] + first + last + second
    work = iter(work + backward_stages(1) + backward_stages(0) + [spread_gain])
    steps = [gathers[piece] for piece in GATHER_ORDER] + [scatters[piece] for piece in SCATTER_ORDER]
    for op in PLAN:
        if op < 0:
            next(work)()
        else:
            steps[op // 8].step(op % 8)
    assert next(work, None) is None
    pick_gains(gain_out[...], gain_outs, place.w * sz.narrow + place.n)
    settle(*KEPT)
    for scatter in scatters.values():
        scatter.finish()


def place_gains(attn_gain, mlp_gain, index):
    own = attn_gain.shape[1]
    per = LANES // own
    row = lax.broadcasted_iota(jnp.int32, (TILE_GAIN[0] // 4, LANES), 0)
    lane = lax.broadcasted_iota(jnp.int32, (TILE_GAIN[0] // 4, LANES), 1) // own
    here = row * per + lane == index
    tiles = []
    for b in range(2):
        for ref in (attn_gain, mlp_gain):
            values = jnp.concatenate([ref[b : b + 1, :]] * per, 1)
            tiles.append(jnp.where(here, values, 0.0))
    return jnp.concatenate(tiles, 0).astype(BF)


def pick_gains(tile, outs, index):
    own = outs[0].shape[1]
    per = LANES // own
    rows = TILE_GAIN[0] // 4
    row = lax.broadcasted_iota(jnp.int32, (rows, own), 0)
    for b in range(2):
        for kind, out in enumerate(outs):
            first = (2 * b + kind) * rows
            total = jnp.zeros((rows, own), F32)
            for j in range(per):
                piece = tile[first : first + rows, j * own : (j + 1) * own]
                total = total + jnp.where(row * per + j == index, piece, 0.0)
            out[b : b + 1, :] = jnp.sum(total, axis=0, keepdims=True)


PLAN = (
    112, 8, 48, 0, 24, 16, 1, 9, 64, 40, 104, 17, 88, 113, 49, 2, 10, 41, 25, 32, 72, 80, 18, 65, 3, 33, 96,
    26, 56, 11, 19, -1, 27, 57, 73, 81, 4, 42, 50, 34, 12, 5, -1, -1, 13, -1, 20, 21, -1, 58, 28, -1, 35, 89,
    97, 74, 51, -1, 66, -1, 43, 59, -1, 29, -1, -1, 75, 82, 90, 36, 37, -1, -1, 67, 44, 52, 98, 45, -1, 105,
    -1, 60, 83, 114, 91, 53, -1, 61, -1, 68, 99, 106, 76, -1, 69, -1, 77, -1, -1, -1, 84, -1, -1, 92, 115,
    107, 85, -1, -1, 100, 93, -1, -1, 101, -1, -1, 108, 116, -1, 120, -1, 128, 109, 117, -1, -1, 129, 121,
    -1, 136, -1, 144, -1, -1, -1, 152, 145, -1, -1, 153, -1, -1, 137, 130, 122, -1, -1, 160, -1, 168, 146,
    -1, 161, -1, -1, 169, -1, -1, 138, -1, 176, 154, 162, -1, 184, 123, 147, 177, -1, -1, -1, 192, 185, 139,
    -1, 200, -1, 193, 178, -1, 124, 201, -1, 208, 163, -1, 170, -1, 209, -1, 179, 186, -1, -1, -1, 216, 194,
    202, -1, 224, 217, 140, -1, -1, 187, 225, -1, 232, 203, 233, 188, 148, 210, 218, 226, 234, 131, 155, 171,
    195, 211, 219, 227, 235, 132, 156, 164, 172, 180, 196, 204, 212, 220, 228, 236, 125, 133, 141, 149, 157,
    165, 173, 181, 189, 197, 205, 213, 221, 229, 237,
)
GATHER_WAYS = (
    0, 0, 0, 0, 0, 0, 2, 0, 2, 0, 0, 0, 0, 0, 2,
)
SCATTER_WAYS = (
    0, 2, 0, 1, 2, 0, 2, 1, 0, 1, 0, 0, 1, 0, 0,
)


def by_kernels(mesh, sz):
    vmem = pl.BlockSpec(memory_space=pltpu.VMEM)
    smem = pl.BlockSpec(memory_space=pltpu.SMEM)
    anyw = pl.BlockSpec(memory_space=pl.ANY)
    shape = jax.ShapeDtypeStruct
    t, w = sz.tokens, sz.width
    acts0 = sz.acts(0)
    clip_shape = shape((sz.slots, sz.patches, w), BF)
    dma = pltpu.SemaphoreType.DMA

    def landing(k, piece):
        full = sz.full(piece[0])
        full = full[:-1] + (full[-1] // SPLIT[piece[0]],)
        kind = F32 if piece[0] == "gain" else BF
        return [pltpu.VMEM(s, kind) for s in Scatter.landing(full, SCATTER_WAYS[k])]

    def run(video, frames, cotangent, qkv_weight, out_weight, in_weight, down_weight, attn_gain, mlp_gain):
        gain_shape = shape(attn_gain.shape, F32)
        shapes = [clip_shape, clip_shape]
        shapes += [shape((2,) + sz.shards[name], F32) for name in NAMES]
        shapes += [gain_shape, gain_shape]
        n_gather = [sum(Gather.semaphores(way)[i] for way in GATHER_WAYS) for i in range(2)]
        n_scatter = [sum(Scatter.semaphores(way)[i] for way in SCATTER_WAYS) for i in range(2)]
        res = pl.pallas_call(
            functools.partial(layer_kernel, sz),
            out_shape=shapes + [shape(*acts0[name]) for name in KEPT],
            in_specs=[vmem, vmem, smem] + [vmem] * 6,
            out_specs=[vmem] * len(shapes) + [anyw] * len(KEPT),
            scratch_shapes=[pltpu.VMEM(*acts0[name]) for name in ACTS]
            + [pltpu.VMEM(*sz.acts(1)["probs"]), pltpu.VMEM((t, w), F32)]
            + [pltpu.VMEM(sz.full(name), BF) for name, _ in [GAIN] + keys_of_weights()]
            + [pltpu.VMEM(sz.full(name), BF) for name in NAMES]
            + [pltpu.VMEM(sz.full("gain"), F32)]
            + [buffer for k, piece in enumerate(SCATTER_ORDER) for buffer in landing(k, piece)]
            + [
                pltpu.VMEM((4, w), F32),
                pltpu.VMEM((sz.group, LANES), F32),
                pltpu.VMEM(TILE_GAIN, F32),
                pltpu.VMEM((t, w), F32),
                pltpu.VMEM((t, w), F32),
                pltpu.VMEM((t, w), F32),
                pltpu.VMEM((t, w), BF),
                pltpu.VMEM((t, w), BF),
                pltpu.VMEM((SUB, w), F32),
                dma((n_gather[0],)),
                dma((n_gather[1],)),
                dma((n_scatter[0],)),
                dma((n_scatter[1],)),
                dma((len(KEPT),)),
            ],
            compiler_params=pltpu.CompilerParams(
                collective_id=0, has_side_effects=True, vmem_limit_bytes=VMEM_LIMIT
            ),
        )(
            video.reshape(t, w),
            cotangent.reshape(clip_shape.shape),
            (frames + 1) // 2,
            attn_gain,
            mlp_gain,
            qkv_weight,
            out_weight,
            in_weight,
            down_weight,
        )
        res = res[: len(shapes)]
        return (res[0].reshape(video.shape), res[1].reshape(video.shape), *res[2:])

    return run


def norm_rows(inputs, scaling):
    centre = jnp.mean(inputs, axis=-1, keepdims=True)
    centred = inputs - centre
    spread = jnp.mean(centred * centred, axis=-1, keepdims=True)
    return centred * lax.rsqrt(spread + EPS) * scaling


def project(rows_in, matrix):
    return jnp.einsum("cspd,de->cspe", rows_in, matrix, preferred_element_type=jnp.float32)


def project_back(rows_in, matrix):
    return jnp.einsum("cspe,de->cspd", rows_in, matrix, preferred_element_type=jnp.float32)


def weight_grad(left, right):
    return jnp.einsum("cspd,cspe->de", left, right, preferred_element_type=jnp.float32)


def pair_scores(first, second, which_block):
    if which_block == 0:
        return jnp.einsum("csphe,csqhe->cshpq", first, second, preferred_element_type=jnp.float32)
    return jnp.einsum("csphe,ctphe->cphst", first, second, preferred_element_type=jnp.float32)


def pair_mix(weighting, second, which_block):
    if which_block == 0:
        return jnp.einsum(
            "cshpq,csqhe->csphe", weighting, second, preferred_element_type=jnp.float32
        )
    return jnp.einsum("cphst,ctphe->csphe", weighting, second, preferred_element_type=jnp.float32)


def pair_back(weighting, first, which_block):
    if which_block == 0:
        return jnp.einsum(
            "cshpq,csphe->csqhe", weighting, first, preferred_element_type=jnp.float32
        )
    return jnp.einsum("cphst,csphe->ctphe", weighting, first, preferred_element_type=jnp.float32)


def masked_scores(queries, key_rows, which_block, allowed):
    head_size = queries.shape[-1]
    scores = pair_scores(queries, key_rows, which_block) * head_size ** (-0.5)
    if which_block == 1:
        scores = jnp.where(allowed[:, None, None], scores, -1000000000.0)
    return scores


def block_forward(inputs, weights, which_block, allowed):
    qkv_matrix, out_matrix, in_matrix, down_matrix, attn_scaling, mlp_scaling = weights
    full_shape = inputs.shape
    head_size = full_shape[-1] // HEADS
    normed, norm_pull = jax.vjp(norm_rows, inputs, attn_scaling.astype(jnp.float32))
    normed_low = normed.astype(jnp.bfloat16)
    qkv_rows = project(normed_low, qkv_matrix).astype(jnp.bfloat16)
    split = qkv_rows.reshape(full_shape[:3] + (3, HEADS, head_size))
    queries = split[:, :, :, 0]
    key_rows = split[:, :, :, 1]
    value_rows = split[:, :, :, 2]
    scores = masked_scores(queries, key_rows, which_block, allowed)
    row_max = jnp.max(scores, axis=-1, keepdims=True)
    shifted = jnp.exp(scores - row_max)
    row_sum = jnp.sum(shifted, axis=-1, keepdims=True)
    log_total = row_max + jnp.log(row_sum)
    probs_low = (shifted / row_sum).astype(jnp.bfloat16)
    attended = pair_mix(probs_low, value_rows, which_block).reshape(full_shape).astype(jnp.bfloat16)
    middle = inputs + project(attended, out_matrix)
    normed_mlp, mlp_pull = jax.vjp(norm_rows, middle, mlp_scaling.astype(jnp.float32))
    normed_mlp_low = normed_mlp.astype(jnp.bfloat16)
    hidden = project(normed_mlp_low, in_matrix)
    active, gelu_pull = jax.vjp(jax.nn.gelu, hidden)
    active_low = active.astype(jnp.bfloat16)
    result = middle + project(active_low, down_matrix)
    stored = (
        norm_pull,
        normed_low,
        queries,
        key_rows,
        value_rows,
        log_total,
        attended,
        mlp_pull,
        normed_mlp_low,
        gelu_pull,
        active_low,
    )
    return (result, stored)


def block_backward(gradient, stored, weights, which_block, allowed):
    qkv_matrix, out_matrix, in_matrix, down_matrix, attn_scaling, mlp_scaling = weights
    (
        norm_pull,
        normed_low,
        queries,
        key_rows,
        value_rows,
        log_total,
        attended,
        mlp_pull,
        normed_mlp_low,
        gelu_pull,
        active_low,
    ) = stored
    full_shape = gradient.shape
    head_size = queries.shape[-1]
    result_low = gradient.astype(jnp.bfloat16)
    grad_down_w = weight_grad(active_low, result_low)
    grad_active = project_back(result_low, down_matrix)
    grad_hidden = gelu_pull(grad_active)[0].astype(jnp.bfloat16)
    grad_in_w = weight_grad(normed_mlp_low, grad_hidden)
    grad_normed_mlp = project_back(grad_hidden, in_matrix)
    middle_part, grad_mlp_scaling = mlp_pull(grad_normed_mlp)
    grad_middle = gradient + middle_part
    middle_low = grad_middle.astype(jnp.bfloat16)
    grad_out_w = weight_grad(attended, middle_low)
    grad_attended = project_back(middle_low, out_matrix).astype(jnp.bfloat16)
    grad_attended = grad_attended.reshape(queries.shape)
    scores = masked_scores(queries, key_rows, which_block, allowed)
    soft_probs = jnp.exp(scores - log_total)
    grad_probs = pair_scores(grad_attended, value_rows, which_block)
    row_delta = jnp.sum(grad_probs * soft_probs, axis=-1, keepdims=True)
    grad_scores = (soft_probs * (grad_probs - row_delta)).astype(jnp.bfloat16)
    score_scale = head_size ** (-0.5)
    grad_queries = pair_mix(grad_scores, key_rows, which_block) * score_scale
    grad_keys = pair_back(grad_scores, queries, which_block) * score_scale
    grad_values = pair_back(soft_probs.astype(jnp.bfloat16), grad_attended, which_block)
    grad_qkv_rows = jnp.stack([grad_queries, grad_keys, grad_values], axis=3).astype(jnp.bfloat16)
    grad_qkv_rows = grad_qkv_rows.reshape(full_shape[:3] + (3 * full_shape[-1],))
    grad_qkv_w = weight_grad(normed_low, grad_qkv_rows)
    grad_normed = project_back(grad_qkv_rows, qkv_matrix)
    input_part, grad_attn_scaling = norm_pull(grad_normed)
    grad_input = grad_middle + input_part
    return (
        grad_input,
        (grad_qkv_w, grad_out_w, grad_in_w, grad_down_w, grad_attn_scaling, grad_mlp_scaling),
    )


def block_shards(qkv_weight, out_weight, in_weight, down_weight, attn_gain, mlp_gain, block_index):
    return (
        qkv_weight[block_index].astype(jnp.bfloat16),
        out_weight[block_index].astype(jnp.bfloat16),
        in_weight[block_index].astype(jnp.bfloat16),
        down_weight[block_index].astype(jnp.bfloat16),
        attn_gain[block_index].astype(jnp.bfloat16),
        mlp_gain[block_index].astype(jnp.bfloat16),
    )


def by_einsums(
    video, frames, cotangent, qkv_weight, out_weight, in_weight, down_weight, attn_gain, mlp_gain
):
    axes = ("wide", "narrow")
    slot_counts = (frames + 1) // 2
    positions = jnp.arange(video.shape[1], dtype=jnp.int32)
    allowed = (positions[None, None, :] <= positions[None, :, None]) & (
        positions[None, None, :] < slot_counts[:, None, None]
    )
    valid_slot = (positions[None, :] < slot_counts[:, None]).astype(jnp.float32)[:, :, None, None]
    weights = (qkv_weight, out_weight, in_weight, down_weight, attn_gain, mlp_gain)
    full = [
        tuple(lax.all_gather(part, axes, axis=0, tiled=True) for part in block_shards(*weights, b))
        for b in range(2)
    ]
    spatial_out, spatial_stored = block_forward(video.astype(jnp.float32), full[0], 0, allowed)
    temporal_out, temporal_stored = block_forward(spatial_out, full[1], 1, allowed)
    output = (temporal_out * valid_slot).astype(jnp.bfloat16)
    gradient = cotangent.astype(jnp.float32) * valid_slot
    grad_between, temporal_grads = block_backward(gradient, temporal_stored, full[1], 1, allowed)
    grad_start, spatial_grads = block_backward(grad_between, spatial_stored, full[0], 0, allowed)
    summed = [
        lax.psum_scatter(jnp.stack(pair), axes, scatter_dimension=1, tiled=True)
        for pair in zip(spatial_grads, temporal_grads)
    ]
    return (output, grad_start.astype(jnp.bfloat16), *summed)


def solution(mesh):
    both = ("wide", "narrow")
    clips = P(both, None, None, None)
    rows = P(None, both, None)
    in_specs = (clips, P(both), clips, rows, rows, rows, rows, P(None, both), P(None, both))
    out_specs = (clips, clips, rows, rows, rows, rows, P(None, both), P(None, both))

    def shards(*args):
        sz = Sizes(mesh, args[0], args[5])
        whole_tiles = all(rows % 16 == 0 for rows, _ in sz.shards.values())
        if whole_tiles and sz.depth == 4 and sz.narrow == 4 and args[0].shape[0] == 1:
            return by_kernels(mesh, sz)(*args)
        return by_einsums(*args)

    return jax.shard_map(shards, mesh=mesh, in_specs=in_specs, out_specs=out_specs, check_vma=False)
```
